32 devices in a mesh: section: 4 (over y, x), dp: 8 (over z, core).
Axes of the slice: x: 2, y: 2, z: 4, core: 2. Of those that a mesh axis runs over, the one named last changes fastest.
Arguments:
- latent: bfloat16 [24576, 256], P('dp'), may hold values from -6 to 6
- lengths: int32 [24576], P('dp'), may hold values from 2 to 4, as said below
- actions: int32 [5, 24576], P(None, 'dp'), may hold values from 0 to 3
- chances: int32 [4, 24576], P(None, 'dp'), may hold values from 0 to 31
- value_bins: int32 [4, 24576], P(None, 'dp'), may hold values from 0 to 600
- reward_bins: int32 [4, 24576], P(None, 'dp'), may hold values from 0 to 600
- entry_w: bfloat16 [4, 2, 256, 256], P('section'), may hold values from -0.375 to 0.375
- action_w: bfloat16 [4, 4, 256], P('section'), may hold values from -6 to 6
- chance_w: bfloat16 [4, 32, 256], P('section'), may hold values from -6 to 6
- block_w: bfloat16 [4, 2, 2, 2, 256, 256], P('section'), may hold values from -0.375 to 0.375
- gain_w: bfloat16 [4, 2, 5, 256], P('section'), may hold values from 0.5 to 1.5
- shift_w: bfloat16 [4, 2, 5, 256], P('section'), may hold values from -1.5 to 1.5
- state_head: bfloat16 [256, 1206], replicated, may hold values from -1.5 to 1.5
- chance_head: bfloat16 [256, 32], replicated, may hold values from -1.5 to 1.5
Outputs:
- latent_grad: float32 [6144, 4, 256], P('dp', 'section')
- entry_grad: float32 [4, 2, 256, 256], P('section')
- action_grad: float32 [4, 4, 256], P('section')
- chance_grad: float32 [4, 32, 256], P('section')
- block_grad: float32 [4, 2, 2, 2, 256, 256], P('section')
- gain_grad: float32 [4, 2, 5, 256], P('section')
- shift_grad: float32 [4, 2, 5, 256], P('section')
- state_head_grad: float32 [256, 1206], replicated
- chance_head_grad: float32 [256, 32], replicated
- loss: float32 [], replicated
The draws below stay inside these ranges and needn't reach their ends.
Inputs may be any that keep to these rules, and one draw needn't show every extreme that they name: `lengths`: every state unrolls either half of 4 steps or all 4.
All inputs are finite; a program needn't handle non-finite values.
Results may differ from the reference program's by a relative error of at most 0.02.
Values may be sent and summed in bfloat16 or wider, within the bound.
A program may use at most 192 MiB of HBM per device.

```python
import math
import jax
import jax.numpy as jnp
import numpy as np
from jax import lax

D = 256
ACT = 4
CHANCE = 32
BINS = 601
BLOCKS = 2
MB_ROWS = 384
BATCH = 24576
HEADS_OUT = 1206
N_SECTION = 4


def draw_lengths(key, part):
    key = jax.random.fold_in(key, 7)
    coin = jax.random.randint(key, (BATCH,), 0, 2)
    coin = coin.at[0].set(1).at[1].set(0)
    return jnp.where(coin == 1, N_SECTION, N_SECTION // 2).astype(jnp.int32)


def touch_ends(values, stream_key, low, top_value):
    longest = values.shape.index(max(values.shape))
    spots = []
    for shift in (0, 1):
        where = [jax.random.randint(jax.random.fold_in(stream_key, axis), (), 0, length) for axis, length in enumerate(values.shape)]
        where[longest] = (where[longest] + shift) % values.shape[longest]
        spots.append(tuple(where))
    return values.at[spots[0]].set(low).at[spots[1]].set(top_value)


def block_scale(rng, dims, cuts, least, largest):
    loudness = 1.0
    for position, parts in cuts:
        heights = jax.random.uniform(jax.random.fold_in(jax.random.fold_in(rng, 6), position), (parts,), jnp.float32, least / len(cuts), largest / len(cuts))
        loudness = loudness * jnp.repeat(jnp.exp(heights), dims[position] // parts).reshape((-1,) + (1,) * (len(dims) - 1 - position))
    return loudness


def rank_bounds(amount, slope):
    weights = [(1 << 20) // math.isqrt(standing ** slope) + 1 for standing in range(1, amount + 1)]
    scale = 1 + sum(weights) // (1 << 30)
    return np.cumsum(np.array([max(1, weight // scale) for weight in weights]))


def skewed_ids(own_key, shape, count, skew):
    listing = rank_bounds(count, skew)
    pick = jax.random.randint(jax.random.fold_in(own_key, 1), shape, 0, int(listing[count - 1]))
    rank = jnp.searchsorted(jnp.asarray(listing, jnp.int32), pick, side="right")
    return jax.random.permutation(jax.random.fold_in(own_key, 2), count)[rank].astype(jnp.int32)


def noise(key, dims, width, bound, shards=(), kind=jnp.bfloat16):
    drawn = width * jax.random.normal(key, dims, jnp.float32)
    if shards:
        drawn = drawn * block_scale(key, dims, shards, -0.22, 0.18)
    return jnp.clip(drawn, -bound, bound).astype(kind)


def setup_inputs(seed: int = 0) -> dict:
    keys = jax.random.split(jax.random.key(seed), 15)
    latent = noise(keys[0], (BATCH, D), 1.0, 6.0, ((0, 8),))
    lengths = draw_lengths(jax.random.fold_in(keys[14], 71), 0)
    actions = touch_ends(jax.random.randint(keys[2], (N_SECTION + 1, BATCH), 0, ACT), jax.random.fold_in(keys[2], 1), 0, ACT - 1).astype(jnp.int32)
    chances = touch_ends(jax.random.randint(keys[3], (N_SECTION, BATCH), 0, CHANCE), jax.random.fold_in(keys[3], 1), 0, CHANCE - 1).astype(jnp.int32)
    value_bins = touch_ends(jax.random.randint(keys[4], (N_SECTION, BATCH), 0, BINS), jax.random.fold_in(keys[4], 1), 0, BINS - 1).astype(jnp.int32)
    reward_bins = touch_ends(skewed_ids(keys[5], (N_SECTION, BATCH), BINS, 2), jax.random.fold_in(keys[5], 3), 0, BINS - 1).astype(jnp.int32)
    entry_w = noise(keys[6], (N_SECTION, 2, D, D), D ** -0.5, 0.375, ((0, 4),))
    action_w = noise(keys[7], (N_SECTION, ACT, D), 1 ** -0.5, 6.0, ((0, 4),))
    chance_w = noise(keys[8], (N_SECTION, CHANCE, D), 1 ** -0.5, 6.0, ((0, 4),))
    block_w = noise(keys[9], (N_SECTION, 2, BLOCKS, 2, D, D), D ** -0.5, 0.375, ((0, 4),))
    gain_w = jnp.clip(1.0 + 0.1 * jax.random.normal(keys[10], (N_SECTION, 2, 1 + 2 * BLOCKS, D), jnp.float32), 0.5, 1.5).astype(jnp.bfloat16)
    shift_w = noise(keys[11], (N_SECTION, 2, 1 + 2 * BLOCKS, D), 0.3, 1.5, ((0, 4),))
    state_head = noise(keys[12], (D, HEADS_OUT), (D // 16) ** -0.5, 1.5)
    chance_head = noise(keys[13], (D, CHANCE), (D // 16) ** -0.5, 1.5)
    return {"latent": latent, "lengths": lengths, "actions": actions, "chances": chances, "value_bins": value_bins, "reward_bins": reward_bins, "entry_w": entry_w, "action_w": action_w, "chance_w": chance_w, "block_w": block_w, "gain_w": gain_w, "shift_w": shift_w, "state_head": state_head, "chance_head": chance_head}


@jax.custom_vjp
def low(v):
    return lax.optimization_barrier(v.astype(jnp.bfloat16)).astype(jnp.float32)

@jax.custom_vjp
def low_back(v):
    return v

def low_keep(v):
    return (low(v), None)

def low_pass(kept, grad):
    return (grad,)

def back_keep(v):
    return (v, None)

def back_low(kept, grad):
    return (low(grad),)
low.defvjp(low_keep, low_pass)
low_back.defvjp(back_keep, back_low)
NORM_EPS = 1e-05
HALF_SCALE = 0.5

def product(left_mat, right_mat):
    return jnp.dot(left_mat, right_mat, precision=lax.Precision.HIGHEST, preferred_element_type=jnp.float32)

def layer_norm(values):
    center = values - lax.optimization_barrier(jnp.mean(values, axis=-1, keepdims=True))
    spread = lax.optimization_barrier(jnp.mean(center * center, axis=-1, keepdims=True))
    return center * lax.rsqrt(spread + NORM_EPS)

def norm_act(values, gain_vec, shift_vec):
    return jax.nn.gelu(layer_norm(values) * gain_vec + shift_vec)

def block_out(residual, branch, gain_vec, shift_vec):
    return jax.nn.gelu(residual + layer_norm(branch) * gain_vec + shift_vec)

def tower(state_in, picked, entry_mat, lookup, blocks, gain_rows, shifts):
    first_sum = low_back(product(state_in, entry_mat) + product(picked, lookup))
    latent_state = norm_act(first_sum, gain_rows[0], shifts[0])
    for block_at in range(BLOCKS):
        pre_act = low_back(product(low(latent_state), blocks[block_at, 0]))
        mid_low = low(norm_act(pre_act, gain_rows[1 + 2 * block_at], shifts[1 + 2 * block_at]))
        post_act = low_back(product(mid_low, blocks[block_at, 1]))
        latent_state = block_out(latent_state, post_act, gain_rows[2 + 2 * block_at], shifts[2 + 2 * block_at])
    return latent_state

def cross_entropy(logits, target):
    picked = jax.nn.one_hot(target, logits.shape[1], dtype=jnp.float32)
    return jax.nn.logsumexp(logits, axis=1) - lax.optimization_barrier(jnp.sum(logits * picked, axis=1))

def unroll_step(state_in, params, head_pair, targets):
    entry_mat, action_mat, chance_mat, blocks, gain_rows, shifts = params
    state_head, chance_head = head_pair
    act_now, act_next, chance_now, value_now, reward_now, live_rows = targets
    pick_action = jax.nn.one_hot(act_now, ACT, dtype=jnp.float32)
    pick_chance = jax.nn.one_hot(chance_now, CHANCE, dtype=jnp.float32)
    after_state = tower(state_in, pick_action, entry_mat[0], action_mat, blocks[0], gain_rows[0], shifts[0])
    after_low = low(after_state)
    chance_logits = low_back(product(after_low, chance_head))
    next_state = tower(after_low, pick_chance, entry_mat[1], chance_mat, blocks[1], gain_rows[1], shifts[1])
    next_low = low(next_state)
    logits = low_back(product(next_low, state_head))
    losses = cross_entropy(logits[:, :BINS], value_now) + cross_entropy(logits[:, BINS:2 * BINS], reward_now) + cross_entropy(logits[:, 2 * BINS:], act_next) + cross_entropy(chance_logits, chance_now)
    return (next_low, jnp.sum(live_rows * losses))

def reference(latent, lengths, actions, chances, value_bins, reward_bins, entry_w, action_w, chance_w, block_w, gain_w, shift_w, state_head, chance_head):
    section_params = tuple((source.astype(jnp.float32) for source in (entry_w, action_w, chance_w, block_w, gain_w, shift_w)))
    head_pair = (state_head.astype(jnp.float32), chance_head.astype(jnp.float32))
    group_count = BATCH // MB_ROWS

    def by_group(source):
        return jnp.moveaxis(source.reshape(source.shape[0], group_count, MB_ROWS), 1, 0)
    inputs_all = (latent.astype(jnp.float32).reshape(group_count, MB_ROWS, D), lengths.reshape(group_count, MB_ROWS), by_group(actions), by_group(chances), by_group(value_bins), by_group(reward_bins))

    def group_pass(carry, group):
        tower_sum, head_sum, loss_sum = carry
        state_in, length_rows, act_rows, chance_rows, value_rows, reward_rows = group

        def targets_at(step_at):
            return (act_rows[step_at], act_rows[step_at + 1], chance_rows[step_at], value_rows[step_at], reward_rows[step_at], (length_rows > step_at).astype(jnp.float32))

        def params_at(step_at):
            return tuple((source[step_at] for source in section_params))
        stored = []
        current = state_in
        for step_at in range(N_SECTION):
            stored.append(current)
            current, unused_loss = unroll_step(current, params_at(step_at), head_pair, targets_at(step_at))
        cotangent = jnp.zeros_like(state_in)
        step_grads = [None] * N_SECTION
        d_state = cotangent
        for step_at in reversed(range(N_SECTION)):
            step_targets = targets_at(step_at)

            def local_step(state_value, params, heads_now):
                return unroll_step(state_value, params, heads_now, step_targets)
            (unused_next, loss_step), pullback = jax.vjp(local_step, stored[step_at], params_at(step_at), head_pair)
            d_state, d_params, d_heads = pullback((cotangent, jnp.float32(1.0)))
            step_grads[step_at] = d_params
            head_sum = jax.tree.map(jnp.add, head_sum, d_heads)
            loss_sum = loss_sum + loss_step
            cotangent = low(HALF_SCALE * d_state)
        stacked = jax.tree.map(lambda *pieces: jnp.stack(pieces), *step_grads)
        tower_sum = jax.tree.map(jnp.add, tower_sum, stacked)
        return ((tower_sum, head_sum, loss_sum), HALF_SCALE * d_state)
    start_carry = (jax.tree.map(jnp.zeros_like, section_params), jax.tree.map(jnp.zeros_like, head_pair), jnp.float32(0.0))
    (tower_sum, head_sum, loss_sum), first_grads = lax.scan(group_pass, start_carry, inputs_all)
    scale = 1.0 / BATCH
    latent_grad = first_grads.reshape(BATCH, D).reshape(BATCH // N_SECTION, N_SECTION, D)
    entry_grad, action_grad, chance_grad, block_grad, gain_grad, shift_grad = tuple((source * scale for source in tower_sum))
    return (latent_grad, entry_grad, action_grad, chance_grad, block_grad, gain_grad, shift_grad, head_sum[0] * scale, head_sum[1] * scale, loss_sum * scale)
```

```python
import jax
import jax.numpy as jnp
from jax import lax
from jax.experimental import pallas as pl
from jax.experimental.pallas import tpu as pltpu
from jax.sharding import PartitionSpec as P

F32 = jnp.float32
BF16 = jnp.bfloat16
ROOT = 0.7978845608028654
K1 = 2.0 * ROOT
K2 = 8.0 * ROOT * 0.044715
EPS = 1e-05
WIDE = 256
LANES = 128
NORMS = 5
ACT_ROW = 32
GAIN_ROW = 36
SHIFT_ROW = 46
MISC_ROWS = 64


def contract(left, right, left_dim, right_dim):
    return lax.dot_general(
        left, right, (((left_dim,), (right_dim,)), ((), ())), preferred_element_type=F32
    )


def gelu_pair(half):
    square = half * half * K2
    inner = half * (square + K1)
    plus = jnp.tanh(inner) + 1.0
    slope = half * (square * 3.0 + K1)
    return half * plus, plus * ((2.0 - plus) * slope + 1.0)


def norm_forward(values, gain, shift, residual):
    feature_count = values.shape[0]
    center = values - jnp.sum(values, axis=0, keepdims=True) * (1.0 / feature_count)
    inverse = lax.rsqrt(jnp.sum(center * center, axis=0, keepdims=True) + feature_count * EPS)
    unit = center * inverse
    half = unit * gain + shift
    if residual is not None:
        half = half + 0.5 * residual
    out, slope = gelu_pair(half)
    return out, slope, unit, inverse


def kernel(
    latent, lengths, actions, chances, values, rewards, entry, blocks, action_w, chance_w, gains, shifts,
    state_head, chance_head,
    latent_out, tower_out, misc_out, head_out, loss_out, spill,
    weights, misc, head, acts, inv, ids, onehot, current, resid, prod_a, prod_b, grad, gb, acc_dy, acc_p,
    logits, dlogits, dchance, head_back, head_sum, misc_grad, sel, stage,
    w_sem, spill_sem,
):
    section = lax.axis_index("section")
    rows = current.shape[1]
    steps = weights.shape[0]
    feat = WIDE
    head_width = state_head.shape[1]
    bins = (head_width - action_w.shape[1]) // 2
    head_pad = head.shape[1]
    action_count = action_w.shape[1]
    chunks = [slice(c, c + WIDE) for c in range(0, rows, WIDE)]

    def subs(part):
        return [slice(c, c + LANES) for c in range(part.start, part.stop, LANES)]

    copies = []
    for k in range(steps):
        for t in range(2):
            copies.append((entry.at[k, t], weights.at[k, 5 * t]))
            for j in range(2):
                for i in range(2):
                    copies.append((blocks.at[k, t, j, i], weights.at[k, 5 * t + 1 + 2 * j + i]))
    for n, (src, dst) in enumerate(copies):
        pltpu.make_async_copy(src, dst, w_sem.at[n]).start()

    for k in range(steps):
        packed = jnp.concatenate(
            [
                chance_w[k].astype(F32),
                action_w[k].astype(F32),
                gains[k].astype(F32),
                shifts[k].astype(F32),
                jnp.zeros((MISC_ROWS - SHIFT_ROW - 2 * NORMS, feat), F32),
            ],
            axis=0,
        )
        misc[k] = packed.astype(BF16)
    head[...] = jnp.zeros_like(head)
    head[:, 0:head_width] = state_head[...]

    steps_of = steps
    pick_at = lax.broadcasted_iota(jnp.int32, (steps_of * WIDE, WIDE), 0)
    pick_to = lax.broadcasted_iota(jnp.int32, (steps_of * WIDE, WIDE), 1)
    sel[...] = (pick_at == steps_of * pick_to + section).astype(F32).astype(BF16)
    stage[...] = jnp.zeros_like(stage)
    stage[0:1] = lengths[...].astype(F32)
    stage[1:6] = actions[...].astype(F32)
    stage[6:10] = chances[...].astype(F32)
    stage[10:14] = lax.shift_right_logical(values[...], 5).astype(F32)
    stage[14:18] = (values[...] & 31).astype(F32)
    stage[18:22] = lax.shift_right_logical(rewards[...], 5).astype(F32)
    stage[22:26] = (rewards[...] & 31).astype(F32)
    for n, part in enumerate(chunks):
        rows_in = slice(n * steps_of * WIDE, (n + 1) * steps_of * WIDE)
        current[:, part] = contract(latent[rows_in], sel[...], 0, 0).astype(BF16)
        got = contract(stage[:, rows_in].astype(BF16), sel[...], 1, 0)
        value_ids = got[10:14] * 32.0 + got[14:18]
        reward_ids = got[18:22] * 32.0 + got[22:26]
        for k in range(steps):
            ids[k, 0:1, part] = got[0:1]
            ids[k, 1:3, part] = got[1 + k : 3 + k]
            ids[k, 3:4, part] = got[6 + k : 7 + k]
            ids[k, 4:5, part] = value_ids[k : k + 1]
            ids[k, 5:6, part] = reward_ids[k : k + 1]

    for n, (src, dst) in enumerate(copies):
        pltpu.make_async_copy(src, dst, w_sem.at[n]).wait()

    head_sum[...] = jnp.zeros_like(head_sum)
    loss_out[...] = jnp.zeros_like(loss_out)

    def spread_norms(k, tower, with_shift):
        count = 2 * NORMS if with_shift else NORMS
        row = lax.broadcasted_iota(jnp.int32, (MISC_ROWS, count * LANES), 0)
        at = lax.broadcasted_iota(jnp.int32, (MISC_ROWS, count * LANES), 1) // LANES
        gain_row = GAIN_ROW + tower * NORMS
        shift_row = SHIFT_ROW + tower * NORMS
        pick = jnp.where((at < NORMS) & (row == gain_row + at), 8.0, 0.0)
        pick = pick + jnp.where((at >= NORMS) & (row == shift_row + at - NORMS), 0.5, 0.0)
        gb[:, 0 : count * LANES] = contract(misc[k], pick.astype(BF16), 0, 0)

    def gain_of(n):
        return gb[:, n * LANES : (n + 1) * LANES]

    def shift_of(n):
        return gb[:, (NORMS + n) * LANES : (NORMS + n + 1) * LANES]

    def lookup(k, tower):
        lo = ACT_ROW if tower == 0 else 0
        return slice(lo, lo + 32)

    def tower_forward(k, tower):
        slot = lax.rem(k, 2)
        act = acts.at[slot, tower]
        spread_norms(k, tower, True)
        act[0] = current[...]
        look = lookup(k, tower)
        for part in chunks:
            first = contract(weights[k, 5 * tower], act[0, :, part], 0, 0)
            first = first + contract(misc[k, look], onehot[look, part], 0, 0)
            for n, sub in enumerate(subs(part)):
                out, slope, unit, inverse = norm_forward(
                    first[:, n * LANES : (n + 1) * LANES], gain_of(0), shift_of(0), None
                )
                resid[:, sub] = out
                act[1, :, sub] = out.astype(BF16)
                act[5, :, sub] = unit.astype(BF16)
                act[10, :, sub] = slope.astype(BF16)
                inv[2 * k + tower, 0:1, sub] = inverse
        for j in range(2):
            for part in chunks:
                pre = contract(weights[k, 5 * tower + 1 + 2 * j], act[1 + j, :, part], 0, 0)
                for n, sub in enumerate(subs(part)):
                    at = 1 + 2 * j
                    out, slope, unit, inverse = norm_forward(
                        pre[:, n * LANES : (n + 1) * LANES], gain_of(at), shift_of(at), None
                    )
                    act[3 + j, :, sub] = out.astype(BF16)
                    act[5 + at, :, sub] = unit.astype(BF16)
                    act[10 + at, :, sub] = slope.astype(BF16)
                    inv[2 * k + tower, at : at + 1, sub] = inverse
            for part in chunks:
                post = contract(weights[k, 5 * tower + 2 + 2 * j], act[3 + j, :, part], 0, 0)
                for n, sub in enumerate(subs(part)):
                    at = 2 + 2 * j
                    out, slope, unit, inverse = norm_forward(
                        post[:, n * LANES : (n + 1) * LANES], gain_of(at), shift_of(at), resid[:, sub]
                    )
                    if j == 0:
                        resid[:, sub] = out
                        act[2, :, sub] = out.astype(BF16)
                    else:
                        current[:, sub] = out.astype(BF16)
                    act[5 + at, :, sub] = unit.astype(BF16)
                    act[10 + at, :, sub] = slope.astype(BF16)
                    inv[2 * k + tower, at : at + 1, sub] = inverse

    def softmax_block(pieces, target, live):
        top = None
        for start, stop, low, high in pieces:
            part = logits[start:stop]
            if (low, high) != (start, stop):
                row = lax.broadcasted_iota(jnp.int32, part.shape, 0) + start
                part = jnp.where((row >= low) & (row < high), part, -jnp.inf)
            best = jnp.max(part, axis=0, keepdims=True)
            top = best if top is None else jnp.maximum(top, best)
        total = None
        hit = None
        for start, stop, low, high in pieces:
            part = logits[start:stop] - top
            row = lax.broadcasted_iota(jnp.int32, part.shape, 0) + start
            found = jnp.sum(jnp.where(row == target, part, 0.0), axis=0, keepdims=True)
            expo = jnp.exp(part)
            if (low, high) != (start, stop):
                keep = (row >= low) & (row < high)
                expo = jnp.where(keep, expo, 0.0)
                logits[start:stop] = jnp.where(keep, expo, logits[start:stop])
            else:
                logits[start:stop] = expo
            amount = jnp.sum(expo, axis=0, keepdims=True)
            total = amount if total is None else total + amount
            hit = found if hit is None else hit + found
        return live * (jnp.log(total) - hit), live / total

    def head_pass(k):
        slot = lax.rem(k, 2)
        for part in chunks:
            for sub in subs(part):
                live = jnp.where(ids[k, 0:1, sub] > k.astype(F32), 1.0, 0.0)
                value_at = ids[k, 4:5, sub].astype(jnp.int32)
                reward_at = ids[k, 5:6, sub].astype(jnp.int32) + bins
                policy_at = ids[k, 2:3, sub].astype(jnp.int32) + 2 * bins
                chance_at = ids[k, 3:4, sub].astype(jnp.int32)
                logits[...] = contract(head[...], current[:, sub], 0, 0)
                edge_a = bins // 8 * 8
                edge_b = 2 * bins // 8 * 8
                loss = None
                scales = []
                for pieces, target in (
                    (((0, edge_a, 0, edge_a), (edge_a, edge_a + 8, edge_a, bins)), value_at),
                    (
                        (
                            (edge_a, edge_a + 8, bins, edge_a + 8),
                            (edge_a + 8, edge_b, edge_a + 8, edge_b),
                            (edge_b, edge_b + 8, edge_b, 2 * bins),
                        ),
                        reward_at,
                    ),
                    (((edge_b, edge_b + 8, 2 * bins, head_width),), policy_at),
                ):
                    lost, scale = softmax_block(pieces, target, live)
                    loss = lost if loss is None else loss + lost
                    scales.append(scale)
                low_a = bins // 16 * 16
                low_b = 2 * bins // 16 * 16
                for start, stop in (
                    (0, low_a),
                    (low_a, low_a + 16),
                    (low_a + 16, low_b),
                    (low_b, low_b + 16),
                ):
                    row = lax.broadcasted_iota(jnp.int32, (stop - start, LANES), 0) + start
                    expo = logits[start:stop]
                    if stop <= bins:
                        delta = expo * scales[0] - jnp.where(row == value_at, live, 0.0)
                    elif start >= bins and stop <= 2 * bins:
                        delta = expo * scales[1] - jnp.where(row == reward_at, live, 0.0)
                    else:
                        scale = jnp.where(row < bins, scales[0], jnp.where(row < 2 * bins, scales[1], scales[2]))
                        delta = expo * scale
                        for target in (value_at, reward_at, policy_at):
                            delta = delta - jnp.where(row == target, live, 0.0)
                        delta = jnp.where(row < head_width, delta, 0.0)
                    dlogits[start:stop, sub] = delta.astype(BF16)
                if low_b + 16 < head_pad:
                    dlogits[low_b + 16 : head_pad, sub] = jnp.zeros((head_pad - low_b - 16, LANES), BF16)
                chance_logit = contract(chance_head[...], acts[slot, 1, 0, :, sub], 0, 0)
                chance_logit = chance_logit - jnp.max(chance_logit, axis=0, keepdims=True)
                expo = jnp.exp(chance_logit)
                total = jnp.sum(expo, axis=0, keepdims=True)
                row = lax.broadcasted_iota(jnp.int32, chance_logit.shape, 0)
                hot = row == chance_at
                hit = jnp.sum(jnp.where(hot, chance_logit, 0.0), axis=0, keepdims=True)
                loss = loss + live * (jnp.log(total) - hit)
                delta = expo * (live / total) - jnp.where(hot, live, 0.0)
                dchance[k, :, sub] = delta.astype(BF16)
                loss_out[0:1] += loss
        head_sum[:, 0:head_pad] += contract(current[...], dlogits[...], 1, 1)
        head_sum[:, head_pad : head_pad + 32] += contract(acts[slot, 1, 0], dchance[k], 1, 1)
        for part in chunks:
            head_back[k, :, part] = contract(head[...], dlogits[:, part], 1, 0)

    def make_onehot(k):
        row = lax.broadcasted_iota(jnp.int32, (MISC_ROWS, rows), 0)
        chance_at = ids[k, 3:4].astype(jnp.int32)
        action_at = ids[k, 1:2].astype(jnp.int32) + ACT_ROW
        onehot[...] = jnp.where((row == chance_at) | (row == action_at), 1.0, 0.0).astype(BF16)

    def spill_copy(k):
        return pltpu.make_async_copy(acts.at[lax.rem(k, 2)], spill.at[k], spill_sem.at[k])

    def fill_copy(k):
        return pltpu.make_async_copy(spill.at[k], acts.at[lax.rem(k, 2)], spill_sem.at[2 + k])

    @pl.loop(0, steps)
    def _(k):
        @pl.when(k >= 2)
        def _():
            spill_copy(k - 2).wait()

        make_onehot(k)
        tower_forward(k, 0)
        tower_forward(k, 1)
        head_pass(k)

        @pl.when(k < steps - 2)
        def _():
            spill_copy(k).start()

    def norm_backward(d_out, slope, unit, gain, inverse, at, first):
        d_two = d_out * slope.astype(F32)
        unit = unit.astype(F32)
        weighted = d_two * unit
        if first:
            acc_dy[at] = d_two
            acc_p[at] = weighted
        else:
            acc_dy[at] += d_two
            acc_p[at] += weighted
        d_unit = d_two * gain
        mean = jnp.sum(d_unit, axis=0, keepdims=True) * (1.0 / WIDE)
        along = jnp.sum(weighted * gain, axis=0, keepdims=True)
        return ((d_unit - mean - unit * along) * inverse).astype(BF16), d_two

    def tower_backward(k, tower, last):
        slot = lax.rem(k, 2)
        act = acts.at[slot, tower]
        spread_norms(k, tower, False)

        def norm_of(d_out, at, sub):
            return norm_backward(
                d_out,
                act[10 + at, :, sub],
                act[5 + at, :, sub],
                gain_of(at),
                inv[2 * k + tower, at : at + 1, sub],
                at,
                sub.start == 0,
            )

        for j in (1, 0):
            outer = 2 + 2 * j
            inner = 1 + 2 * j
            for part in chunks:
                for sub in subs(part):
                    d_post, d_two = norm_of(grad[:, sub], outer, sub)
                    prod_a[:, sub] = d_post
                    grad[:, sub] = 0.5 * d_two
            for part in chunks:
                d_mid = contract(weights[k, 5 * tower + 2 + 2 * j], prod_a[:, part], 1, 0)
                for n, sub in enumerate(subs(part)):
                    d_pre, _ = norm_of(d_mid[:, n * LANES : (n + 1) * LANES], inner, sub)
                    prod_b[:, sub] = d_pre
            tower_out[k, 5 * tower + 2 + 2 * j] = contract(act[3 + j], prod_a[...], 1, 1)
            for part in chunks:
                grad[:, part] += contract(weights[k, 5 * tower + 1 + 2 * j], prod_b[:, part], 1, 0)
            tower_out[k, 5 * tower + 1 + 2 * j] = contract(act[1 + j], prod_b[...], 1, 1)
        for part in chunks:
            for sub in subs(part):
                d_first, _ = norm_of(grad[:, sub], 0, sub)
                prod_a[:, sub] = d_first
        look = lookup(k, tower)
        tower_out[k, 5 * tower] = contract(act[0], prod_a[...], 1, 1)
        got = contract(onehot[look], prod_a[...], 1, 1)
        if tower == 0:
            misc_grad[k, ACT_ROW : ACT_ROW + action_count] = got[0:action_count]
        else:
            misc_grad[k, 0:32] = got
        ones = jnp.ones((16, LANES), BF16)
        for n in range(NORMS):
            total = contract(ones, acc_p[n].astype(BF16), 1, 1)
            misc_grad[k, GAIN_ROW + NORMS * tower + n : GAIN_ROW + NORMS * tower + n + 1] = 8.0 * total[0:1]
            total = contract(ones, acc_dy[n].astype(BF16), 1, 1)
            misc_grad[k, SHIFT_ROW + NORMS * tower + n : SHIFT_ROW + NORMS * tower + n + 1] = 0.5 * total[0:1]

    @pl.loop(0, steps)
    def _(back):
        k = steps - 1 - back

        @pl.when(k < steps - 2)
        def _():
            fill_copy(k).wait()

        make_onehot(k)

        @pl.when(back == 0)
        def _():
            grad[...] = head_back[k]

        @pl.when(back > 0)
        def _():
            grad[...] = (0.5 * grad[...]).astype(BF16).astype(F32) + head_back[k]

        tower_backward(k, 1, False)
        for part in chunks:
            grad[:, part] = contract(weights[k, 5], prod_a[:, part], 1, 0) + contract(
                chance_head[...], dchance[k, :, part], 1, 0
            )
        tower_backward(k, 0, True)

        @pl.when(k > 0)
        def _():
            for part in chunks:
                grad[:, part] = contract(weights[k, 0], prod_a[:, part], 1, 0)

        @pl.when(k == 0)
        def _():
            for part in chunks:
                latent_out[part] = 0.5 * contract(prod_a[:, part], weights[0, 0], 0, 1)

        @pl.when(k >= 2)
        def _():
            fill_copy(k - 2).start()

    misc_out[...] = misc_grad[...]
    head_out[...] = head_sum[...]


def per_device(
    latent, lengths, actions, chances, value_bins, reward_bins,
    entry_w, action_w, chance_w, block_w, gain_w, shift_w, state_head, chance_head,
):
    full = tuple(
        lax.all_gather(source, "section", axis=0, tiled=True)
        for source in (entry_w, block_w, action_w, chance_w, gain_w, shift_w)
    )
    steps = full[0].shape[0]
    rows = latent.shape[0] // steps
    feat = latent.shape[1]
    head_width = state_head.shape[1]
    head_pad = -(-head_width // LANES) * LANES
    gains = full[4].reshape(steps, -1, feat)
    shifts = full[5].reshape(steps, -1, feat)
    vmem = pl.BlockSpec(memory_space=pltpu.VMEM)
    anys = pl.BlockSpec(memory_space=pl.ANY)
    scratch = [
        pltpu.VMEM((steps, 10, feat, feat), BF16),
        pltpu.VMEM((steps, MISC_ROWS, feat), BF16),
        pltpu.VMEM((feat, head_pad), BF16),
        pltpu.VMEM((2, 2, 15, feat, rows), BF16),
        pltpu.VMEM((2 * steps, 8, rows), F32),
        pltpu.VMEM((steps, 8, rows), F32),
        pltpu.VMEM((MISC_ROWS, rows), BF16),
        pltpu.VMEM((feat, rows), BF16),
        pltpu.VMEM((feat, rows), F32),
        pltpu.VMEM((feat, rows), BF16),
        pltpu.VMEM((feat, rows), BF16),
        pltpu.VMEM((feat, rows), F32),
        pltpu.VMEM((feat, 2 * NORMS * LANES), F32),
        pltpu.VMEM((NORMS, feat, LANES), F32),
        pltpu.VMEM((NORMS, feat, LANES), F32),
        pltpu.VMEM((head_pad, LANES), F32),
        pltpu.VMEM((head_pad, rows), BF16),
        pltpu.VMEM((steps, 32, rows), BF16),
        pltpu.VMEM((steps, feat, rows), F32),
        pltpu.VMEM((feat, head_pad + LANES), F32),
        pltpu.VMEM((steps, MISC_ROWS, feat), F32),
        pltpu.VMEM((steps * WIDE, WIDE), BF16),
        pltpu.VMEM((32, latent.shape[0]), F32),
        pltpu.SemaphoreType.DMA((steps * 10,)),
        pltpu.SemaphoreType.DMA((4,)),
    ]
    outs = pl.pallas_call(
        kernel,
        out_shape=(
            jax.ShapeDtypeStruct((rows, feat), F32),
            jax.ShapeDtypeStruct((steps, 10, feat, feat), F32),
            jax.ShapeDtypeStruct((steps, MISC_ROWS, feat), F32),
            jax.ShapeDtypeStruct((feat, head_pad + LANES), F32),
            jax.ShapeDtypeStruct((8, LANES), F32),
            jax.ShapeDtypeStruct((steps - 2, 2, 15, feat, rows), BF16),
        ),
        in_specs=[vmem] * 6 + [anys] * 2 + [vmem] * 6,
        out_specs=(vmem,) * 5 + (anys,),
        scratch_shapes=scratch,
        compiler_params=pltpu.CompilerParams(vmem_limit_bytes=62 * 2**20),
    )(
        latent, lengths.reshape(1, -1), actions, chances, value_bins, reward_bins,
        full[0], full[1], full[2], full[3], gains, shifts, state_head, chance_head,
    )
    latent_grad, tower_grad, misc_grad, head_grad, loss, _ = outs
    tower_grad = lax.psum_scatter(tower_grad.astype(BF16), "section", scatter_dimension=0, tiled=True).astype(F32)
    misc_grad = lax.psum_scatter(misc_grad, "section", scatter_dimension=0, tiled=True)
    tower_grad, misc_grad = lax.psum((tower_grad, misc_grad), "dp")
    head_grad, loss = lax.psum((head_grad, jnp.sum(loss)), ("section", "dp"))
    scale = 1.0 / (latent.shape[0] * lax.axis_size("dp"))
    tower_grad = (tower_grad * scale)[0].reshape(2, 5, feat, feat)
    misc_grad = (misc_grad * scale)[0]
    act_n = action_w.shape[1]
    return (
        latent_grad.reshape(rows, 1, feat),
        tower_grad[:, 0][None],
        misc_grad[None, ACT_ROW : ACT_ROW + act_n],
        misc_grad[None, 0:32],
        tower_grad[:, 1:].reshape(1, 2, 2, 2, feat, feat),
        misc_grad[GAIN_ROW : GAIN_ROW + 10].reshape(1, 2, 5, feat),
        misc_grad[SHIFT_ROW : SHIFT_ROW + 10].reshape(1, 2, 5, feat),
        head_grad[:, :head_width] * scale,
        head_grad[:, head_pad : head_pad + 32] * scale,
        loss * scale,
    )


def solution(mesh):
    placed = (
        P("dp", None), P("dp"), P(None, "dp"), P(None, "dp"), P(None, "dp"), P(None, "dp"),
        P("section", None, None, None), P("section", None, None), P("section", None, None),
        P("section", None, None, None, None, None), P("section", None, None, None), P("section", None, None, None),
        P(), P(),
    )
    return jax.shard_map(
        per_device,
        mesh=mesh,
        in_specs=placed,
        out_specs=(
            P("dp", "section", None), P("section", None, None, None), P("section", None, None),
            P("section", None, None), P("section", None, None, None, None, None),
            P("section", None, None, None), P("section", None, None, None), P(), P(), P(),
        ),
        check_vma=False,
    )
```

```python
import functools

import jax
import jax.numpy as jnp
from jax import lax
from jax.experimental import pallas as pl
from jax.experimental.pallas import tpu as pltpu
from jax.sharding import PartitionSpec as P

F32 = jnp.float32
BF16 = jnp.bfloat16
ROOT = 0.7978845608028654
K1 = 2.0 * ROOT
K2 = 8.0 * ROOT * 0.044715
EPS = 1e-05
WIDE = 256
LANES = 128
NORMS = 5
ACT_ROW = 32
GAIN_ROW = 36
SHIFT_ROW = 46
MISC_ROWS = 64


def contract(left, right, left_dim, right_dim):
    return lax.dot_general(
        left, right, (((left_dim,), (right_dim,)), ((), ())), preferred_element_type=F32
    )


def gelu_pair(half):
    square = half * half * K2
    inner = half * (square + K1)
    plus = jnp.tanh(inner) + 1.0
    slope = half * (square * 3.0 + K1)
    return half * plus, plus * ((2.0 - plus) * slope + 1.0)


def norm_forward(values, gain, shift, residual):
    feature_count = values.shape[0]
    center = values - jnp.sum(values, axis=0, keepdims=True) * (1.0 / feature_count)
    inverse = lax.rsqrt(jnp.sum(center * center, axis=0, keepdims=True) + feature_count * EPS)
    unit = center * inverse
    half = unit * gain + shift
    if residual is not None:
        half = half + 0.5 * residual
    out, slope = gelu_pair(half)
    return out, slope, unit, inverse


QUARTER = 320
LAST = 384
CHAIN = ((0, 1), (1, 2), (2, 3), (3, 4), (4, 6), (6, 8), (8, 10))
EARLY = (7, 0, 1, 2, 3, 4)
LATE = (5, 6)
MESH = pl.DeviceIdType.MESH


def when(condition, action):
    if isinstance(condition, bool):
        if condition:
            action()
    else:
        pl.when(condition)(action)


def kernel(
    scale, near_count, far_count,
    latent, lengths, actions, chances, values, rewards, entry, blocks, action_w, chance_w, gains, shifts,
    state_head, chance_head,
    latent_out, entry_out, block_out, action_out, chance_out, gain_out, shift_out, head_out, chead_out, loss_out, spill,
    weights, misc, head, acts, inv, ids, onehot, current, resid, prod_a, prod_b, grad, gb, acc_dy, acc_p,
    logits, dlogits, dchance, head_back, head_sum, chead_sum, misc_grad, loss_sum, sel, stage, states,
    sent, core_in, core_sum, part_in, part_sum, near_in, far_in, quarter, whole, other, misc_in, loss_in,
    load_sem, spill_sem, chain_send, chain_recv, give_send, step_recv, pass_send, pair_send, pair_recv,
    core_send, core_recv, part_send, part_recv, near_send, near_recv, far_send, far_recv,
    fill_send, fill_recv, own_send, own_recv, lane_send, lane_recv, extra_send, extra_recv, loss_send, loss_recv,
):
    section = lax.axis_index("section")
    line = lax.axis_index("dp")
    core = lax.rem(line, 2)
    near = lax.rem(line // 2, near_count)
    far = line // 2 // near_count
    mate = line + 1 - 2 * core
    rows = current.shape[1]
    steps = weights.shape[0]
    feat = WIDE
    head_width = state_head.shape[0]
    bins = (head_width - action_w.shape[1]) // 2
    head_pad = head.shape[0]
    action_count = action_w.shape[1]
    chance_count = chance_w.shape[1]
    chunks = [slice(c, c + WIDE) for c in range(0, rows, WIDE)]
    batches = 2 * steps

    def subs(part):
        return [slice(c, c + LANES) for c in range(part.start, part.stop, LANES)]

    def near_line(offset):
        return (far * near_count + lax.rem(near + offset, near_count)) * 2 + core

    def far_line(offset):
        return (lax.rem(far + offset, far_count) * near_count + near) * 2 + core

    def section_at(offset):
        return lax.rem(section + offset, steps)

    barrier = pltpu.get_barrier_semaphore()
    peers = [{"dp": mate}]
    peers += [{"section": section_at(o)} for o in range(1, steps)]
    peers += [{"dp": near_line(o)} for o in range(1, near_count)]
    peers += [{"dp": far_line(o)} for o in range(1, far_count)]
    for peer in peers:
        pl.semaphore_signal(barrier, inc=1, device_id=peer, device_id_type=MESH)

    loads = [(entry.at[0, 0], weights.at[section, 0]), (blocks.at[0, 0], weights.at[section, 1:5])]
    loads += [(entry.at[0, 1], weights.at[section, 5]), (blocks.at[0, 1], weights.at[section, 6:10])]
    loads += [(latent, states)]
    loads = [pltpu.make_async_copy(src, dst, load_sem.at[n]) for n, (src, dst) in enumerate(loads)]
    for load in loads:
        load.start()
    head[head_width // 16 * 16 : head_pad] = jnp.zeros((head_pad - head_width // 16 * 16, feat), BF16)
    head[0:head_width] = state_head[...]

    packed = jnp.concatenate(
        [
            chance_w[0].astype(F32),
            action_w[0].astype(F32),
            gains[0, 0].astype(F32),
            gains[0, 1].astype(F32),
            shifts[0, 0].astype(F32),
            shifts[0, 1].astype(F32),
            jnp.zeros((MISC_ROWS - SHIFT_ROW - 2 * NORMS, feat), F32),
        ],
        axis=0,
    )
    misc[section] = packed.astype(BF16)

    def send(src, dst, sender, receiver, peer):
        return pltpu.make_async_remote_copy(
            src_ref=src, dst_ref=dst, send_sem=sender, recv_sem=receiver, device_id=peer, device_id_type=MESH
        )

    def landed(dst, receiver):
        send(dst, dst, load_sem.at[7], receiver, {"dp": mate}).wait_recv()

    place = jnp.where(section >= 2, 5 - section, section)
    after = lax.rem(place + 1 + 2 * core, steps)
    after = jnp.where(after >= 2, 5 - after, after)
    hops = jnp.where(core == 0, place, lax.rem(steps - place, steps))
    side_a = section + 1 - 2 * lax.rem(section, 2)
    side_b = lax.rem(section + 2, steps)
    pass_step = jnp.where(core == 0, side_a, side_b)
    pass_to = jnp.where(core == 0, side_b, side_a)

    def half_of(step, first, last, part):
        at = pl.multiple_of(part * (feat // 2), feat // 2)
        return weights.at[step, first:last, pl.ds(at, feat // 2)]

    def misc_half(step, part):
        return misc.at[step, pl.ds(pl.multiple_of(part * (MISC_ROWS // 2), MISC_ROWS // 2), MISC_ROWS // 2)]

    def piece(step, n, part):
        if isinstance(step, int) and step == 0:
            return misc_half(0, part) if n == 7 else half_of(0, *CHAIN[n], part)
        return misc_half(step, part) if n == 2 else half_of(step, 5 * n, 5 * n + 5, part)

    def chain(n):
        ref = piece(0, n, core)
        return send(ref, ref, chain_send.at[n], chain_recv.at[n], {"section": after})

    def give(way, n):
        ref = piece(section, n, core)
        return send(ref, ref, give_send.at[way, n], step_recv.at[section, n], {"section": (side_a, side_b)[way]})

    def hand_on(n):
        ref = piece(pass_step, n, core)
        return send(ref, ref, pass_send.at[n], step_recv.at[pass_step, n], {"section": pass_to})

    def pair(step, n):
        ref = piece(step, n, core)
        return send(ref, ref, pair_send.at[step, n], pair_recv.at[step, n], {"dp": mate})

    def chain_on(order, onward):
        def run():
            for n in order:
                landed(piece(0, n, core), chain_recv.at[n])
                if onward:
                    chain(n).start()
                pair(0, n).start()

        return run

    def need_first(order):
        def run():
            for n in order:
                landed(piece(0, n, 1 - core), pair_recv.at[0, n])

        when(section != 0, run)

    def hand_on_now(condition, pieces):
        def run():
            for n in pieces:
                landed(piece(pass_step, n, core), step_recv.at[pass_step, n])
                hand_on(n).start()

        when(condition, run)

    def pair_now(step, pieces):
        def run():
            for n in pieces:
                pl.when(pass_step != step)(functools.partial(landed, piece(step, n, core), step_recv.at[step, n]))
                pair(step, n).start()

        when(section != step, run)

    def need(step, pieces):
        def run():
            for n in pieces:
                landed(piece(step, n, 1 - core), pair_recv.at[step, n])

        when(section != step, run)

    def give_now(way):
        def run():
            for n in (2, 0, 1):
                give(way, n).start()

        return run

    pl.semaphore_wait(barrier, len(peers))
    for load in loads[0:4]:
        load.wait()

    @pl.when(hops == 0)
    def _():
        for n in EARLY + LATE:
            chain(n).start()

    pl.when(section == 1)(give_now(0))
    pl.when(section == 2)(give_now(1))

    pick_at = lax.broadcasted_iota(jnp.int32, (steps * WIDE, WIDE), 0)
    pick_to = lax.broadcasted_iota(jnp.int32, (steps * WIDE, WIDE), 1)
    sel[...] = (pick_at == steps * pick_to + section).astype(F32).astype(BF16)
    stage[...] = jnp.zeros_like(stage)
    stage[0:1] = lengths[...].astype(F32)
    stage[1:6] = actions[...].astype(F32)
    stage[6:10] = chances[...].astype(F32)
    stage[10:14] = lax.shift_right_logical(values[...], 5).astype(F32)
    stage[14:18] = (values[...] & 31).astype(F32)
    stage[18:22] = lax.shift_right_logical(rewards[...], 5).astype(F32)
    stage[22:26] = (rewards[...] & 31).astype(F32)
    for load in loads[4:]:
        load.wait()
    for n, part in enumerate(chunks):
        rows_in = slice(n * steps * WIDE, (n + 1) * steps * WIDE)
        current[:, part] = contract(states[rows_in], sel[...], 0, 0).astype(BF16)
        got = contract(stage[:, rows_in].astype(BF16), sel[...], 1, 0)
        value_ids = got[10:14] * 32.0 + got[14:18]
        reward_ids = got[18:22] * 32.0 + got[22:26]
        for k in range(steps):
            ids[k, 0:1, part] = got[0:1]
            ids[k, 1:3, part] = got[1 + k : 3 + k]
            ids[k, 3:4, part] = got[6 + k : 7 + k]
            ids[k, 4:5, part] = value_ids[k : k + 1]
            ids[k, 5:6, part] = reward_ids[k : k + 1]
    head_sum[...] = jnp.zeros_like(head_sum)
    chead_sum[...] = jnp.zeros_like(chead_sum)
    loss_sum[...] = jnp.zeros_like(loss_sum)

    pl.when((hops == 1) | (hops == 2))(chain_on(EARLY + LATE, True))
    pl.when(section == 1)(give_now(1))
    pl.when(section == 2)(give_now(0))
    pl.when(section == 3)(give_now(0))
    pl.when(section == 3)(give_now(1))
    pl.when(hops == 3)(chain_on(EARLY, False))
    need_first(EARLY)

    def spread_norms(k, tower, with_shift):
        count = 2 * NORMS if with_shift else NORMS
        row = lax.broadcasted_iota(jnp.int32, (MISC_ROWS, count * LANES), 0)
        at = lax.broadcasted_iota(jnp.int32, (MISC_ROWS, count * LANES), 1) // LANES
        gain_row = GAIN_ROW + tower * NORMS
        shift_row = SHIFT_ROW + tower * NORMS
        pick = jnp.where((at < NORMS) & (row == gain_row + at), 8.0, 0.0)
        pick = pick + jnp.where((at >= NORMS) & (row == shift_row + at - NORMS), 0.5, 0.0)
        gb[:, 0 : count * LANES] = contract(misc[k], pick.astype(BF16), 0, 0)

    def gain_of(n):
        return gb[:, n * LANES : (n + 1) * LANES]

    def shift_of(n):
        return gb[:, (NORMS + n) * LANES : (NORMS + n + 1) * LANES]

    def lookup(k, tower):
        lo = ACT_ROW if tower == 0 else 0
        return slice(lo, lo + 32)

    def tower_forward(k, tower):
        slot = lax.rem(k, 2)
        act = acts.at[slot, tower]
        spread_norms(k, tower, True)
        act[0] = current[...]
        look = lookup(k, tower)
        for part in chunks:
            first = contract(weights[k, 5 * tower], act[0, :, part], 0, 0)
            first = first + contract(misc[k, look], onehot[look, part], 0, 0)
            for n, sub in enumerate(subs(part)):
                out, slope, unit, inverse = norm_forward(
                    first[:, n * LANES : (n + 1) * LANES], gain_of(0), shift_of(0), None
                )
                resid[:, sub] = out
                act[1, :, sub] = out.astype(BF16)
                act[5, :, sub] = unit.astype(BF16)
                act[10, :, sub] = slope.astype(BF16)
                inv[2 * k + tower, 0:1, sub] = inverse
        for j in range(2):
            for part in chunks:
                pre = contract(weights[k, 5 * tower + 1 + 2 * j], act[1 + j, :, part], 0, 0)
                for n, sub in enumerate(subs(part)):
                    at = 1 + 2 * j
                    out, slope, unit, inverse = norm_forward(
                        pre[:, n * LANES : (n + 1) * LANES], gain_of(at), shift_of(at), None
                    )
                    act[3 + j, :, sub] = out.astype(BF16)
                    act[5 + at, :, sub] = unit.astype(BF16)
                    act[10 + at, :, sub] = slope.astype(BF16)
                    inv[2 * k + tower, at : at + 1, sub] = inverse
            for part in chunks:
                post = contract(weights[k, 5 * tower + 2 + 2 * j], act[3 + j, :, part], 0, 0)
                for n, sub in enumerate(subs(part)):
                    at = 2 + 2 * j
                    out, slope, unit, inverse = norm_forward(
                        post[:, n * LANES : (n + 1) * LANES], gain_of(at), shift_of(at), resid[:, sub]
                    )
                    if j == 0:
                        resid[:, sub] = out
                        act[2, :, sub] = out.astype(BF16)
                    else:
                        current[:, sub] = out.astype(BF16)
                    act[5 + at, :, sub] = unit.astype(BF16)
                    act[10 + at, :, sub] = slope.astype(BF16)
                    inv[2 * k + tower, at : at + 1, sub] = inverse

    def softmax_block(pieces, target, live):
        top = None
        for start, stop, low, high in pieces:
            part = logits[start:stop]
            if (low, high) != (start, stop):
                row = lax.broadcasted_iota(jnp.int32, part.shape, 0) + start
                part = jnp.where((row >= low) & (row < high), part, -jnp.inf)
            best = jnp.max(part, axis=0, keepdims=True)
            top = best if top is None else jnp.maximum(top, best)
        total = None
        hit = None
        for start, stop, low, high in pieces:
            part = logits[start:stop] - top
            row = lax.broadcasted_iota(jnp.int32, part.shape, 0) + start
            found = jnp.sum(jnp.where(row == target, part, 0.0), axis=0, keepdims=True)
            expo = jnp.exp(part)
            if (low, high) != (start, stop):
                keep = (row >= low) & (row < high)
                expo = jnp.where(keep, expo, 0.0)
                logits[start:stop] = jnp.where(keep, expo, logits[start:stop])
            else:
                logits[start:stop] = expo
            amount = jnp.sum(expo, axis=0, keepdims=True)
            total = amount if total is None else total + amount
            hit = found if hit is None else hit + found
        return live * (jnp.log(total) - hit), live / total

    def head_pass(k, tick):
        slot = lax.rem(k, 2)
        for part in chunks:
            if part.start == WIDE:
                tick()
            for sub in subs(part):
                live = jnp.where(ids[k, 0:1, sub] > k.astype(F32), 1.0, 0.0)
                value_at = ids[k, 4:5, sub].astype(jnp.int32)
                reward_at = ids[k, 5:6, sub].astype(jnp.int32) + bins
                policy_at = ids[k, 2:3, sub].astype(jnp.int32) + 2 * bins
                chance_at = ids[k, 3:4, sub].astype(jnp.int32)
                logits[...] = contract(head[...], current[:, sub], 1, 0)
                edge_a = bins // 8 * 8
                edge_b = 2 * bins // 8 * 8
                loss = None
                scales = []
                for pieces, target in (
                    (((0, edge_a, 0, edge_a), (edge_a, edge_a + 8, edge_a, bins)), value_at),
                    (
                        (
                            (edge_a, edge_a + 8, bins, edge_a + 8),
                            (edge_a + 8, edge_b, edge_a + 8, edge_b),
                            (edge_b, edge_b + 8, edge_b, 2 * bins),
                        ),
                        reward_at,
                    ),
                    (((edge_b, edge_b + 8, 2 * bins, head_width),), policy_at),
                ):
                    lost, scale = softmax_block(pieces, target, live)
                    loss = lost if loss is None else loss + lost
                    scales.append(scale)
                low_a = bins // 16 * 16
                low_b = 2 * bins // 16 * 16
                for start, stop in (
                    (0, low_a),
                    (low_a, low_a + 16),
                    (low_a + 16, low_b),
                    (low_b, low_b + 16),
                ):
                    row = lax.broadcasted_iota(jnp.int32, (stop - start, LANES), 0) + start
                    expo = logits[start:stop]
                    if stop <= bins:
                        delta = expo * scales[0] - jnp.where(row == value_at, live, 0.0)
                    elif start >= bins and stop <= 2 * bins:
                        delta = expo * scales[1] - jnp.where(row == reward_at, live, 0.0)
                    else:
                        scale = jnp.where(row < bins, scales[0], jnp.where(row < 2 * bins, scales[1], scales[2]))
                        delta = expo * scale
                        for target in (value_at, reward_at, policy_at):
                            delta = delta - jnp.where(row == target, live, 0.0)
                        delta = jnp.where(row < head_width, delta, 0.0)
                    dlogits[start:stop, sub] = delta.astype(BF16)
                if low_b + 16 < head_pad:
                    dlogits[low_b + 16 : head_pad, sub] = jnp.zeros((head_pad - low_b - 16, LANES), BF16)
                chance_logit = contract(chance_head[...], acts[slot, 1, 0, :, sub], 1, 0)
                chance_logit = chance_logit - jnp.max(chance_logit, axis=0, keepdims=True)
                expo = jnp.exp(chance_logit)
                total = jnp.sum(expo, axis=0, keepdims=True)
                row = lax.broadcasted_iota(jnp.int32, chance_logit.shape, 0)
                hot = row == chance_at
                hit = jnp.sum(jnp.where(hot, chance_logit, 0.0), axis=0, keepdims=True)
                loss = loss + live * (jnp.log(total) - hit)
                delta = expo * (live / total) - jnp.where(hot, live, 0.0)
                dchance[k, :, sub] = delta.astype(BF16)
                loss_sum[0:1] += loss
        head_sum[...] += contract(dlogits[...], current[...], 1, 1)
        chead_sum[...] += contract(dchance[k], acts[slot, 1, 0], 1, 1)
        for part in chunks:
            head_back[k, :, part] = contract(head[...], dlogits[:, part], 0, 0)

    def make_onehot(k):
        row = lax.broadcasted_iota(jnp.int32, (MISC_ROWS, rows), 0)
        chance_at = ids[k, 3:4].astype(jnp.int32)
        action_at = ids[k, 1:2].astype(jnp.int32) + ACT_ROW
        onehot[...] = jnp.where((row == chance_at) | (row == action_at), 1.0, 0.0).astype(BF16)

    def spill_copy(k):
        return pltpu.make_async_copy(acts.at[lax.rem(k, 2)], spill.at[k], spill_sem.at[k])

    def fill_copy(k):
        return pltpu.make_async_copy(spill.at[k], acts.at[lax.rem(k, 2)], spill_sem.at[2 + k])

    @pl.loop(0, steps)
    def _(k):
        @pl.when(k >= 2)
        def _():
            spill_copy(k - 2).wait()

        @pl.when(k == 1)
        def _():
            pair_now(1, (1,))
            need(1, (2, 0))
            hand_on_now(pass_step >= 2, (2, 0))

        @pl.when(k == 2)
        def _():
            need(2, (2, 0))
            pair_now(3, (2, 0))

        @pl.when(k == 3)
        def _():
            need(3, (2, 0))

        make_onehot(k)
        tower_forward(k, 0)

        @pl.when(k == 0)
        def _():
            pl.when(hops == 3)(chain_on(LATE, False))
            need_first(LATE)
            hand_on_now(pass_step == 1, (2, 0))

        @pl.when(k == 1)
        def _():
            need(1, (1,))
            hand_on_now(pass_step >= 2, (1,))

        @pl.when(k == 2)
        def _():
            need(2, (1,))
            pair_now(3, (1,))

        @pl.when(k == 3)
        def _():
            need(3, (1,))

        tower_forward(k, 1)

        @pl.when(k == 0)
        def _():
            hand_on_now(pass_step == 1, (1,))

        @pl.when(k == 1)
        def _():
            pair_now(2, (2, 0))

        def tick():
            @pl.when(k == 0)
            def _():
                pair_now(1, (2, 0))

            @pl.when(k == 1)
            def _():
                pair_now(2, (1,))

        head_pass(k, tick)

        @pl.when(k < steps - 2)
        def _():
            spill_copy(k).start()

    @pl.when(hops < 3)
    def _():
        for n in EARLY + LATE:
            chain(n).wait_send()

    @pl.when(section != 0)
    def _():
        for n in EARLY + LATE:
            pair(0, n).wait_send()
        for way in range(2):
            for n in range(3):
                give(way, n).wait_send()

    @pl.when(pass_step != 0)
    def _():
        for n in range(3):
            hand_on(n).wait_send()

    for step in range(1, steps):
        @pl.when(section != step)
        def _():
            for n in range(3):
                pair(step, n).wait_send()

    def lanes(part):
        return pl.ds(pl.multiple_of(part * LANES, LANES), LANES)

    def core_copy(b, slot, count):
        return send(
            sent.at[slot, :, 0:count, lanes(1 - core)], core_in.at[slot, :, 0:count],
            core_send.at[b], core_recv.at[b], {"dp": mate},
        )

    def part_copy(b, slot, count, offset):
        return send(
            core_sum.at[section_at(offset), 0:count], part_in.at[slot, offset - 1, 0:count],
            part_send.at[b, offset - 1], part_recv.at[b, offset - 1], {"section": section_at(offset)},
        )

    def near_rows(count, offset):
        size = count // near_count
        return pl.ds(pl.multiple_of(lax.rem(near + offset, near_count) * size, 16), size)

    def near_copy(b, slot, count, offset):
        return send(
            part_sum.at[near_rows(count, offset)], near_in.at[slot, offset - 1, 0 : count // near_count],
            near_send.at[b, offset - 1], near_recv.at[b, offset - 1], {"dp": near_line(offset)},
        )

    def far_copy(b, slot, count, offset):
        return send(
            quarter.at[b, near_rows(count, 0)], far_in.at[slot, offset - 1, 0 : count // near_count],
            far_send.at[b, offset - 1], far_recv.at[b, offset - 1], {"dp": far_line(offset)},
        )

    def fill_back(b, count, offset):
        ref = quarter.at[b, near_rows(count, 0)]
        return send(ref, ref, fill_send.at[b, offset - 1], fill_recv.at[b, offset - 1], {"dp": near_line(offset)})

    def core_wait(b, slot, count):
        core_copy(b, slot, count).wait()
        for j in range(steps):
            mine = sent[slot, j, 0:count, lanes(core)].astype(F32)
            core_sum[j, 0:count] = (mine + core_in[slot, j, 0:count].astype(F32)).astype(BF16)
        for offset in range(1, steps):
            part_copy(b, slot, count, offset).start()

    def part_wait(b, slot, count):
        for offset in range(1, steps):
            part_copy(b, slot, count, offset).wait()
        total = core_sum[section, 0:count].astype(F32)
        for n in range(steps - 1):
            total = total + part_in[slot, n, 0:count].astype(F32)
        part_sum[0:count] = total.astype(BF16)
        for offset in range(1, near_count):
            near_copy(b, slot, count, offset).start()

    def near_wait(b, slot, count):
        for offset in range(1, near_count):
            near_copy(b, slot, count, offset).wait()
        size = count // near_count
        total = part_sum[near_rows(count, 0)].astype(F32)
        for n in range(near_count - 1):
            total = total + near_in[slot, n, 0:size].astype(F32)
        quarter[b, near_rows(count, 0)] = total.astype(BF16)
        if far_count > 1:
            for offset in range(1, far_count):
                far_copy(b, slot, count, offset).start()
            for offset in range(1, far_count):
                far_copy(b, slot, count, offset).wait()
            for n in range(far_count - 1):
                total = total + far_in[slot, n, 0:size].astype(F32)
            quarter[b, near_rows(count, 0)] = total.astype(BF16)
        for offset in range(1, near_count):
            fill_back(b, count, offset).start()

    def fill_wait(b, count):
        for offset in range(1, near_count):
            fill_back(b, count, offset).wait_send()
            landed(quarter.at[b, near_rows(count, near_count - offset)], fill_recv.at[b, offset - 1])

    def owner_copy(b, tower, offset):
        return send(
            quarter.at[b, 0:QUARTER], whole.at[tower, section], own_send.at[b, offset - 1],
            own_recv.at[tower, offset - 1], {"section": section_at(steps - offset)},
        )

    def share_start(b, tower):
        whole[tower, section] = quarter[b, 0:QUARTER]
        if tower == 2:
            for offset in range(1, steps):
                owner_copy(b, tower, offset).start()
            return
        owner = steps - 1 - (b - 1) // 2
        for offset in range(1, steps):
            pl.when(lax.rem(section - owner + steps, steps) == offset)(owner_copy(b, tower, offset).start)

    def share_wait(b, tower):
        def take():
            for offset in range(1, steps):
                landed(whole.at[tower, section_at(offset)], own_recv.at[tower, offset - 1])
            lane_copy(tower).start()

        if tower == 2:
            for offset in range(1, steps):
                owner_copy(b, tower, offset).wait_send()
            take()
            return
        owner = steps - 1 - (b - 1) // 2
        for offset in range(1, steps):
            pl.when(lax.rem(section - owner + steps, steps) == offset)(owner_copy(b, tower, offset).wait_send)
        pl.when(section == owner)(take)

    def lane_copy(tower):
        return send(whole.at[tower], other.at[tower], lane_send.at[tower], lane_recv.at[tower], {"dp": mate})

    def finish(b, tower):
        def run():
            lane_copy(tower).wait()
            for buffer, part in ((whole, core), (other, 1 - core)):
                for j in range(steps):
                    values_now = buffer[tower, j].astype(F32) * scale
                    if tower == 2:
                        start = j * QUARTER
                        stop = min(start + QUARTER, head_width)
                        head_out[start:stop, lanes(part)] = values_now[0 : stop - start]
                        if stop < start + QUARTER:
                            at = stop - start
                            chead_out[:, lanes(part)] = values_now[at : at + chance_count]
                        continue
                    size = feat // steps
                    at = slice(j * size, (j + 1) * size)
                    entry_out[0, tower, at, lanes(part)] = values_now[0:size]
                    for m in range(4):
                        block_out_rows = values_now[(m + 1) * size : (m + 2) * size]
                        block_out[0, tower, m // 2, m % 2, at, lanes(part)] = block_out_rows

        if tower == 2:
            run()
        else:
            pl.when(section == steps - 1 - (b - 1) // 2)(run)

    def by_kind(b, odd, action):
        if isinstance(b, int):
            if 0 <= b <= batches:
                action(b, 1 if odd else (2 if b == 0 else 0))
        elif odd:
            pl.when(b >= 0)(functools.partial(action, b, 1))
        else:
            pl.when(b > 0)(functools.partial(action, b, 0))
            pl.when(b == 0)(functools.partial(action, b, 2))

    def rows_of(b):
        return LAST if isinstance(b, int) and b == batches else QUARTER

    def fill_and_share(b, tower):
        fill_wait(b, rows_of(b))
        share_start(b, tower)

    def ticks(at, parity, turn):
        if turn == 0:
            by_kind(at - 2, parity == 1, fill_and_share)
        elif turn == 1:
            if not isinstance(at, int) or at <= batches:
                core_wait(at, parity, rows_of(at))
        elif turn == 2:
            if not isinstance(at, int):
                pl.when(at >= 1)(functools.partial(near_wait, at - 1, 1 - parity, QUARTER))
            elif at - 1 <= batches:
                near_wait(at - 1, 1 - parity, rows_of(at - 1))
        elif turn == 3:
            by_kind(at - 2, parity == 1, share_wait)
        else:
            if not isinstance(at, int) or at <= batches:
                part_wait(at, parity, rows_of(at))
            by_kind(at - 3, parity == 0, finish)

    def norm_backward(d_out, slope, unit, gain, inverse, at, first):
        d_two = d_out * slope.astype(F32)
        unit = unit.astype(F32)
        weighted = d_two * unit
        if first:
            acc_dy[at] = d_two
            acc_p[at] = weighted
        else:
            acc_dy[at] += d_two
            acc_p[at] += weighted
        d_unit = d_two * gain
        mean = jnp.sum(d_unit, axis=0, keepdims=True) * (1.0 / WIDE)
        along = jnp.sum(weighted * gain, axis=0, keepdims=True)
        return ((d_unit - mean - unit * along) * inverse).astype(BF16), d_two

    def tower_backward(k, tower, at):
        slot = lax.rem(k, 2)
        act = acts.at[slot, tower]
        parity = 1 - tower
        slot_out = tower
        ticks(at, parity, 0)
        spread_norms(k, tower, False)

        def put(m, value):
            size = feat // steps
            for j in range(steps):
                sent[slot_out, j, m * size : (m + 1) * size] = value[j * size : (j + 1) * size].astype(BF16)

        turn = 1

        def norm_of(d_out, at, sub):
            return norm_backward(
                d_out,
                act[10 + at, :, sub],
                act[5 + at, :, sub],
                gain_of(at),
                inv[2 * k + tower, at : at + 1, sub],
                at,
                sub.start == 0,
            )

        for j in (1, 0):
            outer = 2 + 2 * j
            inner = 1 + 2 * j
            for part in chunks:
                for sub in subs(part):
                    d_post, d_two = norm_of(grad[:, sub], outer, sub)
                    prod_a[:, sub] = d_post
                    grad[:, sub] = 0.5 * d_two
            ticks(at, parity, turn)
            turn += 1
            for part in chunks:
                d_mid = contract(weights[k, 5 * tower + 2 + 2 * j], prod_a[:, part], 1, 0)
                for n, sub in enumerate(subs(part)):
                    d_pre, _ = norm_of(d_mid[:, n * LANES : (n + 1) * LANES], inner, sub)
                    prod_b[:, sub] = d_pre
            put(2 + 2 * j, contract(act[3 + j], prod_a[...], 1, 1))
            for part in chunks:
                grad[:, part] += contract(weights[k, 5 * tower + 1 + 2 * j], prod_b[:, part], 1, 0)
            put(1 + 2 * j, contract(act[1 + j], prod_b[...], 1, 1))
            ticks(at, parity, turn)
            turn += 1
        for part in chunks:
            for sub in subs(part):
                d_first, _ = norm_of(grad[:, sub], 0, sub)
                prod_a[:, sub] = d_first
        look = lookup(k, tower)
        put(0, contract(act[0], prod_a[...], 1, 1))
        got = contract(onehot[look], prod_a[...], 1, 1)
        if tower == 0:
            misc_grad[k, ACT_ROW : ACT_ROW + action_count] = got[0:action_count]
        else:
            misc_grad[k, 0:32] = got
        ones = jnp.ones((16, LANES), BF16)
        for n in range(NORMS):
            total = contract(ones, acc_p[n].astype(BF16), 1, 1)
            misc_grad[k, GAIN_ROW + NORMS * tower + n : GAIN_ROW + NORMS * tower + n + 1] = 8.0 * total[0:1]
            total = contract(ones, acc_dy[n].astype(BF16), 1, 1)
            misc_grad[k, SHIFT_ROW + NORMS * tower + n : SHIFT_ROW + NORMS * tower + n + 1] = 0.5 * total[0:1]

    head_sum[head_width : head_width + chance_count] = chead_sum[...]
    for j in range(steps):
        sent[0, j, 0:QUARTER] = head_sum[j * QUARTER : (j + 1) * QUARTER].astype(BF16)
    core_copy(0, 0, QUARTER).start()

    @pl.loop(0, steps)
    def _(back):
        k = steps - 1 - back

        @pl.when(k < steps - 2)
        def _():
            fill_copy(k).wait()

        make_onehot(k)

        @pl.when(back == 0)
        def _():
            grad[...] = head_back[k]

        @pl.when(back > 0)
        def _():
            grad[...] = (0.5 * grad[...]).astype(BF16).astype(F32) + head_back[k]

        tower_backward(k, 1, 2 * back)
        core_copy(2 * back + 1, 1, QUARTER).start()
        for part in chunks:
            grad[:, part] = contract(weights[k, 5], prod_a[:, part], 1, 0) + contract(
                chance_head[...], dchance[k, :, part], 0, 0
            )
        tower_backward(k, 0, 2 * back + 1)

        @pl.when(k > 0)
        def _():
            core_copy(2 * back + 2, 0, QUARTER).start()

        @pl.when(k > 0)
        def _():
            for part in chunks:
                grad[:, part] = contract(weights[k, 0], prod_a[:, part], 1, 0)

        @pl.when(k == 0)
        def _():
            for part in chunks:
                latent_out[part] = 0.5 * contract(prod_a[:, part], weights[0, 0], 0, 1)

        @pl.when(k >= 2)
        def _():
            fill_copy(k - 2).start()

    for j in range(steps):
        sent[0, j, QUARTER:LAST] = misc_grad[j].astype(BF16)
    core_copy(batches, 0, LAST).start()

    loss_at = [{"dp": mate}] + [{"section": section_at(o)} for o in range(1, steps)]
    loss_at += [{"dp": near_line(o)} for o in range(1, near_count)]
    loss_at += [{"dp": far_line(o)} for o in range(1, far_count)]
    rounds = [1, steps - 1, near_count - 1, far_count - 1]
    bounds = [sum(rounds[:n]) for n in range(5)]

    def loss_copy(n, stage_at):
        return send(loss_sum.at[stage_at], loss_in.at[n], loss_send.at[n], loss_recv.at[n], loss_at[n])

    def loss_start(stage_at):
        for n in range(bounds[stage_at], bounds[stage_at + 1]):
            loss_copy(n, stage_at).start()

    def loss_wait(stage_at):
        total = loss_sum[stage_at]
        for n in range(bounds[stage_at], bounds[stage_at + 1]):
            loss_copy(n, stage_at).wait()
            total = total + loss_in[n]
        loss_sum[stage_at + 1] = total

    def misc_copy():
        return send(
            quarter.at[batches, QUARTER:LAST], misc_in.at[0], extra_send.at[0], extra_recv.at[0], {"dp": mate}
        )

    loss_start(0)
    for at in range(batches, batches + 4):
        for turn in range(5):
            ticks(at, at % 2, turn)
            if at == batches and turn == 1:
                loss_wait(0)
                loss_start(1)
            if at == batches and turn == 4:
                loss_wait(1)
                loss_start(2)
            if at == batches + 1 and turn == 2:
                loss_wait(2)
                loss_start(3)
            if at == batches + 2 and turn == 0:
                misc_copy().start()
    loss_wait(3)
    loss_out[...] = jnp.sum(loss_sum[4, 0:1], axis=1, keepdims=True) * scale
    misc_copy().wait()
    for source, part in ((quarter[batches, QUARTER:LAST], core), (misc_in[0], 1 - core)):
        got = source.astype(F32) * scale
        chance_out[0, :, lanes(part)] = got[0:chance_count]
        action_out[0, :, lanes(part)] = got[ACT_ROW : ACT_ROW + action_count]
        for tower in range(2):
            at = GAIN_ROW + tower * NORMS
            gain_out[0, tower, :, lanes(part)] = got[at : at + NORMS]
            at = SHIFT_ROW + tower * NORMS
            shift_out[0, tower, :, lanes(part)] = got[at : at + NORMS]


def per_device(
    latent, lengths, actions, chances, value_bins, reward_bins,
    entry_w, action_w, chance_w, block_w, gain_w, shift_w, state_head, chance_head,
):
    steps = lax.axis_size("section")
    lines = lax.axis_size("dp")
    near_count = min(4, lines // 2)
    far_count = lines // 2 // near_count
    rows = latent.shape[0] // steps
    feat = latent.shape[1]
    head_width = state_head.shape[1]
    head_pad = steps * QUARTER
    batches = 2 * steps + 1
    vmem = pl.BlockSpec(memory_space=pltpu.VMEM)
    anys = pl.BlockSpec(memory_space=pl.ANY)
    dma = pltpu.SemaphoreType.DMA
    tiny = 1 + (steps - 1) + (near_count - 1) + (far_count - 1)
    far_slots = max(far_count - 1, 1)
    scratch = [
        pltpu.VMEM((steps, 10, feat, feat), BF16),
        pltpu.VMEM((steps, MISC_ROWS, feat), BF16),
        pltpu.VMEM((head_pad, feat), BF16),
        pltpu.VMEM((2, 2, 15, feat, rows), BF16),
        pltpu.VMEM((2 * steps, 8, rows), F32),
        pltpu.VMEM((steps, 8, rows), F32),
        pltpu.VMEM((MISC_ROWS, rows), BF16),
        pltpu.VMEM((feat, rows), BF16),
        pltpu.VMEM((feat, rows), F32),
        pltpu.VMEM((feat, rows), BF16),
        pltpu.VMEM((feat, rows), BF16),
        pltpu.VMEM((feat, rows), F32),
        pltpu.VMEM((feat, 2 * NORMS * LANES), F32),
        pltpu.VMEM((NORMS, feat, LANES), F32),
        pltpu.VMEM((NORMS, feat, LANES), F32),
        pltpu.VMEM((head_pad, LANES), F32),
        pltpu.VMEM((head_pad, rows), BF16),
        pltpu.VMEM((steps, 32, rows), BF16),
        pltpu.VMEM((steps, feat, rows), F32),
        pltpu.VMEM((head_pad, feat), F32),
        pltpu.VMEM((32, feat), F32),
        pltpu.VMEM((steps, MISC_ROWS, feat), F32),
        pltpu.VMEM((5, 8, LANES), F32),
        pltpu.VMEM((steps * WIDE, WIDE), BF16),
        pltpu.VMEM((32, latent.shape[0]), F32),
        pltpu.VMEM(latent.shape, BF16),
        pltpu.VMEM((2, steps, LAST, feat), BF16),
        pltpu.VMEM((2, steps, LAST, LANES), BF16),
        pltpu.VMEM((steps, LAST, LANES), BF16),
        pltpu.VMEM((2, steps - 1, LAST, LANES), BF16),
        pltpu.VMEM((LAST, LANES), BF16),
        pltpu.VMEM((2, near_count - 1, LAST // near_count, LANES), BF16),
        pltpu.VMEM((2, far_slots, LAST // near_count, LANES), BF16),
        pltpu.VMEM((batches, LAST, LANES), BF16),
        pltpu.VMEM((3, steps, QUARTER, LANES), BF16),
        pltpu.VMEM((3, steps, QUARTER, LANES), BF16),
        pltpu.VMEM((1, MISC_ROWS, LANES), BF16),
        pltpu.VMEM((tiny, 8, LANES), F32),
        dma((8,)),
        dma((4,)),
        dma((8,)), dma((8,)),
        dma((2, 3)), dma((steps, 3)), dma((3,)),
        dma((steps, 8)), dma((steps, 8)),
        dma((batches,)), dma((batches,)),
        dma((batches, steps - 1)), dma((batches, steps - 1)),
        dma((batches, near_count - 1)), dma((batches, near_count - 1)),
        dma((batches, far_slots)), dma((batches, far_slots)),
        dma((batches, near_count - 1)), dma((batches, near_count - 1)),
        dma((batches, steps - 1)), dma((3, steps - 1)),
        dma((3,)), dma((3,)),
        dma((1,)), dma((1,)),
        dma((tiny,)), dma((tiny,)),
    ]
    scale = 1.0 / (latent.shape[0] * lines)
    outs = pl.pallas_call(
        functools.partial(kernel, scale, near_count, far_count),
        out_shape=(
            jax.ShapeDtypeStruct((rows, feat), F32),
            jax.ShapeDtypeStruct(entry_w.shape, F32),
            jax.ShapeDtypeStruct(block_w.shape, F32),
            jax.ShapeDtypeStruct(action_w.shape, F32),
            jax.ShapeDtypeStruct(chance_w.shape, F32),
            jax.ShapeDtypeStruct(gain_w.shape, F32),
            jax.ShapeDtypeStruct(shift_w.shape, F32),
            jax.ShapeDtypeStruct((head_width, feat), F32),
            jax.ShapeDtypeStruct((chance_head.shape[1], feat), F32),
            jax.ShapeDtypeStruct((1, 1), F32),
            jax.ShapeDtypeStruct((steps - 2, 2, 15, feat, rows), BF16),
        ),
        in_specs=[anys] + [vmem] * 5 + [anys] * 2 + [vmem] * 6,
        out_specs=(vmem,) * 10 + (anys,),
        scratch_shapes=scratch,
        compiler_params=pltpu.CompilerParams(
            vmem_limit_bytes=63 * 2**20, collective_id=0, has_side_effects=True
        ),
    )(
        latent, lengths.reshape(1, -1), actions, chances, value_bins, reward_bins,
        entry_w, block_w.reshape(1, 2, 4, feat, feat), action_w, chance_w, gain_w, shift_w,
        state_head.T, chance_head.T,
    )
    return (outs[0].reshape(rows, 1, feat), outs[1], outs[3], outs[4], outs[2], outs[5], outs[6]) + (outs[7].T, outs[8].T, outs[9].reshape(()))


def solution(mesh):
    placed = (
        P("dp", None), P("dp"), P(None, "dp"), P(None, "dp"), P(None, "dp"), P(None, "dp"),
        P("section", None, None, None), P("section", None, None), P("section", None, None),
        P("section", None, None, None, None, None), P("section", None, None, None), P("section", None, None, None),
        P(), P(),
    )
    return jax.shard_map(
        per_device,
        mesh=mesh,
        in_specs=placed,
        out_specs=(
            P("dp", "section", None), P("section", None, None, None), P("section", None, None),
            P("section", None, None), P("section", None, None, None, None, None),
            P("section", None, None, None), P("section", None, None, None), P(), P(), P(),
        ),
        check_vma=False,
    )
```

```python
import functools

import jax
import jax.numpy as jnp
from jax import lax
from jax.experimental import pallas as pl
from jax.experimental.pallas import tpu as pltpu
from jax.sharding import PartitionSpec as P

F32 = jnp.float32
BF16 = jnp.bfloat16
ROOT = 0.7978845608028654
K1 = 2.0 * ROOT
K2 = 8.0 * ROOT * 0.044715
EPS = 1e-05
WIDE = 256
LANES = 128
NORMS = 5
ACT_ROW = 32
GAIN_ROW = 36
SHIFT_ROW = 46
MISC_ROWS = 64


def contract(left, right, left_dim, right_dim):
    return lax.dot_general(
        left, right, (((left_dim,), (right_dim,)), ((), ())), preferred_element_type=F32
    )


def gelu_pair(half):
    inner = half * (half * half * K2 + K1)
    plus = jnp.tanh(inner) + 1.0
    out = half * plus
    slope = inner * 3.0 - half * (2.0 * K1)
    return out, (plus * ((2.0 - plus) * slope + 1.0)).astype(BF16)


BAND = 32
QUARTER = 320
LAST = 384
CHAIN = ((0, 1), (1, 2), (2, 3), (3, 4), (4, 6), (6, 8), (8, 10))
EARLY = (7, 0, 1, 2, 3, 4)
LATE = (5, 6)
MESH = pl.DeviceIdType.MESH
TICK_AT = 1
PART_LAG, NEAR_LAG, FILL_LAG, OWN_LAG, DONE_LAG = 2, 4, 6, 9, 10


def when(condition, action):
    if isinstance(condition, bool):
        if condition:
            action()
    else:
        pl.when(condition)(action)


def kernel(
    scale, near_count, far_count,
    latent, lengths, actions, chances, values, rewards, entry, blocks, action_w, chance_w, gains, shifts,
    state_head, chance_head,
    latent_out, both, misc_both, loss_out, spill,
    weights, misc, head, acts, inv, ids, onehot, current, resid, prod_a, prod_b, grad, gb, acc_dy, acc_p,
    logits, dlogits, dchance, head_back, head_sum, chead_sum, misc_grad, loss_sum, sel, stage, states,
    sent, core_in, core_sum, part_in, part_sum, near_in, far_in, quarter, loss_in,
    load_sem, spill_sem, chain_send, chain_recv, give_send, step_recv, pass_send, pair_send, pair_recv,
    core_send, core_recv, part_send, part_recv, near_send, near_recv, far_send, far_recv,
    fill_send, fill_recv, own_send, own_recv, lane_send, lane_recv, extra_send, extra_recv, loss_send, loss_recv,
):
    section = lax.axis_index("section")
    line = lax.axis_index("dp")
    core = lax.rem(line, 2)
    near = lax.rem(line // 2, near_count)
    far = line // 2 // near_count
    mate = line + 1 - 2 * core
    rows = current.shape[1]
    steps = weights.shape[0]
    feat = WIDE
    head_width = state_head.shape[0]
    bins = (head_width - action_w.shape[1]) // 2
    head_pad = head.shape[0]
    action_count = action_w.shape[1]
    chance_count = chance_w.shape[1]
    chunks = [slice(c, c + WIDE) for c in range(0, rows, WIDE)]
    batches = 2 * steps

    def subs(part):
        return [slice(c, c + LANES) for c in range(part.start, part.stop, LANES)]

    def near_line(offset):
        return (far * near_count + lax.rem(near + offset, near_count)) * 2 + core

    def far_line(offset):
        return (lax.rem(far + offset, far_count) * near_count + near) * 2 + core

    def section_at(offset):
        return lax.rem(section + offset, steps)

    barrier = pltpu.get_barrier_semaphore()
    peers = [{"dp": mate}]
    peers += [{"section": section_at(o)} for o in range(1, steps)]
    peers += [{"dp": near_line(o)} for o in range(1, near_count)]
    peers += [{"dp": far_line(o)} for o in range(1, far_count)]
    for peer in peers:
        pl.semaphore_signal(barrier, inc=1, device_id=peer, device_id_type=MESH)

    loads = [(entry.at[0, 0], weights.at[section, 0]), (blocks.at[0, 0], weights.at[section, 1:5])]
    loads += [(entry.at[0, 1], weights.at[section, 5]), (blocks.at[0, 1], weights.at[section, 6:10])]
    loads += [(latent, states)]
    loads = [pltpu.make_async_copy(src, dst, load_sem.at[n]) for n, (src, dst) in enumerate(loads)]
    for load in loads:
        load.start()
    head[head_width // 16 * 16 : head_pad] = jnp.zeros((head_pad - head_width // 16 * 16, feat), BF16)
    head[0:head_width] = state_head[...]

    packed = jnp.concatenate(
        [
            chance_w[0].astype(F32),
            action_w[0].astype(F32),
            gains[0, :, 0].astype(F32),
            gains[0, :, 1].astype(F32),
            shifts[0, :, 0].astype(F32),
            shifts[0, :, 1].astype(F32),
            jnp.zeros((MISC_ROWS - SHIFT_ROW - 2 * NORMS, feat), F32),
        ],
        axis=0,
    )
    misc[section] = packed.astype(BF16)

    def send(src, dst, sender, receiver, peer):
        return pltpu.make_async_remote_copy(
            src_ref=src, dst_ref=dst, send_sem=sender, recv_sem=receiver, device_id=peer, device_id_type=MESH
        )

    def landed(dst, receiver):
        send(dst, dst, load_sem.at[7], receiver, {"dp": mate}).wait_recv()

    place = jnp.where(section >= 2, 5 - section, section)
    after = lax.rem(place + 1 + 2 * core, steps)
    after = jnp.where(after >= 2, 5 - after, after)
    hops = jnp.where(core == 0, place, lax.rem(steps - place, steps))
    side_a = section + 1 - 2 * lax.rem(section, 2)
    side_b = lax.rem(section + 2, steps)
    pass_step = jnp.where(core == 0, side_a, side_b)
    pass_to = jnp.where(core == 0, side_b, side_a)

    def half_of(step, first, last, part):
        at = pl.multiple_of(part * (feat // 2), feat // 2)
        return weights.at[step, first:last, pl.ds(at, feat // 2)]

    def misc_half(step, part):
        return misc.at[step, pl.ds(pl.multiple_of(part * (MISC_ROWS // 2), MISC_ROWS // 2), MISC_ROWS // 2)]

    def piece(step, n, part):
        if isinstance(step, int) and step == 0:
            return misc_half(0, part) if n == 7 else half_of(0, *CHAIN[n], part)
        return misc_half(step, part) if n == 2 else half_of(step, 5 * n, 5 * n + 5, part)

    def chain(n):
        ref = piece(0, n, core)
        return send(ref, ref, chain_send.at[n], chain_recv.at[n], {"section": after})

    def give(way, n):
        ref = piece(section, n, core)
        return send(ref, ref, give_send.at[way, n], step_recv.at[section, n], {"section": (side_a, side_b)[way]})

    def hand_on(n):
        ref = piece(pass_step, n, core)
        return send(ref, ref, pass_send.at[n], step_recv.at[pass_step, n], {"section": pass_to})

    def pair(step, n):
        ref = piece(step, n, core)
        return send(ref, ref, pair_send.at[step, n], pair_recv.at[step, n], {"dp": mate})

    def chain_on(order, onward):
        def run():
            for n in order:
                landed(piece(0, n, core), chain_recv.at[n])
                if onward:
                    chain(n).start()
                pair(0, n).start()

        return run

    def need_first(order):
        def run():
            for n in order:
                landed(piece(0, n, 1 - core), pair_recv.at[0, n])

        when(section != 0, run)

    def hand_on_now(condition, pieces):
        def run():
            for n in pieces:
                landed(piece(pass_step, n, core), step_recv.at[pass_step, n])
                hand_on(n).start()

        when(condition, run)

    def pair_now(step, pieces):
        def run():
            for n in pieces:
                pl.when(pass_step != step)(functools.partial(landed, piece(step, n, core), step_recv.at[step, n]))
                pair(step, n).start()

        when(section != step, run)

    def need(step, pieces):
        def run():
            for n in pieces:
                landed(piece(step, n, 1 - core), pair_recv.at[step, n])

        when(section != step, run)

    def give_now(way):
        def run():
            for n in (2, 0, 1):
                give(way, n).start()

        return run

    pl.semaphore_wait(barrier, len(peers))
    for load in loads[0:4]:
        load.wait()

    @pl.when(hops == 0)
    def _():
        for n in EARLY + LATE:
            chain(n).start()

    pl.when(section == 1)(give_now(0))
    pl.when(section == 2)(give_now(1))

    pick_at = lax.broadcasted_iota(jnp.int32, (steps * WIDE, WIDE), 0)
    pick_to = lax.broadcasted_iota(jnp.int32, (steps * WIDE, WIDE), 1)
    sel[...] = (pick_at == steps * pick_to + section).astype(F32).astype(BF16)
    stage[...] = jnp.zeros_like(stage)
    stage[0:1] = lengths[...].astype(F32)
    stage[1:6] = actions[...].astype(F32)
    stage[6:10] = chances[...].astype(F32)
    stage[10:14] = lax.shift_right_logical(values[...], 5).astype(F32)
    stage[14:18] = (values[...] & 31).astype(F32)
    stage[18:22] = lax.shift_right_logical(rewards[...], 5).astype(F32)
    stage[22:26] = (rewards[...] & 31).astype(F32)
    for load in loads[4:]:
        load.wait()
    for n, part in enumerate(chunks):
        rows_in = slice(n * steps * WIDE, (n + 1) * steps * WIDE)
        current[:, part] = contract(states[rows_in], sel[...], 0, 0).astype(BF16)
        got = contract(stage[:, rows_in].astype(BF16), sel[...], 1, 0)
        value_ids = got[10:14] * 32.0 + got[14:18]
        reward_ids = got[18:22] * 32.0 + got[22:26]
        for k in range(steps):
            ids[k, 0:1, part] = got[0:1]
            ids[k, 1:3, part] = got[1 + k : 3 + k]
            ids[k, 3:4, part] = got[6 + k : 7 + k]
            ids[k, 4:5, part] = value_ids[k : k + 1]
            ids[k, 5:6, part] = reward_ids[k : k + 1]
    head_sum[...] = jnp.zeros_like(head_sum)
    chead_sum[...] = jnp.zeros_like(chead_sum)
    loss_sum[...] = jnp.zeros_like(loss_sum)

    pl.when((hops == 1) | (hops == 2))(chain_on(EARLY + LATE, True))
    pl.when(hops == 3)(chain_on(EARLY[:4], False))
    pl.when((section == 1) & (core == 1))(give_now(1))
    pl.when((section == 2) & (core == 1))(give_now(0))
    pl.when(section == 3)(give_now(1))
    pl.when(hops == 3)(chain_on(EARLY[4:], False))
    pl.when((section == 2) & (core == 0))(give_now(0))
    need_first(EARLY)

    def spread_norms(k, tower, with_shift):
        count = 2 * NORMS if with_shift else NORMS
        row = lax.broadcasted_iota(jnp.int32, (MISC_ROWS, count * LANES), 0)
        at = lax.broadcasted_iota(jnp.int32, (MISC_ROWS, count * LANES), 1) // LANES
        gain_row = GAIN_ROW + tower * NORMS
        shift_row = SHIFT_ROW + tower * NORMS
        pick = jnp.where((at < NORMS) & (row == gain_row + at), 8.0, 0.0)
        pick = pick + jnp.where((at >= NORMS) & (row == shift_row + at - NORMS), 0.5, 0.0)
        gb[:, 0 : count * LANES] = contract(misc[k], pick.astype(BF16), 0, 0)

    def gain_of(n, band=slice(None)):
        return gb[band, n * LANES : (n + 1) * LANES]

    def shift_of(n, band=slice(None)):
        return gb[band, (NORMS + n) * LANES : (NORMS + n + 1) * LANES]

    def lookup(k, tower):
        lo = ACT_ROW if tower == 0 else 0
        return slice(lo, lo + 32)

    def tower_forward(k, tower):
        slot = lax.rem(k, 2)
        act = acts.at[slot, tower]
        spread_norms(k, tower, True)
        act[0] = current[...]
        look = lookup(k, tower)

        def multiply(n, part):
            matrix = weights[k, 5 * tower + n]
            if n == 0:
                got = contract(matrix, act[0, :, part], 0, 0)
                return got + contract(misc[k, look], onehot[look, part], 0, 0)
            return contract(matrix, act[1 + n // 2 if n % 2 == 1 else 2 + n // 2, :, part], 0, 0)

        def apply(n, sub, values):
            values = values - jnp.sum(values, axis=0, keepdims=True) * (1.0 / feat)
            inverse = lax.rsqrt(jnp.sum(values * values, axis=0, keepdims=True) + feat * EPS)
            inv[2 * k + tower, n : n + 1, sub] = inverse
            for r in range(0, feat, BAND):
                band = slice(r, r + BAND)
                unit = values[band] * inverse
                half = unit * gain_of(n, band) + shift_of(n, band)
                if n > 0 and n % 2 == 0:
                    half = half + 0.5 * resid[band, sub]
                out, slope = gelu_pair(half)
                if n == 0 or n == 2:
                    resid[band, sub] = out
                if n == 4:
                    current[band, sub] = out.astype(BF16)
                else:
                    act[1 + n // 2 if n % 2 == 0 else 3 + n // 2, band, sub] = out.astype(BF16)
                act[5 + n, band, sub] = unit.astype(BF16)
                act[10 + n, band, sub] = slope

        for n in range(NORMS):
            for part in chunks:
                values = multiply(n, part)
                for c, sub in enumerate(subs(part)):
                    apply(n, sub, values[:, c * LANES : (c + 1) * LANES])

    def softmax_block(pieces, target, live):
        top = None
        for start, stop, low, high in pieces:
            part = logits[start:stop]
            if (low, high) != (start, stop):
                row = lax.broadcasted_iota(jnp.int32, part.shape, 0) + start
                part = jnp.where((row >= low) & (row < high), part, -jnp.inf)
            best = jnp.max(part, axis=0, keepdims=True)
            top = best if top is None else jnp.maximum(top, best)
        total = None
        hit = None
        for start, stop, low, high in pieces:
            part = logits[start:stop] - top
            row = lax.broadcasted_iota(jnp.int32, part.shape, 0) + start
            found = jnp.sum(jnp.where(row == target, part, 0.0), axis=0, keepdims=True)
            expo = jnp.exp(part)
            if (low, high) != (start, stop):
                keep = (row >= low) & (row < high)
                expo = jnp.where(keep, expo, 0.0)
                logits[start:stop] = jnp.where(keep, expo, logits[start:stop])
            else:
                logits[start:stop] = expo
            amount = jnp.sum(expo, axis=0, keepdims=True)
            total = amount if total is None else total + amount
            hit = found if hit is None else hit + found
        return live * (jnp.log(total) - hit), live / total

    def head_pass(k, tick):
        slot = lax.rem(k, 2)
        for part in chunks:
            if part.start == WIDE:
                tick()
            for sub in subs(part):
                live = jnp.where(ids[k, 0:1, sub] > k.astype(F32), 1.0, 0.0)
                value_at = ids[k, 4:5, sub].astype(jnp.int32)
                reward_at = ids[k, 5:6, sub].astype(jnp.int32) + bins
                policy_at = ids[k, 2:3, sub].astype(jnp.int32) + 2 * bins
                chance_at = ids[k, 3:4, sub].astype(jnp.int32)
                logits[...] = contract(head[...], current[:, sub], 1, 0)
                edge_a = bins // 8 * 8
                edge_b = 2 * bins // 8 * 8
                loss = None
                scales = []
                for pieces, target in (
                    (((0, edge_a, 0, edge_a), (edge_a, edge_a + 8, edge_a, bins)), value_at),
                    (
                        (
                            (edge_a, edge_a + 8, bins, edge_a + 8),
                            (edge_a + 8, edge_b, edge_a + 8, edge_b),
                            (edge_b, edge_b + 8, edge_b, 2 * bins),
                        ),
                        reward_at,
                    ),
                    (((edge_b, edge_b + 8, 2 * bins, head_width),), policy_at),
                ):
                    lost, scale = softmax_block(pieces, target, live)
                    loss = lost if loss is None else loss + lost
                    scales.append(scale)
                low_a = bins // 16 * 16
                low_b = 2 * bins // 16 * 16
                for start, stop in (
                    (0, low_a),
                    (low_a, low_a + 16),
                    (low_a + 16, low_b),
                    (low_b, low_b + 16),
                ):
                    row = lax.broadcasted_iota(jnp.int32, (stop - start, LANES), 0) + start
                    expo = logits[start:stop]
                    if stop <= bins:
                        delta = expo * scales[0] - jnp.where(row == value_at, live, 0.0)
                    elif start >= bins and stop <= 2 * bins:
                        delta = expo * scales[1] - jnp.where(row == reward_at, live, 0.0)
                    else:
                        scale = jnp.where(row < bins, scales[0], jnp.where(row < 2 * bins, scales[1], scales[2]))
                        delta = expo * scale
                        for target in (value_at, reward_at, policy_at):
                            delta = delta - jnp.where(row == target, live, 0.0)
                        delta = jnp.where(row < head_width, delta, 0.0)
                    dlogits[start:stop, sub] = delta.astype(BF16)
                if low_b + 16 < head_pad:
                    dlogits[low_b + 16 : head_pad, sub] = jnp.zeros((head_pad - low_b - 16, LANES), BF16)
                chance_logit = contract(chance_head[...], acts[slot, 1, 0, :, sub], 1, 0)
                chance_logit = chance_logit - jnp.max(chance_logit, axis=0, keepdims=True)
                expo = jnp.exp(chance_logit)
                total = jnp.sum(expo, axis=0, keepdims=True)
                row = lax.broadcasted_iota(jnp.int32, chance_logit.shape, 0)
                hot = row == chance_at
                hit = jnp.sum(jnp.where(hot, chance_logit, 0.0), axis=0, keepdims=True)
                loss = loss + live * (jnp.log(total) - hit)
                delta = expo * (live / total) - jnp.where(hot, live, 0.0)
                dchance[k, :, sub] = delta.astype(BF16)
                loss_sum[0:1] += loss
        head_sum[...] += contract(dlogits[...], current[...], 1, 1)
        chead_sum[...] += contract(dchance[k], acts[slot, 1, 0], 1, 1)
        for part in chunks:
            head_back[k, :, part] = contract(head[...], dlogits[:, part], 0, 0)

    def make_onehot(k):
        row = lax.broadcasted_iota(jnp.int32, (MISC_ROWS, rows), 0)
        chance_at = ids[k, 3:4].astype(jnp.int32)
        action_at = ids[k, 1:2].astype(jnp.int32) + ACT_ROW
        onehot[...] = jnp.where((row == chance_at) | (row == action_at), 1.0, 0.0).astype(BF16)

    def spill_copy(k):
        return pltpu.make_async_copy(acts.at[lax.rem(k, 2)], spill.at[k], spill_sem.at[k])

    def fill_copy(k):
        return pltpu.make_async_copy(spill.at[k], acts.at[lax.rem(k, 2)], spill_sem.at[2 + k])

    @pl.loop(0, steps)
    def _(k):
        @pl.when(k >= 2)
        def _():
            spill_copy(k - 2).wait()

        @pl.when(k == 1)
        def _():
            need(1, (2, 0))
            hand_on_now(pass_step == 2, (2, 0))

        @pl.when(k == 2)
        def _():
            need(2, (2, 0))

        @pl.when(k == 3)
        def _():
            need(3, (2, 0))

        make_onehot(k)
        tower_forward(k, 0)

        @pl.when(k == 0)
        def _():
            pl.when(hops == 3)(chain_on(LATE, False))
            need_first(LATE)
            pl.when((section == 1) & (core == 0))(give_now(1))
            hand_on_now(pass_step == 1, (2, 0))

        @pl.when(k == 1)
        def _():
            pair_now(1, (1,))
            hand_on_now(pass_step == 2, (1,))
            need(1, (1,))

        @pl.when(k == 2)
        def _():
            hand_on_now(pass_step == 3, (1,))
            need(2, (1,))

        @pl.when(k == 3)
        def _():
            pair_now(3, (1,))
            need(3, (1,))

        tower_forward(k, 1)

        @pl.when(k == 0)
        def _():
            hand_on_now(pass_step == 1, (1,))
            pl.when(section == 3)(give_now(0))

        @pl.when(k == 1)
        def _():
            pair_now(2, (2, 0))

        def tick():
            @pl.when(k == 0)
            def _():
                pair_now(1, (2, 0))

            @pl.when(k == 1)
            def _():
                pair_now(2, (1,))
                hand_on_now(pass_step == 3, (2, 0))

            @pl.when(k == 2)
            def _():
                pair_now(3, (2, 0))

        head_pass(k, tick)

        @pl.when(k < steps - 2)
        def _():
            spill_copy(k).start()

    @pl.when(hops < 3)
    def _():
        for n in EARLY + LATE:
            chain(n).wait_send()

    @pl.when(section != 0)
    def _():
        for n in EARLY + LATE:
            pair(0, n).wait_send()
        for way in range(2):
            for n in range(3):
                give(way, n).wait_send()

    @pl.when(pass_step != 0)
    def _():
        for n in range(3):
            hand_on(n).wait_send()

    for step in range(1, steps):
        @pl.when(section != step)
        def _():
            for n in range(3):
                pair(step, n).wait_send()

    def lanes(part):
        return pl.ds(pl.multiple_of(part * LANES, LANES), LANES)

    def core_copy(b, slot, count):
        return send(
            sent.at[slot, :, 0:count, lanes(1 - core)], core_in.at[slot, :, 0:count],
            core_send.at[b], core_recv.at[b], {"dp": mate},
        )

    def part_copy(b, slot, count, offset):
        return send(
            core_sum.at[slot, section_at(offset), 0:count], part_in.at[b, offset - 1, 0:count],
            part_send.at[b, offset - 1], part_recv.at[b, offset - 1], {"section": section_at(offset)},
        )

    def near_rows(count, offset):
        size = count // near_count
        return pl.ds(pl.multiple_of(lax.rem(near + offset, near_count) * size, 16), size)

    def near_copy(b, slot, count, offset):
        return send(
            part_sum.at[slot, near_rows(count, offset)], near_in.at[b, offset - 1, 0 : count // near_count],
            near_send.at[b, offset - 1], near_recv.at[b, offset - 1], {"dp": near_line(offset)},
        )

    def far_copy(b, slot, count, offset):
        return send(
            quarter.at[b, near_rows(count, 0)], far_in.at[b, offset - 1, 0 : count // near_count],
            far_send.at[b, offset - 1], far_recv.at[b, offset - 1], {"dp": far_line(offset)},
        )

    def fill_back(b, count, offset):
        ref = quarter.at[b, near_rows(count, 0)]
        return send(ref, ref, fill_send.at[b, offset - 1], fill_recv.at[b, offset - 1], {"dp": near_line(offset)})

    def core_wait(b, slot, count):
        core_copy(b, slot, count).wait()
        for j in range(steps):
            mine = sent[slot, j, 0:count, lanes(core)].astype(F32)
            core_sum[slot, j, 0:count] = (mine + core_in[slot, j, 0:count].astype(F32)).astype(BF16)
        for offset in range(1, steps):
            part_copy(b, slot, count, offset).start()

    def part_wait(b, slot, count):
        for offset in range(1, steps):
            part_copy(b, slot, count, offset).wait()
        total = core_sum[slot, section, 0:count].astype(F32)
        for n in range(steps - 1):
            total = total + part_in[b, n, 0:count].astype(F32)
        part_sum[slot, 0:count] = total.astype(BF16)
        for offset in range(1, near_count):
            near_copy(b, slot, count, offset).start()

    def near_wait(b, slot, count):
        for offset in range(1, near_count):
            near_copy(b, slot, count, offset).wait()
        size = count // near_count
        total = part_sum[slot, near_rows(count, 0)].astype(F32)
        for n in range(near_count - 1):
            total = total + near_in[b, n, 0:size].astype(F32)
        quarter[b, near_rows(count, 0)] = total.astype(BF16)
        if far_count > 1:
            for offset in range(1, far_count):
                far_copy(b, slot, count, offset).start()
            for offset in range(1, far_count):
                far_copy(b, slot, count, offset).wait()
            for n in range(far_count - 1):
                total = total + far_in[b, n, 0:size].astype(F32)
            quarter[b, near_rows(count, 0)] = total.astype(BF16)
        for offset in range(1, near_count):
            fill_back(b, count, offset).start()

    def fill_wait(b, count):
        for offset in range(1, near_count):
            fill_back(b, count, offset).wait_send()
            landed(quarter.at[b, near_rows(count, near_count - offset)], fill_recv.at[b, offset - 1])

    def owner_copy(b, tower, offset):
        return send(
            quarter.at[b, 0:QUARTER], both.at[core, tower, section], own_send.at[b, offset - 1],
            own_recv.at[tower, offset - 1], {"section": section_at(steps - offset)},
        )

    def share_start(b, tower):
        def keep():
            both[core, tower, section] = quarter[b, 0:QUARTER]

        if tower == 2:
            keep()
            for offset in range(1, steps):
                owner_copy(b, tower, offset).start()
            return
        owner = steps - 1 - (b - 1) // 2
        pl.when(section == owner)(keep)
        for offset in range(1, steps):
            pl.when(lax.rem(section - owner + steps, steps) == offset)(owner_copy(b, tower, offset).start)

    def share_wait(b, tower):
        def take():
            for offset in range(1, steps):
                landed(both.at[core, tower, section_at(offset)], own_recv.at[tower, offset - 1])
            lane_copy(tower).start()

        if tower == 2:
            for offset in range(1, steps):
                owner_copy(b, tower, offset).wait_send()
            take()
            return
        owner = steps - 1 - (b - 1) // 2
        for offset in range(1, steps):
            pl.when(lax.rem(section - owner + steps, steps) == offset)(owner_copy(b, tower, offset).wait_send)
        pl.when(section == owner)(take)

    def lane_copy(tower):
        ref = both.at[core, tower]
        return send(ref, ref, lane_send.at[tower], lane_recv.at[tower], {"dp": mate})

    def finish(b, tower):
        def run():
            lane_copy(tower).wait_send()
            landed(both.at[1 - core, tower], lane_recv.at[tower])

        if tower == 2:
            run()
        else:
            pl.when(section == steps - 1 - (b - 1) // 2)(run)

    def by_kind(b, odd, action):
        if isinstance(b, int):
            if 0 <= b <= batches:
                action(b, 1 if odd else (2 if b == 0 else 0))
        elif odd:
            pl.when(b >= 0)(functools.partial(action, b, 1))
        else:
            pl.when(b > 0)(functools.partial(action, b, 0))
            pl.when(b == 0)(functools.partial(action, b, 2))

    def rows_of(b):
        return LAST if isinstance(b, int) and b == batches else QUARTER

    def fill_and_share(b, tower):
        fill_wait(b, rows_of(b))
        share_start(b, tower)

    def ticks(at, parity):
        inside = not isinstance(at, int)

        def odd(lag):
            return (parity + lag) % 2 == 1

        by_kind(at - DONE_LAG, odd(DONE_LAG), finish)
        by_kind(at - OWN_LAG, odd(OWN_LAG), share_wait)
        by_kind(at - FILL_LAG, odd(FILL_LAG), fill_and_share)
        if inside:
            pl.when(at >= NEAR_LAG)(functools.partial(near_wait, at - NEAR_LAG, parity, QUARTER))
            pl.when(at >= PART_LAG)(functools.partial(part_wait, at - PART_LAG, parity, QUARTER))
            core_wait(at, parity, QUARTER)
        else:
            if at - NEAR_LAG <= batches:
                near_wait(at - NEAR_LAG, parity, rows_of(at - NEAR_LAG))
            if at - PART_LAG <= batches:
                part_wait(at - PART_LAG, parity, rows_of(at - PART_LAG))
            if at <= batches:
                core_wait(at, parity, rows_of(at))

    def norm_backward(d_out, slope, unit, gain, inverse, at, first):
        d_two = d_out * slope.astype(F32)
        unit = unit.astype(F32)
        weighted = d_two * unit
        if first:
            acc_dy[at] = d_two
            acc_p[at] = weighted
        else:
            acc_dy[at] += d_two
            acc_p[at] += weighted
        d_unit = d_two * gain
        mean = jnp.sum(d_unit, axis=0, keepdims=True) * (1.0 / WIDE)
        along = jnp.sum(weighted * gain, axis=0, keepdims=True)
        return ((d_unit - mean - unit * along) * inverse).astype(BF16), d_two

    def tower_backward(k, tower, at):
        slot = lax.rem(k, 2)
        act = acts.at[slot, tower]
        slot_out = tower
        spread_norms(k, tower, False)

        def put(m, value):
            size = feat // steps
            for j in range(steps):
                sent[slot_out, j, m * size : (m + 1) * size] = value[j * size : (j + 1) * size].astype(BF16)


        def norm_of(d_out, at, sub):
            return norm_backward(
                d_out,
                act[10 + at, :, sub],
                act[5 + at, :, sub],
                gain_of(at),
                inv[2 * k + tower, at : at + 1, sub],
                at,
                sub.start == 0,
            )

        for j in (1, 0):
            outer = 2 + 2 * j
            inner = 1 + 2 * j
            for part in chunks:
                for sub in subs(part):
                    d_post, d_two = norm_of(grad[:, sub], outer, sub)
                    prod_a[:, sub] = d_post
                    grad[:, sub] = 0.5 * d_two
            if j == TICK_AT:
                ticks(at, 1 - tower)
            for part in chunks:
                d_mid = contract(weights[k, 5 * tower + 2 + 2 * j], prod_a[:, part], 1, 0)
                for n, sub in enumerate(subs(part)):
                    d_pre, _ = norm_of(d_mid[:, n * LANES : (n + 1) * LANES], inner, sub)
                    prod_b[:, sub] = d_pre
            put(2 + 2 * j, contract(act[3 + j], prod_a[...], 1, 1))
            for part in chunks:
                grad[:, part] += contract(weights[k, 5 * tower + 1 + 2 * j], prod_b[:, part], 1, 0)
            put(1 + 2 * j, contract(act[1 + j], prod_b[...], 1, 1))
        for part in chunks:
            for sub in subs(part):
                d_first, _ = norm_of(grad[:, sub], 0, sub)
                prod_a[:, sub] = d_first
        look = lookup(k, tower)
        put(0, contract(act[0], prod_a[...], 1, 1))
        got = contract(onehot[look], prod_a[...], 1, 1)
        if tower == 0:
            misc_grad[k, ACT_ROW : ACT_ROW + action_count] = got[0:action_count]
        else:
            misc_grad[k, 0:32] = got
        ones = jnp.ones((16, LANES), BF16)
        for n in range(NORMS):
            total = contract(ones, acc_p[n].astype(BF16), 1, 1)
            misc_grad[k, GAIN_ROW + NORMS * tower + n : GAIN_ROW + NORMS * tower + n + 1] = 8.0 * total[0:1]
            total = contract(ones, acc_dy[n].astype(BF16), 1, 1)
            misc_grad[k, SHIFT_ROW + NORMS * tower + n : SHIFT_ROW + NORMS * tower + n + 1] = 0.5 * total[0:1]

    head_sum[head_width : head_width + chance_count] = chead_sum[...]
    for j in range(steps):
        sent[0, j, 0:QUARTER] = head_sum[j * QUARTER : (j + 1) * QUARTER].astype(BF16)
    core_copy(0, 0, QUARTER).start()

    @pl.loop(0, steps)
    def _(back):
        k = steps - 1 - back

        @pl.when(k < steps - 2)
        def _():
            fill_copy(k).wait()

        make_onehot(k)

        @pl.when(back == 0)
        def _():
            grad[...] = head_back[k]

        @pl.when(back > 0)
        def _():
            grad[...] = (0.5 * grad[...]).astype(BF16).astype(F32) + head_back[k]

        tower_backward(k, 1, 2 * back)
        core_copy(2 * back + 1, 1, QUARTER).start()
        for part in chunks:
            grad[:, part] = contract(weights[k, 5], prod_a[:, part], 1, 0) + contract(
                chance_head[...], dchance[k, :, part], 0, 0
            )
        tower_backward(k, 0, 2 * back + 1)

        @pl.when(k > 0)
        def _():
            core_copy(2 * back + 2, 0, QUARTER).start()

        @pl.when(k > 0)
        def _():
            for part in chunks:
                grad[:, part] = contract(weights[k, 0], prod_a[:, part], 1, 0)

        @pl.when(k == 0)
        def _():
            for part in chunks:
                latent_out[part] = 0.5 * contract(prod_a[:, part], weights[0, 0], 0, 1)

        @pl.when(k >= 2)
        def _():
            fill_copy(k - 2).start()

    for j in range(steps):
        sent[0, j, QUARTER:LAST] = misc_grad[j].astype(BF16)
    core_copy(batches, 0, LAST).start()

    loss_at = [{"dp": mate}] + [{"section": section_at(o)} for o in range(1, steps)]
    loss_at += [{"dp": near_line(o)} for o in range(1, near_count)]
    loss_at += [{"dp": far_line(o)} for o in range(1, far_count)]
    rounds = [1, steps - 1, near_count - 1, far_count - 1]
    bounds = [sum(rounds[:n]) for n in range(5)]

    def loss_copy(n, stage_at):
        return send(loss_sum.at[stage_at], loss_in.at[n], loss_send.at[n], loss_recv.at[n], loss_at[n])

    def loss_start(stage_at):
        for n in range(bounds[stage_at], bounds[stage_at + 1]):
            loss_copy(n, stage_at).start()

    def loss_wait(stage_at):
        total = loss_sum[stage_at]
        for n in range(bounds[stage_at], bounds[stage_at + 1]):
            loss_copy(n, stage_at).wait()
            total = total + loss_in[n]
        loss_sum[stage_at + 1] = total

    def misc_copy():
        return send(
            quarter.at[batches, QUARTER:LAST], misc_both.at[core], extra_send.at[0], extra_recv.at[0], {"dp": mate}
        )

    loss_start(0)
    for at in range(batches, batches + DONE_LAG + 1):
        ticks(at, at % 2)
        if at < batches + 3:
            loss_wait(at - batches)
            loss_start(at - batches + 1)
        if at == batches + FILL_LAG:
            misc_copy().start()
    loss_wait(3)
    loss_out[...] = jnp.sum(loss_sum[4, 0:1], axis=1, keepdims=True) * scale
    misc_both[core] = quarter[batches, QUARTER:LAST]
    misc_copy().wait_send()
    landed(misc_both.at[1 - core], extra_recv.at[0])


def finish_kernel(
    scale, latent_in, both, misc_both,
    latent_out, entry_out, block_out, action_out, chance_out, gain_out, shift_out, head_out, chead_out,
):
    steps = both.shape[2]
    feat = entry_out.shape[-1]
    size = feat // steps
    head_width = head_out.shape[0]
    chance_count = chead_out.shape[0]
    latent_out[:, 0, :] = latent_in[...]
    for part in range(2):
        lanes = slice(part * LANES, (part + 1) * LANES)
        for j in range(steps):
            at = slice(j * size, (j + 1) * size)
            for tower in range(2):
                got = both[part, tower, j].astype(F32) * scale
                entry_out[0, tower, at, lanes] = got[0:size]
                for m in range(4):
                    block_out[0, tower, m // 2, m % 2, at, lanes] = got[(m + 1) * size : (m + 2) * size]
            got = both[part, 2, j].astype(F32) * scale
            start = j * QUARTER
            stop = min(start + QUARTER, head_width)
            head_out[start:stop, lanes] = got[0 : stop - start]
            if stop < start + QUARTER:
                chead_out[:, lanes] = got[stop - start : stop - start + chance_count]
        got = misc_both[part].astype(F32) * scale
        chance_out[0, :, lanes] = got[0:chance_count]
        action_out[0, :, lanes] = got[ACT_ROW : ACT_ROW + action_out.shape[1]]
        for tower in range(2):
            for n in range(NORMS):
                at = GAIN_ROW + tower * NORMS + n
                gain_out[0, n, tower : tower + 1, lanes] = got[at : at + 1]
                at = SHIFT_ROW + tower * NORMS + n
                shift_out[0, n, tower : tower + 1, lanes] = got[at : at + 1]


def per_device(
    latent, lengths, actions, chances, value_bins, reward_bins,
    entry_w, action_w, chance_w, block_w, gain_w, shift_w, state_head, chance_head,
):
    steps = lax.axis_size("section")
    lines = lax.axis_size("dp")
    near_count = min(4, lines // 2)
    far_count = lines // 2 // near_count
    rows = latent.shape[0] // steps
    feat = latent.shape[1]
    head_width = state_head.shape[1]
    head_pad = steps * QUARTER
    batches = 2 * steps + 1
    vmem = pl.BlockSpec(memory_space=pltpu.VMEM)
    anys = pl.BlockSpec(memory_space=pl.ANY)
    dma = pltpu.SemaphoreType.DMA
    tiny = 1 + (steps - 1) + (near_count - 1) + (far_count - 1)
    far_slots = max(far_count - 1, 1)
    scratch = [
        pltpu.VMEM((steps, 10, feat, feat), BF16),
        pltpu.VMEM((steps, MISC_ROWS, feat), BF16),
        pltpu.VMEM((head_pad, feat), BF16),
        pltpu.VMEM((2, 2, 15, feat, rows), BF16),
        pltpu.VMEM((2 * steps, 8, rows), F32),
        pltpu.VMEM((steps, 8, rows), F32),
        pltpu.VMEM((MISC_ROWS, rows), BF16),
        pltpu.VMEM((feat, rows), BF16),
        pltpu.VMEM((feat, rows), F32),
        pltpu.VMEM((feat, rows), BF16),
        pltpu.VMEM((feat, rows), BF16),
        pltpu.VMEM((feat, rows), F32),
        pltpu.VMEM((feat, 2 * NORMS * LANES), F32),
        pltpu.VMEM((NORMS, feat, LANES), F32),
        pltpu.VMEM((NORMS, feat, LANES), F32),
        pltpu.VMEM((head_pad, LANES), F32),
        pltpu.VMEM((head_pad, rows), BF16),
        pltpu.VMEM((steps, 32, rows), BF16),
        pltpu.VMEM((steps, feat, rows), F32),
        pltpu.VMEM((head_pad, feat), F32),
        pltpu.VMEM((32, feat), F32),
        pltpu.VMEM((steps, MISC_ROWS, feat), F32),
        pltpu.VMEM((5, 8, LANES), F32),
        pltpu.VMEM((steps * WIDE, WIDE), BF16),
        pltpu.VMEM((32, latent.shape[0]), F32),
        pltpu.VMEM(latent.shape, BF16),
        pltpu.VMEM((2, steps, LAST, feat), BF16),
        pltpu.VMEM((2, steps, LAST, LANES), BF16),
        pltpu.VMEM((2, steps, LAST, LANES), BF16),
        pltpu.VMEM((batches, steps - 1, LAST, LANES), BF16),
        pltpu.VMEM((2, LAST, LANES), BF16),
        pltpu.VMEM((batches, near_count - 1, LAST // near_count, LANES), BF16),
        pltpu.VMEM((batches, far_slots, LAST // near_count, LANES), BF16),
        pltpu.VMEM((batches, LAST, LANES), BF16),
        pltpu.VMEM((tiny, 8, LANES), F32),
        dma((8,)),
        dma((4,)),
        dma((8,)), dma((8,)),
        dma((2, 3)), dma((steps, 3)), dma((3,)),
        dma((steps, 8)), dma((steps, 8)),
        dma((batches,)), dma((batches,)),
        dma((batches, steps - 1)), dma((batches, steps - 1)),
        dma((batches, near_count - 1)), dma((batches, near_count - 1)),
        dma((batches, far_slots)), dma((batches, far_slots)),
        dma((batches, near_count - 1)), dma((batches, near_count - 1)),
        dma((batches, steps - 1)), dma((3, steps - 1)),
        dma((3,)), dma((3,)),
        dma((1,)), dma((1,)),
        dma((tiny,)), dma((tiny,)),
    ]
    scale = 1.0 / (latent.shape[0] * lines)
    outs = pl.pallas_call(
        functools.partial(kernel, scale, near_count, far_count),
        out_shape=(
            jax.ShapeDtypeStruct((rows, feat), F32),
            jax.ShapeDtypeStruct((2, 3, steps, QUARTER, LANES), BF16),
            jax.ShapeDtypeStruct((2, MISC_ROWS, LANES), BF16),
            jax.ShapeDtypeStruct((1, 1), F32),
            jax.ShapeDtypeStruct((steps - 2, 2, 15, feat, rows), BF16),
        ),
        in_specs=[anys] + [vmem] * 5 + [anys] * 2 + [vmem] * 6,
        out_specs=(vmem,) * 4 + (anys,),
        scratch_shapes=scratch,
        compiler_params=pltpu.CompilerParams(
            vmem_limit_bytes=63 * 2**20, collective_id=0, has_side_effects=True
        ),
    )(
        latent, lengths.reshape(1, -1), actions, chances, value_bins, reward_bins,
        entry_w, block_w.reshape(1, 2, 4, feat, feat), action_w, chance_w,
        jnp.swapaxes(gain_w, 1, 2), jnp.swapaxes(shift_w, 1, 2), state_head.T, chance_head.T,
    )
    swapped = (1, gain_w.shape[2], gain_w.shape[1], feat)
    done = pl.pallas_call(
        functools.partial(finish_kernel, scale),
        out_shape=(
            jax.ShapeDtypeStruct((rows, 1, feat), F32),
            jax.ShapeDtypeStruct(entry_w.shape, F32),
            jax.ShapeDtypeStruct(block_w.shape, F32),
            jax.ShapeDtypeStruct(action_w.shape, F32),
            jax.ShapeDtypeStruct(chance_w.shape, F32),
            jax.ShapeDtypeStruct(swapped, F32),
            jax.ShapeDtypeStruct(swapped, F32),
            jax.ShapeDtypeStruct((head_width, feat), F32),
            jax.ShapeDtypeStruct((chance_head.shape[1], feat), F32),
        ),
        in_specs=[vmem] * 3,
        out_specs=(vmem,) * 9,
        compiler_params=pltpu.CompilerParams(vmem_limit_bytes=32 * 2**20),
    )(outs[0], outs[1], outs[2])
    latent_grad, entry_grad, block_grad, action_grad, chance_grad, gain_grad, shift_grad, head_grad, chead_grad = done
    return (
        latent_grad, entry_grad, action_grad, chance_grad, block_grad,
        jnp.swapaxes(gain_grad, 1, 2), jnp.swapaxes(shift_grad, 1, 2),
        head_grad.T, chead_grad.T, outs[3].reshape(()),
    )


def solution(mesh):
    placed = (
        P("dp", None), P("dp"), P(None, "dp"), P(None, "dp"), P(None, "dp"), P(None, "dp"),
        P("section", None, None, None), P("section", None, None), P("section", None, None),
        P("section", None, None, None, None, None), P("section", None, None, None), P("section", None, None, None),
        P(), P(),
    )
    return jax.shard_map(
        per_device,
        mesh=mesh,
        in_specs=placed,
        out_specs=(
            P("dp", "section", None), P("section", None, None, None), P("section", None, None),
            P("section", None, None), P("section", None, None, None, None, None),
            P("section", None, None, None), P("section", None, None, None), P(), P(), P(),
        ),
        check_vma=False,
    )
```

```python
import functools

import jax
import jax.numpy as jnp
from jax import lax
from jax.experimental import pallas as pl
from jax.experimental.pallas import tpu as pltpu
from jax.sharding import PartitionSpec as P

F32 = jnp.float32
BF16 = jnp.bfloat16
ROOT = 0.7978845608028654
K1 = 2.0 * ROOT
K2 = 8.0 * ROOT * 0.044715
EPS = 1e-05
WIDE = 256
LANES = 128
NORMS = 5
ACT_ROW = 32
GAIN_ROW = 36
SHIFT_ROW = 46
MISC_ROWS = 64


def contract(left, right, left_dim, right_dim):
    return lax.dot_general(
        left, right, (((left_dim,), (right_dim,)), ((), ())), preferred_element_type=F32
    )


def gelu_pair(half):
    inner = half * (half * half * K2 + K1)
    plus = jnp.tanh(inner) + 1.0
    out = half * plus
    slope = inner * 3.0 - half * (2.0 * K1)
    return out, (plus * ((2.0 - plus) * slope + 1.0)).astype(BF16)


BAND = 32
QUARTER = 320
LAST = 384
CHAIN = ((0, 1), (1, 2), (2, 3), (3, 4), (4, 5), (5, 6), (6, 8), (8, 10))
EARLY = (0, 8, 1, 2, 3, 4)
LATE = (5, 6, 7)
MESH = pl.DeviceIdType.MESH
TICK_AT = 1
PLACE = (4, 3, 0, 1, 2)
PART_LAG, NEAR_LAG, FILL_LAG, OWN_LAG, DONE_LAG = 2, 4, 6, 9, 10


def when(condition, action):
    if isinstance(condition, bool):
        if condition:
            action()
    else:
        pl.when(condition)(action)


def kernel(
    scale, near_count, far_count,
    latent, lengths_in, actions_in, chances_in, values_in, rewards_in, entry, blocks, action_in, chance_in, gains_in,
    shifts_in, state_in, chance_head_in,
    latent_to, both_to, misc_to, loss_out, spill,
    weights, misc, head, acts, inv, ids, onehot, current, resid, prod_a, prod_b, grad, gb, acc,
    logits, dlogits, dchance, head_back, head_sum, chead_sum, misc_grad, loss_sum, sel, stage, states,
    sent, core_in, core_sum, part_in, part_sum, near_in, far_in, quarter, loss_in,
    lengths, actions, chances, values, rewards, action_w, chance_w, gains, shifts, state_head, chance_head,
    pick, latent_out, both, misc_both, load_sem, small_sem, out_sem, spill_sem, chain_send, chain_recv, give_send, step_recv, pass_send, pair_send, pair_recv,
    core_send, core_recv, part_send, part_recv, near_send, near_recv, far_send, far_recv,
    fill_send, fill_recv, own_send, own_recv, lane_send, lane_recv, extra_send, extra_recv, loss_send, loss_recv,
):
    section = lax.axis_index("section")
    line = lax.axis_index("dp")
    core = lax.rem(line, 2)
    near = lax.rem(line // 2, near_count)
    far = line // 2 // near_count
    mate = line + 1 - 2 * core
    rows = current.shape[1]
    steps = weights.shape[0]
    feat = WIDE
    head_width = state_head.shape[0]
    bins = (head_width - action_w.shape[1]) // 2
    head_pad = head.shape[0]
    action_count = action_w.shape[1]
    chance_count = chance_w.shape[1]
    chunks = [slice(c, c + WIDE) for c in range(0, rows, WIDE)]
    batches = 2 * steps

    def subs(part):
        return [slice(c, c + LANES) for c in range(part.start, part.stop, LANES)]

    def near_line(offset):
        return (far * near_count + lax.rem(near + offset, near_count)) * 2 + core

    def far_line(offset):
        return (lax.rem(far + offset, far_count) * near_count + near) * 2 + core

    def section_at(offset):
        return lax.rem(section + offset, steps)

    barrier = pltpu.get_barrier_semaphore()
    peers = [{"dp": mate}]
    peers += [{"section": section_at(o)} for o in range(1, steps)]
    peers += [{"dp": near_line(o)} for o in range(1, near_count)]
    peers += [{"dp": far_line(o)} for o in range(1, far_count)]
    for peer in peers:
        pl.semaphore_signal(barrier, inc=1, device_id=peer, device_id_type=MESH)

    loads = [(entry.at[0, 0], weights.at[section, 0]), (blocks.at[0, 0], weights.at[section, 1:5])]
    loads += [(entry.at[0, 1], weights.at[section, 5]), (blocks.at[0, 1], weights.at[section, 6:10])]
    loads += [(latent, states)]
    small = [(chance_in, chance_w), (action_in, action_w), (gains_in, gains), (shifts_in, shifts)]
    small += [(lengths_in, lengths), (actions_in, actions), (chances_in, chances), (values_in, values)]
    small += [(rewards_in, rewards), (state_in, state_head), (chance_head_in, chance_head)]
    small = [pltpu.make_async_copy(src, dst, small_sem.at[n]) for n, (src, dst) in enumerate(small)]
    loads = [pltpu.make_async_copy(src, dst, load_sem.at[n]) for n, (src, dst) in enumerate(loads)]
    for load in loads[0:4] + small + loads[4:]:
        load.start()

    def send(src, dst, sender, receiver, peer):
        return pltpu.make_async_remote_copy(
            src_ref=src, dst_ref=dst, send_sem=sender, recv_sem=receiver, device_id=peer, device_id_type=MESH
        )

    def landed(dst, receiver):
        send(dst, dst, load_sem.at[7], receiver, {"dp": mate}).wait_recv()

    place = jnp.where(section >= 2, 5 - section, section)
    after = lax.rem(place + 1 + 2 * core, steps)
    after = jnp.where(after >= 2, 5 - after, after)
    hops = jnp.where(core == 0, place, lax.rem(steps - place, steps))
    side_a = section + 1 - 2 * lax.rem(section, 2)
    side_b = lax.rem(section + 2, steps)
    pass_step = jnp.where(core == 0, side_a, side_b)
    pass_to = jnp.where(core == 0, side_b, side_a)

    def half_of(step, first, last, part):
        at = pl.multiple_of(part * (feat // 2), feat // 2)
        return weights.at[step, first:last, pl.ds(at, feat // 2)]

    def misc_half(step, part):
        return misc.at[step, pl.ds(pl.multiple_of(part * (MISC_ROWS // 2), MISC_ROWS // 2), MISC_ROWS // 2)]

    def piece(step, n, part):
        if isinstance(step, int) and step == 0:
            return misc_half(0, part) if n == len(CHAIN) else half_of(0, *CHAIN[n], part)
        return misc_half(step, part) if n == 2 else half_of(step, 5 * n, 5 * n + 5, part)

    def chain(n):
        ref = piece(0, n, core)
        return send(ref, ref, chain_send.at[n], chain_recv.at[n], {"section": after})

    def give(way, n):
        ref = piece(section, n, core)
        return send(ref, ref, give_send.at[way, n], step_recv.at[section, n], {"section": (side_a, side_b)[way]})

    def hand_on(n):
        ref = piece(pass_step, n, core)
        return send(ref, ref, pass_send.at[n], step_recv.at[pass_step, n], {"section": pass_to})

    def pair(step, n):
        ref = piece(step, n, core)
        return send(ref, ref, pair_send.at[step, n], pair_recv.at[step, n], {"dp": mate})

    def chain_on(order, onward):
        def run():
            for n in order:
                landed(piece(0, n, core), chain_recv.at[n])
                if onward:
                    chain(n).start()
                pair(0, n).start()

        return run

    def need_first(order):
        def run():
            for n in order:
                landed(piece(0, n, 1 - core), pair_recv.at[0, n])

        when(section != 0, run)

    def hand_on_now(condition, pieces):
        def run():
            for n in pieces:
                landed(piece(pass_step, n, core), step_recv.at[pass_step, n])
                hand_on(n).start()

        when(condition, run)

    def pair_now(step, pieces):
        def run():
            for n in pieces:
                pl.when(pass_step != step)(functools.partial(landed, piece(step, n, core), step_recv.at[step, n]))
                pair(step, n).start()

        when(section != step, run)

    def need(step, pieces):
        def run():
            for n in pieces:
                landed(piece(step, n, 1 - core), pair_recv.at[step, n])

        when(section != step, run)

    def give_now(way):
        def run():
            for n in (2, 0, 1):
                give(way, n).start()

        return run

    pl.semaphore_wait(barrier, len(peers))
    for load in loads[0:2]:
        load.wait()

    @pl.when(hops == 0)
    def _():
        chain(0).start()

    for load in small[0:4]:
        load.wait()
    packed = jnp.concatenate(
        [
            chance_w[0].astype(F32),
            action_w[0].astype(F32),
            gains[0, :, 0].astype(F32),
            gains[0, :, 1].astype(F32),
            shifts[0, :, 0].astype(F32),
            shifts[0, :, 1].astype(F32),
            jnp.zeros((MISC_ROWS - SHIFT_ROW - 2 * NORMS, feat), F32),
        ],
        axis=0,
    )
    misc[section] = packed.astype(BF16)

    @pl.when(hops == 0)
    def _():
        for n in EARLY[1:]:
            chain(n).start()

    for load in loads[2:4]:
        load.wait()

    @pl.when(hops == 0)
    def _():
        for n in LATE:
            chain(n).start()

    pl.when(section == 1)(give_now(0))
    pl.when(section == 2)(give_now(1))

    pick_at = lax.broadcasted_iota(jnp.int32, (steps * WIDE, WIDE), 0)
    pick_to = lax.broadcasted_iota(jnp.int32, (steps * WIDE, WIDE), 1)
    for tower in range(2):
        row = lax.broadcasted_iota(jnp.int32, (MISC_ROWS, 2 * NORMS * LANES), 0)
        at = lax.broadcasted_iota(jnp.int32, (MISC_ROWS, 2 * NORMS * LANES), 1) // LANES
        chosen = jnp.where((at < NORMS) & (row == GAIN_ROW + tower * NORMS + at), 8.0, 0.0)
        chosen = chosen + jnp.where((at >= NORMS) & (row == SHIFT_ROW + tower * NORMS + at - NORMS), 0.5, 0.0)
        pick[tower] = chosen.astype(BF16)
    for load in small[4:]:
        load.wait()
    head[head_width // 16 * 16 : head_pad] = jnp.zeros((head_pad - head_width // 16 * 16, feat), BF16)
    head[0:head_width] = state_head[...]
    sel[...] = (pick_at == steps * pick_to + section).astype(F32).astype(BF16)
    stage[...] = jnp.zeros_like(stage)
    stage[0:1] = lengths[...].astype(F32)
    stage[1:6] = actions[...].astype(F32)
    stage[6:10] = chances[...].astype(F32)
    stage[10:14] = lax.shift_right_logical(values[...], 5).astype(F32)
    stage[14:18] = (values[...] & 31).astype(F32)
    stage[18:22] = lax.shift_right_logical(rewards[...], 5).astype(F32)
    stage[22:26] = (rewards[...] & 31).astype(F32)
    for load in loads[4:]:
        load.wait()
    for n, part in enumerate(chunks):
        rows_in = slice(n * steps * WIDE, (n + 1) * steps * WIDE)
        current[:, part] = contract(states[rows_in], sel[...], 0, 0).astype(BF16)
        got = contract(stage[:, rows_in].astype(BF16), sel[...], 1, 0)
        value_ids = got[10:14] * 32.0 + got[14:18]
        reward_ids = got[18:22] * 32.0 + got[22:26]
        for k in range(steps):
            ids[k, 0:1, part] = got[0:1]
            ids[k, 1:3, part] = got[1 + k : 3 + k]
            ids[k, 3:4, part] = got[6 + k : 7 + k]
            ids[k, 4:5, part] = value_ids[k : k + 1]
            ids[k, 5:6, part] = reward_ids[k : k + 1]
    head_sum[...] = jnp.zeros_like(head_sum)
    chead_sum[...] = jnp.zeros_like(chead_sum)
    loss_sum[...] = jnp.zeros_like(loss_sum)

    pl.when((hops == 1) | (hops == 2))(chain_on(EARLY + LATE, True))
    pl.when(hops == 3)(chain_on(EARLY[:4], False))
    pl.when((section == 1) & (core == 1))(give_now(1))
    pl.when((section == 2) & (core == 1))(give_now(0))
    pl.when(section == 3)(give_now(1))
    pl.when(hops == 3)(chain_on(EARLY[4:], False))
    pl.when((section == 2) & (core == 0))(give_now(0))
    need_first(EARLY)

    def spread_norms(k, tower, with_shift):
        width = (2 * NORMS if with_shift else NORMS) * LANES
        gb[:, 0:width] = contract(misc[k], pick[tower, :, 0:width], 0, 0)

    def gain_of(n, band=slice(None)):
        return gb[band, n * LANES : (n + 1) * LANES]

    def shift_of(n, band=slice(None)):
        return gb[band, (NORMS + n) * LANES : (NORMS + n + 1) * LANES]

    def lookup(k, tower):
        lo = ACT_ROW if tower == 0 else 0
        return slice(lo, lo + 32)

    def tower_forward(k, tower):
        slot = lax.rem(k, 2)
        act = acts.at[slot, tower]
        spread_norms(k, tower, True)
        act[0] = current[...]
        look = lookup(k, tower)

        def multiply(n, part):
            matrix = weights[k, 5 * tower + n]
            if n == 0:
                got = contract(matrix, act[0, :, part], 0, 0)
                return got + contract(misc[k, look], onehot[look, part], 0, 0)
            return contract(matrix, act[1 + n // 2 if n % 2 == 1 else 2 + n // 2, :, part], 0, 0)

        def apply(n, sub, values):
            values = values - jnp.sum(values, axis=0, keepdims=True) * (1.0 / feat)
            inverse = lax.rsqrt(jnp.sum(values * values, axis=0, keepdims=True) + feat * EPS)
            inv[2 * k + tower, n : n + 1, sub] = inverse
            for r in range(0, feat, BAND):
                band = slice(r, r + BAND)
                unit = values[band] * inverse
                half = unit * gain_of(n, band) + shift_of(n, band)
                if n > 0 and n % 2 == 0:
                    half = half + 0.5 * resid[band, sub]
                out, slope = gelu_pair(half)
                if n == 0 or n == 2:
                    resid[band, sub] = out
                if n == 4:
                    current[band, sub] = out.astype(BF16)
                else:
                    act[1 + n // 2 if n % 2 == 0 else 3 + n // 2, band, sub] = out.astype(BF16)
                act[5 + n, band, sub] = unit.astype(BF16)
                act[10 + n, band, sub] = slope

        for n in range(NORMS):
            for part in chunks:
                values = multiply(n, part)
                for c, sub in enumerate(subs(part)):
                    apply(n, sub, values[:, c * LANES : (c + 1) * LANES])

    def softmax_block(pieces, target, live):
        bands = []
        for start, stop, low, high in pieces:
            for at in range(start, stop, BAND):
                bands.append((at, min(at + BAND, stop), low, high, (low, high) != (start, stop)))

        def fold(values, op):
            parts = [values[r : r + 8] for r in range(0, values.shape[0], 8)]
            return functools.reduce(op, parts)

        top = None
        for start, stop, low, high, mixed in bands:
            part = logits[start:stop]
            if mixed:
                row = lax.broadcasted_iota(jnp.int32, part.shape, 0) + start
                part = jnp.where((row >= low) & (row < high), part, -jnp.inf)
            best = fold(part, jnp.maximum)
            top = best if top is None else jnp.maximum(top, best)
        top = jnp.max(top, axis=0, keepdims=True)
        total, hit = None, None
        for start, stop, low, high, mixed in bands:
            part = logits[start:stop] - top
            row = lax.broadcasted_iota(jnp.int32, part.shape, 0)
            found = fold(jnp.where(row == target - start, part, 0.0), jnp.add)
            expo = jnp.exp(part)
            if mixed:
                keep = (row >= low - start) & (row < high - start)
                expo = jnp.where(keep, expo, 0.0)
                logits[start:stop] = jnp.where(keep, expo, logits[start:stop])
            else:
                logits[start:stop] = expo
            amount = fold(expo, jnp.add)
            total = amount if total is None else total + amount
            hit = found if hit is None else hit + found
        total = jnp.sum(total, axis=0, keepdims=True)
        hit = jnp.sum(hit, axis=0, keepdims=True)
        return live * (jnp.log(total) - hit), live / total

    def head_pass(k, tick):
        slot = lax.rem(k, 2)
        for part in chunks:
            if part.start == WIDE:
                tick()
            for sub in subs(part):
                live = jnp.where(ids[k, 0:1, sub] > k.astype(F32), 1.0, 0.0)
                value_at = ids[k, 4:5, sub].astype(jnp.int32)
                reward_at = ids[k, 5:6, sub].astype(jnp.int32) + bins
                policy_at = ids[k, 2:3, sub].astype(jnp.int32) + 2 * bins
                chance_at = ids[k, 3:4, sub].astype(jnp.int32)
                logits[...] = contract(head[...], current[:, sub], 1, 0)
                edge_a = bins // 8 * 8
                edge_b = 2 * bins // 8 * 8
                loss = None
                scales = []
                for pieces, target in (
                    (((0, edge_a, 0, edge_a), (edge_a, edge_a + 8, edge_a, bins)), value_at),
                    (
                        (
                            (edge_a, edge_a + 8, bins, edge_a + 8),
                            (edge_a + 8, edge_b, edge_a + 8, edge_b),
                            (edge_b, edge_b + 8, edge_b, 2 * bins),
                        ),
                        reward_at,
                    ),
                    (((edge_b, edge_b + 8, 2 * bins, head_width),), policy_at),
                ):
                    lost, scale = softmax_block(pieces, target, live)
                    loss = lost if loss is None else loss + lost
                    scales.append(scale)
                low_a = bins // 16 * 16
                low_b = 2 * bins // 16 * 16
                cuts = [*range(0, low_a, BAND), low_a, *range(low_a + 16, low_b, BAND), low_b, low_b + 16]
                for start, stop in zip(cuts[:-1], cuts[1:]):
                    row = lax.broadcasted_iota(jnp.int32, (stop - start, LANES), 0)
                    expo = logits[start:stop]
                    if stop <= bins:
                        delta = expo * scales[0] - jnp.where(row == value_at - start, live, 0.0)
                    elif start >= bins and stop <= 2 * bins:
                        delta = expo * scales[1] - jnp.where(row == reward_at - start, live, 0.0)
                    else:
                        row = row + start
                        scale = jnp.where(row < bins, scales[0], jnp.where(row < 2 * bins, scales[1], scales[2]))
                        delta = expo * scale
                        for target in (value_at, reward_at, policy_at):
                            delta = delta - jnp.where(row == target, live, 0.0)
                        delta = jnp.where(row < head_width, delta, 0.0)
                    dlogits[start:stop, sub] = delta.astype(BF16)
                if low_b + 16 < head_pad:
                    dlogits[low_b + 16 : head_pad, sub] = jnp.zeros((head_pad - low_b - 16, LANES), BF16)
                chance_logit = contract(chance_head[...], acts[slot, 1, 0, :, sub], 1, 0)
                chance_logit = chance_logit - jnp.max(chance_logit, axis=0, keepdims=True)
                expo = jnp.exp(chance_logit)
                total = jnp.sum(expo, axis=0, keepdims=True)
                row = lax.broadcasted_iota(jnp.int32, chance_logit.shape, 0)
                hot = row == chance_at
                hit = jnp.sum(jnp.where(hot, chance_logit, 0.0), axis=0, keepdims=True)
                loss = loss + live * (jnp.log(total) - hit)
                delta = expo * (live / total) - jnp.where(hot, live, 0.0)
                dchance[k, :, sub] = delta.astype(BF16)
                loss_sum[0:1] += loss
        head_sum[...] += contract(dlogits[...], current[...], 1, 1)
        chead_sum[...] += contract(dchance[k], acts[slot, 1, 0], 1, 1)
        for part in chunks:
            head_back[k, :, part] = contract(head[...], dlogits[:, part], 0, 0)

    def make_onehot(k):
        row = lax.broadcasted_iota(jnp.int32, (MISC_ROWS, rows), 0)
        chance_at = ids[k, 3:4].astype(jnp.int32)
        action_at = ids[k, 1:2].astype(jnp.int32) + ACT_ROW
        onehot[...] = jnp.where((row == chance_at) | (row == action_at), 1.0, 0.0).astype(BF16)

    def spill_copy(k):
        return pltpu.make_async_copy(acts.at[lax.rem(k, 2)], spill.at[k], spill_sem.at[k])

    def fill_copy(k):
        return pltpu.make_async_copy(spill.at[k], acts.at[lax.rem(k, 2)], spill_sem.at[2 + k])

    @pl.loop(0, steps)
    def _(k):
        @pl.when(k >= 2)
        def _():
            spill_copy(k - 2).wait()

        @pl.when(k == 1)
        def _():
            need(1, (2, 0))
            hand_on_now(pass_step == 2, (2, 0))

        @pl.when(k == 2)
        def _():
            need(2, (2, 0))

        @pl.when(k == 3)
        def _():
            need(3, (2, 0))

        make_onehot(k)
        tower_forward(k, 0)

        @pl.when(k == 0)
        def _():
            pl.when(hops == 3)(chain_on(LATE, False))
            need_first(LATE)
            pl.when((section == 1) & (core == 0))(give_now(1))
            hand_on_now(pass_step == 1, (2, 0))

        @pl.when(k == 1)
        def _():
            pair_now(1, (1,))
            hand_on_now(pass_step == 2, (1,))
            need(1, (1,))

        @pl.when(k == 2)
        def _():
            hand_on_now(pass_step == 3, (1,))
            need(2, (1,))

        @pl.when(k == 3)
        def _():
            pair_now(3, (1,))
            need(3, (1,))

        tower_forward(k, 1)

        @pl.when(k == 0)
        def _():
            hand_on_now(pass_step == 1, (1,))
            pl.when(section == 3)(give_now(0))

        @pl.when(k == 1)
        def _():
            pair_now(2, (2, 0))

        def tick():
            @pl.when(k == 0)
            def _():
                pair_now(1, (2, 0))

            @pl.when(k == 1)
            def _():
                pair_now(2, (1,))
                hand_on_now(pass_step == 3, (2, 0))

            @pl.when(k == 2)
            def _():
                pair_now(3, (2, 0))

        head_pass(k, tick)

        @pl.when(k < steps - 2)
        def _():
            spill_copy(k).start()

    @pl.when(hops < 3)
    def _():
        for n in EARLY + LATE:
            chain(n).wait_send()

    @pl.when(section != 0)
    def _():
        for n in EARLY + LATE:
            pair(0, n).wait_send()
        for way in range(2):
            for n in range(3):
                give(way, n).wait_send()

    @pl.when(pass_step != 0)
    def _():
        for n in range(3):
            hand_on(n).wait_send()

    for step in range(1, steps):
        @pl.when(section != step)
        def _():
            for n in range(3):
                pair(step, n).wait_send()

    def lanes(part):
        return pl.ds(pl.multiple_of(part * LANES, LANES), LANES)

    def span(b):
        if isinstance(b, int) and b >= batches:
            return (b - batches) * (LAST // 2), LAST // 2
        return 0, QUARTER

    def held(b):
        return min(b, batches) if isinstance(b, int) else b

    def rows_of(b):
        low, count = span(b)
        return slice(low, low + count)

    def matrix_rows(b):
        low, count = span(b)
        return slice(low, min(low + count, QUARTER))

    def turn(b, tower):
        return 3 if isinstance(b, int) and b > batches else tower

    def core_copy(b, slot):
        return send(
            sent.at[slot, :, rows_of(b), lanes(1 - core)], core_in.at[slot, :, rows_of(b)],
            core_send.at[b], core_recv.at[b], {"dp": mate},
        )

    def part_copy(b, slot, offset):
        return send(
            core_sum.at[slot, section_at(offset), rows_of(b)], part_in.at[b, offset - 1, 0 : span(b)[1]],
            part_send.at[b, offset - 1], part_recv.at[b, offset - 1], {"section": section_at(offset)},
        )

    def near_rows(b, offset):
        low, count = span(b)
        size = count // near_count
        return pl.ds(pl.multiple_of(low + lax.rem(near + offset, near_count) * size, 16), size)

    def near_copy(b, slot, offset):
        return send(
            part_sum.at[slot, near_rows(b, offset)], near_in.at[b, offset - 1, 0 : span(b)[1] // near_count],
            near_send.at[b, offset - 1], near_recv.at[b, offset - 1], {"dp": near_line(offset)},
        )

    def far_copy(b, offset):
        return send(
            quarter.at[held(b), near_rows(b, 0)], far_in.at[b, offset - 1, 0 : span(b)[1] // near_count],
            far_send.at[b, offset - 1], far_recv.at[b, offset - 1], {"dp": far_line(offset)},
        )

    def fill_back(b, offset):
        ref = quarter.at[held(b), near_rows(b, 0)]
        return send(ref, ref, fill_send.at[b, offset - 1], fill_recv.at[b, offset - 1], {"dp": near_line(offset)})

    def core_wait(b, slot):
        core_copy(b, slot).wait()
        for j in range(steps):
            mine = sent[slot, j, rows_of(b), lanes(core)].astype(F32)
            core_sum[slot, j, rows_of(b)] = (mine + core_in[slot, j, rows_of(b)].astype(F32)).astype(BF16)
        for offset in range(1, steps):
            part_copy(b, slot, offset).start()

    def part_wait(b, slot):
        for offset in range(1, steps):
            part_copy(b, slot, offset).wait()
        total = core_sum[slot, section, rows_of(b)].astype(F32)
        for n in range(steps - 1):
            total = total + part_in[b, n, 0 : span(b)[1]].astype(F32)
        part_sum[slot, rows_of(b)] = total.astype(BF16)
        for offset in range(1, near_count):
            near_copy(b, slot, offset).start()

    def near_wait(b, slot):
        for offset in range(1, near_count):
            near_copy(b, slot, offset).wait()
        size = span(b)[1] // near_count
        total = part_sum[slot, near_rows(b, 0)].astype(F32)
        for n in range(near_count - 1):
            total = total + near_in[b, n, 0:size].astype(F32)
        quarter[held(b), near_rows(b, 0)] = total.astype(BF16)
        if far_count > 1:
            for offset in range(1, far_count):
                far_copy(b, offset).start()
            for offset in range(1, far_count):
                far_copy(b, offset).wait()
            for n in range(far_count - 1):
                total = total + far_in[b, n, 0:size].astype(F32)
            quarter[held(b), near_rows(b, 0)] = total.astype(BF16)
        for offset in range(1, near_count):
            fill_back(b, offset).start()

    def fill_wait(b):
        for offset in range(1, near_count):
            fill_back(b, offset).wait_send()
            landed(quarter.at[held(b), near_rows(b, near_count - offset)], fill_recv.at[b, offset - 1])

    def owner_copy(b, tower, offset):
        return send(
            quarter.at[held(b), matrix_rows(b)], both.at[core, tower, section, matrix_rows(b)],
            own_send.at[b, offset - 1], own_recv.at[turn(b, tower), offset - 1], {"section": section_at(steps - offset)},
        )

    def owner_of(b):
        return 0 if isinstance(b, int) and b >= batches else steps - 1 - (b - 1) // 2

    def share_start(b, tower):
        def keep():
            both[core, tower, section, matrix_rows(b)] = quarter[held(b), matrix_rows(b)]

        if tower == 2:
            keep()
            for offset in range(1, steps):
                owner_copy(b, tower, offset).start()
            return
        pl.when(section == owner_of(b))(keep)
        for offset in range(1, steps):
            pl.when(lax.rem(section - owner_of(b) + steps, steps) == offset)(owner_copy(b, tower, offset).start)

    def share_wait(b, tower):
        def take():
            for offset in range(1, steps):
                landed(
                    both.at[core, tower, section_at(offset), matrix_rows(b)], own_recv.at[turn(b, tower), offset - 1]
                )
            lane_copy(b, tower).start()

        if tower == 2:
            for offset in range(1, steps):
                owner_copy(b, tower, offset).wait_send()
            take()
            return
        for offset in range(1, steps):
            pl.when(lax.rem(section - owner_of(b) + steps, steps) == offset)(owner_copy(b, tower, offset).wait_send)
        pl.when(section == owner_of(b))(take)

    def lane_copy(b, tower):
        ref = both.at[core, tower, :, matrix_rows(b)]
        return send(ref, ref, lane_send.at[turn(b, tower)], lane_recv.at[turn(b, tower)], {"dp": mate})

    def finish(b, tower):
        def run():
            lane_copy(b, tower).wait_send()
            landed(both.at[1 - core, tower, :, matrix_rows(b)], lane_recv.at[turn(b, tower)])

        if tower == 2:
            run()
        else:
            pl.when(section == owner_of(b))(run)

    def by_kind(b, odd, action):
        if odd:
            pl.when(b >= 0)(functools.partial(action, b, 1))
        else:
            pl.when(b > 0)(functools.partial(action, b, 0))
            pl.when(b == 0)(functools.partial(action, b, 2))

    def fill_and_share(b, tower):
        fill_wait(b)
        share_start(b, tower)

    def ticks(at, parity):
        def odd(lag):
            return (parity + lag) % 2 == 1

        by_kind(at - DONE_LAG, odd(DONE_LAG), finish)
        by_kind(at - OWN_LAG, odd(OWN_LAG), share_wait)
        by_kind(at - FILL_LAG, odd(FILL_LAG), fill_and_share)
        pl.when(at >= NEAR_LAG)(functools.partial(near_wait, at - NEAR_LAG, parity))
        pl.when(at >= PART_LAG)(functools.partial(part_wait, at - PART_LAG, parity))
        core_wait(at, parity)

    def tower_backward(k, tower, at):
        slot = lax.rem(k, 2)
        act = acts.at[slot, tower]
        slot_out = tower
        spread_norms(k, tower, False)

        def put(m, value):
            size = feat // steps
            at_row = PLACE[m] * size
            for j in range(steps):
                sent[slot_out, j, at_row : at_row + size] = value[j * size : (j + 1) * size].astype(BF16)

        def norm_of(d_out, at, sub, target, keep):
            means, along = None, None
            kept = []
            for r in range(0, feat, BAND):
                band = slice(r, r + BAND)
                d_two = d_out[band] * act[10 + at, band, sub].astype(F32)
                weighted = d_two * act[5 + at, band, sub].astype(F32)
                if sub.start == 0:
                    acc[NORMS + at, band] = d_two
                    acc[at, band] = weighted
                else:
                    acc[NORMS + at, band] += d_two
                    acc[at, band] += weighted
                if keep:
                    grad[band, sub] = 0.5 * d_two
                gain = gain_of(at, band)
                d_unit = d_two * gain
                kept.append(d_unit)
                part_mean = jnp.sum(d_unit.reshape(BAND // 8, 8, LANES), axis=0)
                part_along = jnp.sum((weighted * gain).reshape(BAND // 8, 8, LANES), axis=0)
                means = part_mean if means is None else means + part_mean
                along = part_along if along is None else along + part_along
            mean = jnp.sum(means, axis=0, keepdims=True) * (1.0 / feat)
            along = jnp.sum(along, axis=0, keepdims=True)
            inverse = inv[2 * k + tower, at : at + 1, sub]
            for n, r in enumerate(range(0, feat, BAND)):
                band = slice(r, r + BAND)
                unit = act[5 + at, band, sub].astype(F32)
                target[band, sub] = ((kept[n] - mean - unit * along) * inverse).astype(BF16)

        for j in (1, 0):
            outer = 2 + 2 * j
            inner = 1 + 2 * j
            for part in chunks:
                for sub in subs(part):
                    norm_of(grad[:, sub], outer, sub, prod_a, True)
            if j == TICK_AT:
                ticks(at, 1 - tower)
            for part in chunks:
                d_mid = contract(weights[k, 5 * tower + 2 + 2 * j], prod_a[:, part], 1, 0)
                for n, sub in enumerate(subs(part)):
                    norm_of(d_mid[:, n * LANES : (n + 1) * LANES], inner, sub, prod_b, False)
            put(2 + 2 * j, contract(act[3 + j], prod_a[...], 1, 1))
            if tower == 0 and j == 0:
                pl.when(k == 0)(core_copy(batches, 0).start)
            for part in chunks:
                grad[:, part] += contract(weights[k, 5 * tower + 1 + 2 * j], prod_b[:, part], 1, 0)
            put(1 + 2 * j, contract(act[1 + j], prod_b[...], 1, 1))
        for part in chunks:
            for sub in subs(part):
                norm_of(grad[:, sub], 0, sub, prod_a, False)
        look = lookup(k, tower)
        put(0, contract(act[0], prod_a[...], 1, 1))
        got = contract(onehot[look], prod_a[...], 1, 1)
        if tower == 0:
            misc_grad[k, ACT_ROW : ACT_ROW + action_count] = got[0:action_count]
        else:
            misc_grad[k, 0:32] = got
        ones = jnp.ones((16, LANES), BF16)
        both_sums = acc[...].reshape(2 * NORMS * feat, LANES).astype(BF16)
        total = contract(ones, both_sums, 1, 1)
        for n in range(NORMS):
            at_gain = GAIN_ROW + NORMS * tower + n
            at_shift = SHIFT_ROW + NORMS * tower + n
            misc_grad[k, at_gain : at_gain + 1] = 8.0 * total[0:1, n * feat : (n + 1) * feat]
            misc_grad[k, at_shift : at_shift + 1] = 0.5 * total[0:1, (NORMS + n) * feat : (NORMS + n + 1) * feat]

    head_sum[head_width : head_width + chance_count] = chead_sum[...]
    for j in range(steps):
        sent[0, j, 0:QUARTER] = head_sum[j * QUARTER : (j + 1) * QUARTER].astype(BF16)
    core_copy(0, 0).start()

    @pl.loop(0, steps)
    def _(back):
        k = steps - 1 - back

        @pl.when(k < steps - 2)
        def _():
            fill_copy(k).wait()

        make_onehot(k)

        @pl.when(back == 0)
        def _():
            grad[...] = head_back[k]

        @pl.when(back > 0)
        def _():
            grad[...] = (0.5 * grad[...]).astype(BF16).astype(F32) + head_back[k]

        tower_backward(k, 1, 2 * back)
        core_copy(2 * back + 1, 1).start()
        for part in chunks:
            grad[:, part] = contract(weights[k, 5], prod_a[:, part], 1, 0) + contract(
                chance_head[...], dchance[k, :, part], 0, 0
            )
        tower_backward(k, 0, 2 * back + 1)

        @pl.when(k > 0)
        def _():
            core_copy(2 * back + 2, 0).start()

        @pl.when(k > 0)
        def _():
            for part in chunks:
                grad[:, part] = contract(weights[k, 0], prod_a[:, part], 1, 0)

        @pl.when(k >= 2)
        def _():
            fill_copy(k - 2).start()

    for j in range(steps):
        sent[0, j, QUARTER:LAST] = misc_grad[j].astype(BF16)
    core_copy(batches + 1, 0).start()

    loss_at = [{"dp": mate}] + [{"section": section_at(o)} for o in range(1, steps)]
    loss_at += [{"dp": near_line(o)} for o in range(1, near_count)]
    loss_at += [{"dp": far_line(o)} for o in range(1, far_count)]
    rounds = [1, steps - 1, near_count - 1, far_count - 1]
    bounds = [sum(rounds[:n]) for n in range(5)]

    def loss_copy(n, stage_at):
        return send(loss_sum.at[stage_at], loss_in.at[n], loss_send.at[n], loss_recv.at[n], loss_at[n])

    def loss_start(stage_at):
        for n in range(bounds[stage_at], bounds[stage_at + 1]):
            loss_copy(n, stage_at).start()

    def loss_wait(stage_at):
        total = loss_sum[stage_at]
        for n in range(bounds[stage_at], bounds[stage_at + 1]):
            loss_copy(n, stage_at).wait()
            total = total + loss_in[n]
        loss_sum[stage_at + 1] = total

    def misc_copy():
        return send(
            quarter.at[batches, QUARTER:LAST], misc_both.at[core], extra_send.at[0], extra_recv.at[0], {"dp": mate}
        )

    loss_start(0)
    def run(phase, *numbers):
        for b in numbers:
            if phase is finish or phase is share_wait or phase is fill_and_share:
                phase(b, 2 if b == 0 else (0 if b > batches else b % 2))
            else:
                phase(b, 0 if b > batches else b % 2)

    last = batches
    run(near_wait, last - 4)
    run(part_wait, last - 2)
    run(core_wait, last)
    for part in chunks:
        latent_out[part] = 0.5 * contract(prod_a[:, part], weights[0, 0], 0, 1)
    run(core_wait, last + 1)
    outs = [(latent_out, latent_to), (misc_both, misc_to)]
    outs += [(both.at[:, n], both_to.at[:, n]) for n in (2, 1, 0)]
    outs = [pltpu.make_async_copy(src, dst, out_sem.at[n]) for n, (src, dst) in enumerate(outs)]
    outs[0].start()
    loss_wait(0)
    loss_start(1)
    run(near_wait, last - 3)
    run(fill_and_share, last - 6, last - 5)
    run(share_wait, last - 8)
    run(part_wait, last - 1)
    run(near_wait, last - 2)
    run(fill_and_share, last - 4)
    run(share_wait, last - 7)
    run(finish, last - 8)
    run(part_wait, last, last + 1)
    loss_wait(1)
    loss_start(2)
    run(fill_and_share, last - 3)
    run(near_wait, last - 1)
    run(fill_and_share, last - 2)
    run(share_wait, last - 6, last - 5)
    run(near_wait, last, last + 1)
    loss_wait(2)
    loss_start(3)
    run(fill_and_share, last - 1)
    run(share_wait, last - 4, last - 3)
    run(finish, last - 7, last - 6, last - 5)
    run(fill_and_share, last, last + 1)
    misc_copy().start()
    run(share_wait, last - 2, last - 1)
    run(finish, last - 4, last - 3, last - 2)
    outs[2].start()
    run(share_wait, last, last + 1)
    run(finish, last - 1)
    outs[3].start()
    run(finish, last, last + 1)
    outs[4].start()
    loss_wait(3)
    loss_out[...] = jnp.sum(loss_sum[4, 0:1], axis=1, keepdims=True) * scale
    misc_both[core] = quarter[batches, QUARTER:LAST]
    misc_copy().wait_send()
    landed(misc_both.at[1 - core], extra_recv.at[0])
    outs[1].start()
    for out in outs:
        out.wait()


def finish_kernel(
    scale, latent_from, both_from, misc_from,
    latent_out, entry_out, block_out, action_out, chance_out, gain_out, shift_out, head_out, chead_out,
    latent_in, both, misc_both, sem,
):
    copies = [(both_from, both), (misc_from, misc_both), (latent_from, latent_in)]
    copies = [pltpu.make_async_copy(src, dst, sem.at[n]) for n, (src, dst) in enumerate(copies)]
    for copy in copies:
        copy.start()
    steps = both.shape[2]
    feat = entry_out.shape[-1]
    size = feat // steps
    head_width = head_out.shape[0]
    chance_count = chead_out.shape[0]
    copies[0].wait()
    copies[1].wait()
    for part in range(2):
        lanes = slice(part * LANES, (part + 1) * LANES)
        for j in range(steps):
            at = slice(j * size, (j + 1) * size)
            for tower in range(2):
                got = both[part, tower, j].astype(F32) * scale
                entry_out[0, tower, at, lanes] = got[PLACE[0] * size : (PLACE[0] + 1) * size]
                for m in range(4):
                    row = PLACE[m + 1] * size
                    block_out[0, tower, m // 2, m % 2, at, lanes] = got[row : row + size]
            got = both[part, 2, j].astype(F32) * scale
            start = j * QUARTER
            stop = min(start + QUARTER, head_width)
            head_out[start:stop, lanes] = got[0 : stop - start]
            if stop < start + QUARTER:
                chead_out[:, lanes] = got[stop - start : stop - start + chance_count]
        got = misc_both[part].astype(F32) * scale
        chance_out[0, :, lanes] = got[0:chance_count]
        action_out[0, :, lanes] = got[ACT_ROW : ACT_ROW + action_out.shape[1]]
        for tower in range(2):
            for n in range(NORMS):
                at = GAIN_ROW + tower * NORMS + n
                gain_out[0, n, tower : tower + 1, lanes] = got[at : at + 1]
                at = SHIFT_ROW + tower * NORMS + n
                shift_out[0, n, tower : tower + 1, lanes] = got[at : at + 1]
    copies[2].wait()
    latent_out[:, 0, :] = latent_in[...]


def per_device(
    latent, lengths, actions, chances, value_bins, reward_bins,
    entry_w, action_w, chance_w, block_w, gain_w, shift_w, state_head, chance_head,
):
    steps = lax.axis_size("section")
    lines = lax.axis_size("dp")
    near_count = min(4, lines // 2)
    far_count = lines // 2 // near_count
    rows = latent.shape[0] // steps
    feat = latent.shape[1]
    head_width = state_head.shape[1]
    head_pad = steps * QUARTER
    batches = 2 * steps + 2
    vmem = pl.BlockSpec(memory_space=pltpu.VMEM)
    anys = pl.BlockSpec(memory_space=pl.ANY)
    dma = pltpu.SemaphoreType.DMA
    tiny = 1 + (steps - 1) + (near_count - 1) + (far_count - 1)
    far_slots = max(far_count - 1, 1)
    scratch = [
        pltpu.VMEM((steps, 10, feat, feat), BF16),
        pltpu.VMEM((steps, MISC_ROWS, feat), BF16),
        pltpu.VMEM((head_pad, feat), BF16),
        pltpu.VMEM((2, 2, 15, feat, rows), BF16),
        pltpu.VMEM((2 * steps, 8, rows), F32),
        pltpu.VMEM((steps, 8, rows), F32),
        pltpu.VMEM((MISC_ROWS, rows), BF16),
        pltpu.VMEM((feat, rows), BF16),
        pltpu.VMEM((feat, rows), F32),
        pltpu.VMEM((feat, rows), BF16),
        pltpu.VMEM((feat, rows), BF16),
        pltpu.VMEM((feat, rows), F32),
        pltpu.VMEM((feat, 2 * NORMS * LANES), F32),
        pltpu.VMEM((2 * NORMS, feat, LANES), F32),
        pltpu.VMEM((head_pad, LANES), F32),
        pltpu.VMEM((head_pad, rows), BF16),
        pltpu.VMEM((steps, 32, rows), BF16),
        pltpu.VMEM((steps, feat, rows), F32),
        pltpu.VMEM((head_pad, feat), F32),
        pltpu.VMEM((32, feat), F32),
        pltpu.VMEM((steps, MISC_ROWS, feat), F32),
        pltpu.VMEM((5, 8, LANES), F32),
        pltpu.VMEM((steps * WIDE, WIDE), BF16),
        pltpu.VMEM((32, latent.shape[0]), F32),
        pltpu.VMEM(latent.shape, BF16),
        pltpu.VMEM((2, steps, LAST, feat), BF16),
        pltpu.VMEM((2, steps, LAST, LANES), BF16),
        pltpu.VMEM((2, steps, LAST, LANES), BF16),
        pltpu.VMEM((batches, steps - 1, QUARTER, LANES), BF16),
        pltpu.VMEM((2, LAST, LANES), BF16),
        pltpu.VMEM((batches, near_count - 1, QUARTER // near_count, LANES), BF16),
        pltpu.VMEM((batches, far_slots, QUARTER // near_count, LANES), BF16),
        pltpu.VMEM((batches - 1, LAST, LANES), BF16),
        pltpu.VMEM((tiny, 8, LANES), F32),
        pltpu.VMEM((1, latent.shape[0]), jnp.int32),
        pltpu.VMEM(actions.shape, jnp.int32),
        pltpu.VMEM(chances.shape, jnp.int32),
        pltpu.VMEM(value_bins.shape, jnp.int32),
        pltpu.VMEM(reward_bins.shape, jnp.int32),
        pltpu.VMEM(action_w.shape, BF16),
        pltpu.VMEM(chance_w.shape, BF16),
        pltpu.VMEM((1, gain_w.shape[2], gain_w.shape[1], feat), BF16),
        pltpu.VMEM((1, gain_w.shape[2], gain_w.shape[1], feat), BF16),
        pltpu.VMEM((head_width, feat), BF16),
        pltpu.VMEM((chance_head.shape[1], feat), BF16),
        pltpu.VMEM((2, MISC_ROWS, 2 * NORMS * LANES), BF16),
        pltpu.VMEM((rows, feat), F32),
        pltpu.VMEM((2, 3, steps, QUARTER, LANES), BF16),
        pltpu.VMEM((2, MISC_ROWS, LANES), BF16),
        dma((8,)),
        dma((11,)),
        dma((6,)),
        dma((4,)),
        dma((9,)), dma((9,)),
        dma((2, 3)), dma((steps, 3)), dma((3,)),
        dma((steps, 9)), dma((steps, 9)),
        dma((batches,)), dma((batches,)),
        dma((batches, steps - 1)), dma((batches, steps - 1)),
        dma((batches, near_count - 1)), dma((batches, near_count - 1)),
        dma((batches, far_slots)), dma((batches, far_slots)),
        dma((batches, near_count - 1)), dma((batches, near_count - 1)),
        dma((batches, steps - 1)), dma((4, steps - 1)),
        dma((4,)), dma((4,)),
        dma((1,)), dma((1,)),
        dma((tiny,)), dma((tiny,)),
    ]
    scale = 1.0 / (latent.shape[0] * lines)
    outs = pl.pallas_call(
        functools.partial(kernel, scale, near_count, far_count),
        out_shape=(
            jax.ShapeDtypeStruct((rows, feat), F32),
            jax.ShapeDtypeStruct((2, 3, steps, QUARTER, LANES), BF16),
            jax.ShapeDtypeStruct((2, MISC_ROWS, LANES), BF16),
            jax.ShapeDtypeStruct((1, 1), F32),
            jax.ShapeDtypeStruct((steps - 2, 2, 15, feat, rows), BF16),
        ),
        in_specs=[anys] * 14,
        out_specs=(anys,) * 3 + (vmem, anys),
        scratch_shapes=scratch,
        compiler_params=pltpu.CompilerParams(
            vmem_limit_bytes=63 * 2**20, collective_id=0, has_side_effects=True
        ),
    )(
        latent, lengths.reshape(1, -1), actions, chances, value_bins, reward_bins,
        entry_w, block_w.reshape(1, 2, 4, feat, feat), action_w, chance_w,
        jnp.swapaxes(gain_w, 1, 2), jnp.swapaxes(shift_w, 1, 2), state_head.T, chance_head.T,
    )
    swapped = (1, gain_w.shape[2], gain_w.shape[1], feat)
    done = pl.pallas_call(
        functools.partial(finish_kernel, scale),
        out_shape=(
            jax.ShapeDtypeStruct((rows, 1, feat), F32),
            jax.ShapeDtypeStruct(entry_w.shape, F32),
            jax.ShapeDtypeStruct(block_w.shape, F32),
            jax.ShapeDtypeStruct(action_w.shape, F32),
            jax.ShapeDtypeStruct(chance_w.shape, F32),
            jax.ShapeDtypeStruct(swapped, F32),
            jax.ShapeDtypeStruct(swapped, F32),
            jax.ShapeDtypeStruct((head_width, feat), F32),
            jax.ShapeDtypeStruct((chance_head.shape[1], feat), F32),
        ),
        in_specs=[anys] * 3,
        out_specs=(vmem,) * 9,
        scratch_shapes=[
            pltpu.VMEM((rows, feat), F32),
            pltpu.VMEM((2, 3, steps, QUARTER, LANES), BF16),
            pltpu.VMEM((2, MISC_ROWS, LANES), BF16),
            dma((3,)),
        ],
        compiler_params=pltpu.CompilerParams(vmem_limit_bytes=63 * 2**20),
    )(outs[0], outs[1], outs[2])
    latent_grad, entry_grad, block_grad, action_grad, chance_grad, gain_grad, shift_grad, head_grad, chead_grad = done
    return (
        latent_grad, entry_grad, action_grad, chance_grad, block_grad,
        jnp.swapaxes(gain_grad, 1, 2), jnp.swapaxes(shift_grad, 1, 2),
        head_grad.T, chead_grad.T, outs[3].reshape(()),
    )


def solution(mesh):
    placed = (
        P("dp", None), P("dp"), P(None, "dp"), P(None, "dp"), P(None, "dp"), P(None, "dp"),
        P("section", None, None, None), P("section", None, None), P("section", None, None),
        P("section", None, None, None, None, None), P("section", None, None, None), P("section", None, None, None),
        P(), P(),
    )
    return jax.shard_map(
        per_device,
        mesh=mesh,
        in_specs=placed,
        out_specs=(
            P("dp", "section", None), P("section", None, None, None), P("section", None, None),
            P("section", None, None), P("section", None, None, None, None, None),
            P("section", None, None, None), P("section", None, None, None), P(), P(), P(),
        ),
        check_vma=False,
    )
```

```python
import functools

import jax
import jax.numpy as jnp
from jax import lax
from jax.experimental import pallas as pl
from jax.experimental.pallas import tpu as pltpu
from jax.sharding import PartitionSpec as P

F32 = jnp.float32
BF16 = jnp.bfloat16
ROOT = 0.7978845608028654
K1 = 2.0 * ROOT
K2 = 8.0 * ROOT * 0.044715
EPS = 1e-05
WIDE = 256
LANES = 128
NORMS = 5
ACT_ROW = 32
GAIN_ROW = 36
SHIFT_ROW = 46
MISC_ROWS = 64


def contract(left, right, left_dim, right_dim):
    return lax.dot_general(
        left, right, (((left_dim,), (right_dim,)), ((), ())), preferred_element_type=F32
    )


def gelu_pair(half, short):
    inner = half * (half * half * K2 + K1)
    plus = jnp.tanh(inner) + 1.0
    out = half * plus
    if short:
        half, inner, plus = half.astype(BF16), inner.astype(BF16), plus.astype(BF16)
    slope = inner * 3.0 - half * (2.0 * K1)
    return out, (plus * ((2.0 - plus) * slope + 1.0)).astype(BF16)


BAND = 32
QUARTER = 320
LAST = 384
CHAIN = ((0, 1), (1, 2), (2, 3), (3, 4), (4, 5), (5, 6), (6, 8), (8, 10))
EARLY = (0, 8, 1, 2, 3, 4)
LATE = (5, 6, 7)
MESH = pl.DeviceIdType.MESH
TICK_AT = 1
PLACE = (4, 3, 0, 1, 2)
PART_LAG, NEAR_LAG, FILL_LAG, OWN_LAG, DONE_LAG = 2, 4, 6, 9, 10


def when(condition, action):
    if isinstance(condition, bool):
        if condition:
            action()
    else:
        pl.when(condition)(action)


def kernel(
    scale, near_count, far_count,
    latent, lengths_in, actions_in, chances_in, values_in, rewards_in, entry, blocks, action_in, chance_in, gains_in,
    shifts_in, state_in, chance_head_in,
    latent_to, both_to, misc_to, loss_out, spill,
    weights, misc, head, acts, inv, ids, onehot, current, resid, prod_a, prod_b, grad, gb, acc,
    logits, dlogits, dchance, head_back, head_sum, chead_sum, misc_grad, loss_sum, sel, stage, states,
    sent, core_in, core_sum, part_in, part_sum, near_in, far_in, quarter, loss_in,
    lengths, actions, chances, values, rewards, action_w, chance_w, gains, shifts, state_head, chance_head,
    pick, latent_out, both, misc_both, load_sem, small_sem, out_sem, spill_sem, chain_send, chain_recv, give_send, step_recv, pass_send, pair_send, pair_recv,
    core_send, core_recv, part_send, part_recv, near_send, near_recv, far_send, far_recv,
    fill_send, fill_recv, own_send, own_recv, lane_send, lane_recv, extra_send, extra_recv, loss_send, loss_recv,
):
    section = lax.axis_index("section")
    line = lax.axis_index("dp")
    core = lax.rem(line, 2)
    near = lax.rem(line // 2, near_count)
    far = line // 2 // near_count
    mate = line + 1 - 2 * core
    rows = current.shape[1]
    steps = weights.shape[0]
    feat = WIDE
    head_width = state_head.shape[0]
    bins = (head_width - action_w.shape[1]) // 2
    head_pad = head.shape[0]
    action_count = action_w.shape[1]
    chance_count = chance_w.shape[1]
    chunks = [slice(c, c + WIDE) for c in range(0, rows, WIDE)]
    batches = 2 * steps

    def subs(part):
        return [slice(c, c + LANES) for c in range(part.start, part.stop, LANES)]

    def near_line(offset):
        return (far * near_count + lax.rem(near + offset, near_count)) * 2 + core

    def far_line(offset):
        return (lax.rem(far + offset, far_count) * near_count + near) * 2 + core

    def section_at(offset):
        return lax.rem(section + offset, steps)

    barrier = pltpu.get_barrier_semaphore()
    peers = [{"dp": mate}]
    peers += [{"section": section_at(o)} for o in range(1, steps)]
    peers += [{"dp": near_line(o)} for o in range(1, near_count)]
    peers += [{"dp": far_line(o)} for o in range(1, far_count)]
    for peer in peers:
        pl.semaphore_signal(barrier, inc=1, device_id=peer, device_id_type=MESH)

    loads = [(entry.at[0, 0], weights.at[section, 0]), (blocks.at[0, 0], weights.at[section, 1:5])]
    loads += [(entry.at[0, 1], weights.at[section, 5]), (blocks.at[0, 1], weights.at[section, 6:10])]
    loads += [(latent, states)]
    small = [(chance_in, chance_w), (action_in, action_w), (gains_in, gains), (shifts_in, shifts)]
    small += [(lengths_in, lengths), (actions_in, actions), (chances_in, chances), (values_in, values)]
    small += [(rewards_in, rewards), (state_in, state_head), (chance_head_in, chance_head)]
    small = [pltpu.make_async_copy(src, dst, small_sem.at[n]) for n, (src, dst) in enumerate(small)]
    loads = [pltpu.make_async_copy(src, dst, load_sem.at[n]) for n, (src, dst) in enumerate(loads)]
    for load in loads[0:4] + small + loads[4:]:
        load.start()

    def send(src, dst, sender, receiver, peer):
        return pltpu.make_async_remote_copy(
            src_ref=src, dst_ref=dst, send_sem=sender, recv_sem=receiver, device_id=peer, device_id_type=MESH
        )

    def landed(dst, receiver):
        send(dst, dst, load_sem.at[7], receiver, {"dp": mate}).wait_recv()

    place = jnp.where(section >= 2, 5 - section, section)
    after = lax.rem(place + 1 + 2 * core, steps)
    after = jnp.where(after >= 2, 5 - after, after)
    hops = jnp.where(core == 0, place, lax.rem(steps - place, steps))
    side_a = section + 1 - 2 * lax.rem(section, 2)
    side_b = lax.rem(section + 2, steps)
    pass_step = jnp.where(core == 0, side_a, side_b)
    pass_to = jnp.where(core == 0, side_b, side_a)

    def half_of(step, first, last, part):
        at = pl.multiple_of(part * (feat // 2), feat // 2)
        return weights.at[step, first:last, pl.ds(at, feat // 2)]

    def misc_half(step, part):
        return misc.at[step, pl.ds(pl.multiple_of(part * (MISC_ROWS // 2), MISC_ROWS // 2), MISC_ROWS // 2)]

    def piece(step, n, part):
        if isinstance(step, int) and step == 0:
            return misc_half(0, part) if n == len(CHAIN) else half_of(0, *CHAIN[n], part)
        return misc_half(step, part) if n == 2 else half_of(step, 5 * n, 5 * n + 5, part)

    def chain(n):
        ref = piece(0, n, core)
        return send(ref, ref, chain_send.at[n], chain_recv.at[n], {"section": after})

    def give(way, n):
        ref = piece(section, n, core)
        return send(ref, ref, give_send.at[way, n], step_recv.at[section, n], {"section": (side_a, side_b)[way]})

    def hand_on(n):
        ref = piece(pass_step, n, core)
        return send(ref, ref, pass_send.at[n], step_recv.at[pass_step, n], {"section": pass_to})

    def pair(step, n):
        ref = piece(step, n, core)
        return send(ref, ref, pair_send.at[step, n], pair_recv.at[step, n], {"dp": mate})

    def chain_on(order, onward):
        def run():
            for n in order:
                landed(piece(0, n, core), chain_recv.at[n])
                if onward:
                    chain(n).start()
                pair(0, n).start()

        return run

    def need_first(order):
        def run():
            for n in order:
                landed(piece(0, n, 1 - core), pair_recv.at[0, n])

        when(section != 0, run)

    def hand_on_now(condition, pieces):
        def run():
            for n in pieces:
                landed(piece(pass_step, n, core), step_recv.at[pass_step, n])
                hand_on(n).start()

        when(condition, run)

    def pair_now(step, pieces):
        def run():
            for n in pieces:
                pl.when(pass_step != step)(functools.partial(landed, piece(step, n, core), step_recv.at[step, n]))
                pair(step, n).start()

        when(section != step, run)

    def need(step, pieces):
        def run():
            for n in pieces:
                landed(piece(step, n, 1 - core), pair_recv.at[step, n])

        when(section != step, run)

    def give_now(way):
        def run():
            for n in (2, 0, 1):
                give(way, n).start()

        return run

    pl.semaphore_wait(barrier, len(peers))
    for load in loads[0:2]:
        load.wait()

    @pl.when(hops == 0)
    def _():
        chain(0).start()

    for load in small[0:4]:
        load.wait()
    packed = jnp.concatenate(
        [
            chance_w[0].astype(F32),
            action_w[0].astype(F32),
            gains[0, :, 0].astype(F32),
            gains[0, :, 1].astype(F32),
            shifts[0, :, 0].astype(F32),
            shifts[0, :, 1].astype(F32),
            jnp.zeros((MISC_ROWS - SHIFT_ROW - 2 * NORMS, feat), F32),
        ],
        axis=0,
    )
    misc[section] = packed.astype(BF16)

    @pl.when(hops == 0)
    def _():
        for n in EARLY[1:]:
            chain(n).start()

    for load in loads[2:4]:
        load.wait()

    @pl.when(hops == 0)
    def _():
        for n in LATE:
            chain(n).start()

    pl.when(section == 1)(give_now(0))
    pl.when(section == 2)(give_now(1))

    pick_at = lax.broadcasted_iota(jnp.int32, (steps * WIDE, WIDE), 0)
    pick_to = lax.broadcasted_iota(jnp.int32, (steps * WIDE, WIDE), 1)
    for tower in range(2):
        row = lax.broadcasted_iota(jnp.int32, (MISC_ROWS, 2 * NORMS * LANES), 0)
        at = lax.broadcasted_iota(jnp.int32, (MISC_ROWS, 2 * NORMS * LANES), 1) // LANES
        chosen = jnp.where((at < NORMS) & (row == GAIN_ROW + tower * NORMS + at), 8.0, 0.0)
        chosen = chosen + jnp.where((at >= NORMS) & (row == SHIFT_ROW + tower * NORMS + at - NORMS), 0.5, 0.0)
        pick[tower] = chosen.astype(BF16)
    for load in small[4:]:
        load.wait()
    head[head_width // 16 * 16 : head_pad] = jnp.zeros((head_pad - head_width // 16 * 16, feat), BF16)
    head[0:head_width] = state_head[...]
    sel[...] = (pick_at == steps * pick_to + section).astype(F32).astype(BF16)
    stage[...] = jnp.zeros_like(stage)
    stage[0:1] = lengths[...].astype(F32)
    stage[1:6] = actions[...].astype(F32)
    stage[6:10] = chances[...].astype(F32)
    stage[10:14] = lax.shift_right_logical(values[...], 5).astype(F32)
    stage[14:18] = (values[...] & 31).astype(F32)
    stage[18:22] = lax.shift_right_logical(rewards[...], 5).astype(F32)
    stage[22:26] = (rewards[...] & 31).astype(F32)
    for load in loads[4:]:
        load.wait()
    for n, part in enumerate(chunks):
        rows_in = slice(n * steps * WIDE, (n + 1) * steps * WIDE)
        current[:, part] = contract(states[rows_in], sel[...], 0, 0).astype(BF16)
        got = contract(stage[:, rows_in].astype(BF16), sel[...], 1, 0)
        value_ids = got[10:14] * 32.0 + got[14:18]
        reward_ids = got[18:22] * 32.0 + got[22:26]
        for k in range(steps):
            ids[k, 0:1, part] = got[0:1]
            ids[k, 1:3, part] = got[1 + k : 3 + k]
            ids[k, 3:4, part] = got[6 + k : 7 + k]
            ids[k, 4:5, part] = value_ids[k : k + 1]
            ids[k, 5:6, part] = reward_ids[k : k + 1]
    head_sum[...] = jnp.zeros_like(head_sum)
    chead_sum[...] = jnp.zeros_like(chead_sum)
    loss_sum[...] = jnp.zeros_like(loss_sum)

    pl.when((hops == 1) | (hops == 2))(chain_on(EARLY + LATE, True))
    pl.when(hops == 3)(chain_on(EARLY[:4], False))
    pl.when((section == 1) & (core == 1))(give_now(1))
    pl.when((section == 2) & (core == 1))(give_now(0))
    pl.when(section == 3)(give_now(1))
    pl.when(hops == 3)(chain_on(EARLY[4:], False))
    pl.when((section == 2) & (core == 0))(give_now(0))
    need_first(EARLY)

    def spread_norms(k, tower, with_shift):
        width = (2 * NORMS if with_shift else NORMS) * LANES
        gb[:, 0:width] = contract(misc[k], pick[tower, :, 0:width], 0, 0)

    def gain_of(n, band=slice(None)):
        return gb[band, n * LANES : (n + 1) * LANES]

    def shift_of(n, band=slice(None)):
        return gb[band, (NORMS + n) * LANES : (NORMS + n + 1) * LANES]

    def lookup(k, tower):
        lo = ACT_ROW if tower == 0 else 0
        return slice(lo, lo + 32)

    def tower_forward(k, tower):
        slot = lax.rem(k, 2)
        act = acts.at[slot, tower]
        spread_norms(k, tower, True)
        act[0] = current[...]
        look = lookup(k, tower)

        def multiply(n, part):
            matrix = weights[k, 5 * tower + n]
            if n == 0:
                got = contract(matrix, act[0, :, part], 0, 0)
                return got + contract(misc[k, look], onehot[look, part], 0, 0)
            return contract(matrix, act[1 + n // 2 if n % 2 == 1 else 2 + n // 2, :, part], 0, 0)

        def apply(n, sub, values):
            values = values - jnp.sum(values, axis=0, keepdims=True) * (1.0 / feat)
            inverse = lax.rsqrt(jnp.sum(values * values, axis=0, keepdims=True) + feat * EPS)
            inv[2 * k + tower, n : n + 1, sub] = inverse
            for r in range(0, feat, BAND):
                band = slice(r, r + BAND)
                unit = values[band] * inverse
                half = unit * gain_of(n, band) + shift_of(n, band)
                if n > 0 and n % 2 == 0:
                    half = half + 0.5 * resid[band, sub]
                out, slope = gelu_pair(half, n % 2 == 1)
                if n == 0 or n == 2:
                    resid[band, sub] = out
                if n == 4:
                    current[band, sub] = out.astype(BF16)
                else:
                    act[1 + n // 2 if n % 2 == 0 else 3 + n // 2, band, sub] = out.astype(BF16)
                act[5 + n, band, sub] = unit.astype(BF16)
                act[10 + n, band, sub] = slope

        for n in range(NORMS):
            for part in chunks:
                values = multiply(n, part)
                for c, sub in enumerate(subs(part)):
                    apply(n, sub, values[:, c * LANES : (c + 1) * LANES])

    def softmax_block(pieces, target, live):
        bands = []
        for start, stop, low, high in pieces:
            for at in range(start, stop, BAND):
                bands.append((at, min(at + BAND, stop), low, high, (low, high) != (start, stop)))

        def fold(values, op):
            parts = [values[r : r + 8] for r in range(0, values.shape[0], 8)]
            return functools.reduce(op, parts)

        top = None
        for start, stop, low, high, mixed in bands:
            part = logits[start:stop]
            if mixed:
                row = lax.broadcasted_iota(jnp.int32, part.shape, 0) + start
                part = jnp.where((row >= low) & (row < high), part, -jnp.inf)
            best = fold(part, jnp.maximum)
            top = best if top is None else jnp.maximum(top, best)
        top = jnp.max(top, axis=0, keepdims=True)
        total, hit = None, None
        for start, stop, low, high, mixed in bands:
            part = logits[start:stop] - top
            row = lax.broadcasted_iota(jnp.int32, part.shape, 0)
            found = fold(jnp.where(row == target - start, part, 0.0), jnp.add)
            expo = jnp.exp(part)
            if mixed:
                keep = (row >= low - start) & (row < high - start)
                expo = jnp.where(keep, expo, 0.0)
                logits[start:stop] = jnp.where(keep, expo, logits[start:stop])
            else:
                logits[start:stop] = expo
            amount = fold(expo, jnp.add)
            total = amount if total is None else total + amount
            hit = found if hit is None else hit + found
        total = jnp.sum(total, axis=0, keepdims=True)
        hit = jnp.sum(hit, axis=0, keepdims=True)
        return live * (jnp.log(total) - hit), live / total

    def head_pass(k, tick):
        slot = lax.rem(k, 2)
        for part in chunks:
            if part.start == WIDE:
                tick()
            for sub in subs(part):
                live = jnp.where(ids[k, 0:1, sub] > k.astype(F32), 1.0, 0.0)
                value_at = ids[k, 4:5, sub].astype(jnp.int32)
                reward_at = ids[k, 5:6, sub].astype(jnp.int32) + bins
                policy_at = ids[k, 2:3, sub].astype(jnp.int32) + 2 * bins
                chance_at = ids[k, 3:4, sub].astype(jnp.int32)
                logits[...] = contract(head[...], current[:, sub], 1, 0)
                edge_a = bins // 8 * 8
                edge_b = 2 * bins // 8 * 8
                loss = None
                scales = []
                for pieces, target in (
                    (((0, edge_a, 0, edge_a), (edge_a, edge_a + 8, edge_a, bins)), value_at),
                    (
                        (
                            (edge_a, edge_a + 8, bins, edge_a + 8),
                            (edge_a + 8, edge_b, edge_a + 8, edge_b),
                            (edge_b, edge_b + 8, edge_b, 2 * bins),
                        ),
                        reward_at,
                    ),
                    (((edge_b, edge_b + 8, 2 * bins, head_width),), policy_at),
                ):
                    lost, scale = softmax_block(pieces, target, live)
                    loss = lost if loss is None else loss + lost
                    scales.append(scale)
                low_a = bins // 16 * 16
                low_b = 2 * bins // 16 * 16
                cuts = [*range(0, low_a, BAND), low_a, *range(low_a + 16, low_b, BAND), low_b, low_b + 16]
                for start, stop in zip(cuts[:-1], cuts[1:]):
                    row = lax.broadcasted_iota(jnp.int32, (stop - start, LANES), 0)
                    expo = logits[start:stop]
                    if stop <= bins:
                        delta = expo * scales[0] - jnp.where(row == value_at - start, live, 0.0)
                    elif start >= bins and stop <= 2 * bins:
                        delta = expo * scales[1] - jnp.where(row == reward_at - start, live, 0.0)
                    else:
                        row = row + start
                        scale = jnp.where(row < bins, scales[0], jnp.where(row < 2 * bins, scales[1], scales[2]))
                        delta = expo * scale
                        for target in (value_at, reward_at, policy_at):
                            delta = delta - jnp.where(row == target, live, 0.0)
                        delta = jnp.where(row < head_width, delta, 0.0)
                    dlogits[start:stop, sub] = delta.astype(BF16)
                if low_b + 16 < head_pad:
                    dlogits[low_b + 16 : head_pad, sub] = jnp.zeros((head_pad - low_b - 16, LANES), BF16)
                chance_logit = contract(chance_head[...], acts[slot, 1, 0, :, sub], 1, 0)
                chance_logit = chance_logit - jnp.max(chance_logit, axis=0, keepdims=True)
                expo = jnp.exp(chance_logit)
                total = jnp.sum(expo, axis=0, keepdims=True)
                row = lax.broadcasted_iota(jnp.int32, chance_logit.shape, 0)
                hot = row == chance_at
                hit = jnp.sum(jnp.where(hot, chance_logit, 0.0), axis=0, keepdims=True)
                loss = loss + live * (jnp.log(total) - hit)
                delta = expo * (live / total) - jnp.where(hot, live, 0.0)
                dchance[k, :, sub] = delta.astype(BF16)
                loss_sum[0:1] += loss
        head_sum[...] += contract(dlogits[...], current[...], 1, 1)
        chead_sum[...] += contract(dchance[k], acts[slot, 1, 0], 1, 1)
        for part in chunks:
            head_back[k, :, part] = contract(head[...], dlogits[:, part], 0, 0)

    def make_onehot(k):
        row = lax.broadcasted_iota(jnp.int32, (MISC_ROWS, rows), 0)
        chance_at = ids[k, 3:4].astype(jnp.int32)
        action_at = ids[k, 1:2].astype(jnp.int32) + ACT_ROW
        onehot[...] = jnp.where((row == chance_at) | (row == action_at), 1.0, 0.0).astype(BF16)

    def spill_copy(k):
        return pltpu.make_async_copy(acts.at[lax.rem(k, 2)], spill.at[k], spill_sem.at[k])

    def fill_copy(k):
        return pltpu.make_async_copy(spill.at[k], acts.at[lax.rem(k, 2)], spill_sem.at[2 + k])

    @pl.loop(0, steps)
    def _(k):
        @pl.when(k >= 2)
        def _():
            spill_copy(k - 2).wait()

        @pl.when(k == 1)
        def _():
            need(1, (2, 0))
            hand_on_now(pass_step == 2, (2, 0))

        @pl.when(k == 2)
        def _():
            need(2, (2, 0))

        @pl.when(k == 3)
        def _():
            need(3, (2, 0))

        make_onehot(k)
        tower_forward(k, 0)

        @pl.when(k == 0)
        def _():
            pl.when(hops == 3)(chain_on(LATE, False))
            need_first(LATE)
            pl.when((section == 1) & (core == 0))(give_now(1))
            hand_on_now(pass_step == 1, (2, 0))

        @pl.when(k == 1)
        def _():
            pair_now(1, (1,))
            hand_on_now(pass_step == 2, (1,))
            need(1, (1,))

        @pl.when(k == 2)
        def _():
            hand_on_now(pass_step == 3, (1,))
            need(2, (1,))

        @pl.when(k == 3)
        def _():
            pair_now(3, (1,))
            need(3, (1,))

        tower_forward(k, 1)

        @pl.when(k == 0)
        def _():
            hand_on_now(pass_step == 1, (1,))
            pl.when(section == 3)(give_now(0))

        @pl.when(k == 1)
        def _():
            pair_now(2, (2, 0))

        def tick():
            @pl.when(k == 0)
            def _():
                pair_now(1, (2, 0))

            @pl.when(k == 1)
            def _():
                pair_now(2, (1,))
                hand_on_now(pass_step == 3, (2, 0))

            @pl.when(k == 2)
            def _():
                pair_now(3, (2, 0))

        head_pass(k, tick)

        @pl.when(k < steps - 2)
        def _():
            spill_copy(k).start()

    @pl.when(hops < 3)
    def _():
        for n in EARLY + LATE:
            chain(n).wait_send()

    @pl.when(section != 0)
    def _():
        for n in EARLY + LATE:
            pair(0, n).wait_send()
        for way in range(2):
            for n in range(3):
                give(way, n).wait_send()

    @pl.when(pass_step != 0)
    def _():
        for n in range(3):
            hand_on(n).wait_send()

    for step in range(1, steps):
        @pl.when(section != step)
        def _():
            for n in range(3):
                pair(step, n).wait_send()

    def lanes(part):
        return pl.ds(pl.multiple_of(part * LANES, LANES), LANES)

    def span(b):
        if isinstance(b, int) and b >= batches:
            return (b - batches) * (LAST // 2), LAST // 2
        return 0, QUARTER

    def held(b):
        return min(b, batches) if isinstance(b, int) else b

    def rows_of(b):
        low, count = span(b)
        return slice(low, low + count)

    def matrix_rows(b):
        low, count = span(b)
        return slice(low, min(low + count, QUARTER))

    def turn(b, tower):
        return 3 if isinstance(b, int) and b > batches else tower

    def core_copy(b, slot):
        return send(
            sent.at[slot, :, rows_of(b), lanes(1 - core)], core_in.at[slot, :, rows_of(b)],
            core_send.at[b], core_recv.at[b], {"dp": mate},
        )

    def part_copy(b, slot, offset):
        return send(
            core_sum.at[slot, section_at(offset), rows_of(b)], part_in.at[b, offset - 1, 0 : span(b)[1]],
            part_send.at[b, offset - 1], part_recv.at[b, offset - 1], {"section": section_at(offset)},
        )

    def near_rows(b, offset):
        low, count = span(b)
        size = count // near_count
        return pl.ds(pl.multiple_of(low + lax.rem(near + offset, near_count) * size, 16), size)

    def near_copy(b, slot, offset):
        return send(
            part_sum.at[slot, near_rows(b, offset)], near_in.at[b, offset - 1, 0 : span(b)[1] // near_count],
            near_send.at[b, offset - 1], near_recv.at[b, offset - 1], {"dp": near_line(offset)},
        )

    def far_copy(b, offset):
        return send(
            quarter.at[held(b), near_rows(b, 0)], far_in.at[b, offset - 1, 0 : span(b)[1] // near_count],
            far_send.at[b, offset - 1], far_recv.at[b, offset - 1], {"dp": far_line(offset)},
        )

    def fill_back(b, offset):
        ref = quarter.at[held(b), near_rows(b, 0)]
        return send(ref, ref, fill_send.at[b, offset - 1], fill_recv.at[b, offset - 1], {"dp": near_line(offset)})

    def core_wait(b, slot):
        core_copy(b, slot).wait()
        for j in range(steps):
            mine = sent[slot, j, rows_of(b), lanes(core)].astype(F32)
            core_sum[slot, j, rows_of(b)] = (mine + core_in[slot, j, rows_of(b)].astype(F32)).astype(BF16)
        for offset in range(1, steps):
            part_copy(b, slot, offset).start()

    def part_wait(b, slot):
        for offset in range(1, steps):
            part_copy(b, slot, offset).wait()
        total = core_sum[slot, section, rows_of(b)].astype(F32)
        for n in range(steps - 1):
            total = total + part_in[b, n, 0 : span(b)[1]].astype(F32)
        part_sum[slot, rows_of(b)] = total.astype(BF16)
        for offset in range(1, near_count):
            near_copy(b, slot, offset).start()

    def near_wait(b, slot):
        for offset in range(1, near_count):
            near_copy(b, slot, offset).wait()
        size = span(b)[1] // near_count
        total = part_sum[slot, near_rows(b, 0)].astype(F32)
        for n in range(near_count - 1):
            total = total + near_in[b, n, 0:size].astype(F32)
        quarter[held(b), near_rows(b, 0)] = total.astype(BF16)
        if far_count > 1:
            for offset in range(1, far_count):
                far_copy(b, offset).start()
            for offset in range(1, far_count):
                far_copy(b, offset).wait()
            for n in range(far_count - 1):
                total = total + far_in[b, n, 0:size].astype(F32)
            quarter[held(b), near_rows(b, 0)] = total.astype(BF16)
        for offset in range(1, near_count):
            fill_back(b, offset).start()

    def fill_wait(b):
        for offset in range(1, near_count):
            fill_back(b, offset).wait_send()
            landed(quarter.at[held(b), near_rows(b, near_count - offset)], fill_recv.at[b, offset - 1])

    def owner_copy(b, tower, offset):
        return send(
            quarter.at[held(b), matrix_rows(b)], both.at[core, tower, section, matrix_rows(b)],
            own_send.at[b, offset - 1], own_recv.at[turn(b, tower), offset - 1], {"section": section_at(steps - offset)},
        )

    def owner_of(b):
        return 0 if isinstance(b, int) and b >= batches else steps - 1 - (b - 1) // 2

    def share_start(b, tower):
        def keep():
            both[core, tower, section, matrix_rows(b)] = quarter[held(b), matrix_rows(b)]

        if tower == 2:
            keep()
            for offset in range(1, steps):
                owner_copy(b, tower, offset).start()
            return
        pl.when(section == owner_of(b))(keep)
        for offset in range(1, steps):
            pl.when(lax.rem(section - owner_of(b) + steps, steps) == offset)(owner_copy(b, tower, offset).start)

    def share_wait(b, tower):
        def take():
            for offset in range(1, steps):
                landed(
                    both.at[core, tower, section_at(offset), matrix_rows(b)], own_recv.at[turn(b, tower), offset - 1]
                )
            lane_copy(b, tower).start()

        if tower == 2:
            for offset in range(1, steps):
                owner_copy(b, tower, offset).wait_send()
            take()
            return
        for offset in range(1, steps):
            pl.when(lax.rem(section - owner_of(b) + steps, steps) == offset)(owner_copy(b, tower, offset).wait_send)
        pl.when(section == owner_of(b))(take)

    def lane_copy(b, tower):
        ref = both.at[core, tower, :, matrix_rows(b)]
        return send(ref, ref, lane_send.at[turn(b, tower)], lane_recv.at[turn(b, tower)], {"dp": mate})

    def finish(b, tower):
        def run():
            lane_copy(b, tower).wait_send()
            landed(both.at[1 - core, tower, :, matrix_rows(b)], lane_recv.at[turn(b, tower)])

        if tower == 2:
            run()
        else:
            pl.when(section == owner_of(b))(run)

    def by_kind(b, odd, action):
        if odd:
            pl.when(b >= 0)(functools.partial(action, b, 1))
        else:
            pl.when(b > 0)(functools.partial(action, b, 0))
            pl.when(b == 0)(functools.partial(action, b, 2))

    def fill_and_share(b, tower):
        fill_wait(b)
        share_start(b, tower)

    def ticks(at, parity):
        def odd(lag):
            return (parity + lag) % 2 == 1

        by_kind(at - DONE_LAG, odd(DONE_LAG), finish)
        by_kind(at - OWN_LAG, odd(OWN_LAG), share_wait)
        by_kind(at - FILL_LAG, odd(FILL_LAG), fill_and_share)
        pl.when(at >= NEAR_LAG)(functools.partial(near_wait, at - NEAR_LAG, parity))
        pl.when(at >= PART_LAG)(functools.partial(part_wait, at - PART_LAG, parity))
        core_wait(at, parity)

    def tower_backward(k, tower, at):
        slot = lax.rem(k, 2)
        act = acts.at[slot, tower]
        slot_out = tower
        spread_norms(k, tower, False)

        def put(m, value):
            size = feat // steps
            at_row = PLACE[m] * size
            for j in range(steps):
                sent[slot_out, j, at_row : at_row + size] = value[j * size : (j + 1) * size].astype(BF16)

        def norm_of(d_out, at, sub, target, keep):
            means, along = None, None
            kept = []
            for r in range(0, feat, BAND):
                band = slice(r, r + BAND)
                d_two = d_out[band] * act[10 + at, band, sub].astype(F32)
                weighted = d_two * act[5 + at, band, sub].astype(F32)
                if sub.start == 0:
                    acc[NORMS + at, band] = d_two
                    acc[at, band] = weighted
                else:
                    acc[NORMS + at, band] += d_two
                    acc[at, band] += weighted
                if keep:
                    grad[band, sub] = 0.5 * d_two
                gain = gain_of(at, band)
                d_unit = d_two * gain
                kept.append(d_unit)
                part_mean = jnp.sum(d_unit.reshape(BAND // 8, 8, LANES), axis=0)
                part_along = jnp.sum((weighted * gain).reshape(BAND // 8, 8, LANES), axis=0)
                means = part_mean if means is None else means + part_mean
                along = part_along if along is None else along + part_along
            mean = jnp.sum(means, axis=0, keepdims=True) * (1.0 / feat)
            along = jnp.sum(along, axis=0, keepdims=True)
            inverse = inv[2 * k + tower, at : at + 1, sub]
            for n, r in enumerate(range(0, feat, BAND)):
                band = slice(r, r + BAND)
                unit = act[5 + at, band, sub].astype(F32)
                target[band, sub] = ((kept[n] - mean - unit * along) * inverse).astype(BF16)

        for j in (1, 0):
            outer = 2 + 2 * j
            inner = 1 + 2 * j
            for part in chunks:
                for sub in subs(part):
                    norm_of(grad[:, sub], outer, sub, prod_a, True)
            if j == TICK_AT:
                ticks(at, 1 - tower)
            for part in chunks:
                d_mid = contract(weights[k, 5 * tower + 2 + 2 * j], prod_a[:, part], 1, 0)
                for n, sub in enumerate(subs(part)):
                    norm_of(d_mid[:, n * LANES : (n + 1) * LANES], inner, sub, prod_b, False)
            put(2 + 2 * j, contract(act[3 + j], prod_a[...], 1, 1))
            if tower == 0 and j == 0:
                pl.when(k == 0)(core_copy(batches, 0).start)
            for part in chunks:
                grad[:, part] += contract(weights[k, 5 * tower + 1 + 2 * j], prod_b[:, part], 1, 0)
            put(1 + 2 * j, contract(act[1 + j], prod_b[...], 1, 1))
        for part in chunks:
            for sub in subs(part):
                norm_of(grad[:, sub], 0, sub, prod_a, False)
        look = lookup(k, tower)
        put(0, contract(act[0], prod_a[...], 1, 1))
        got = contract(onehot[look], prod_a[...], 1, 1)
        if tower == 0:
            misc_grad[k, ACT_ROW : ACT_ROW + action_count] = got[0:action_count]
        else:
            misc_grad[k, 0:32] = got
        ones = jnp.ones((16, LANES), BF16)
        both_sums = acc[...].reshape(2 * NORMS * feat, LANES).astype(BF16)
        total = contract(ones, both_sums, 1, 1)
        for n in range(NORMS):
            at_gain = GAIN_ROW + NORMS * tower + n
            at_shift = SHIFT_ROW + NORMS * tower + n
            misc_grad[k, at_gain : at_gain + 1] = 8.0 * total[0:1, n * feat : (n + 1) * feat]
            misc_grad[k, at_shift : at_shift + 1] = 0.5 * total[0:1, (NORMS + n) * feat : (NORMS + n + 1) * feat]

    head_sum[head_width : head_width + chance_count] = chead_sum[...]
    for j in range(steps):
        sent[0, j, 0:QUARTER] = head_sum[j * QUARTER : (j + 1) * QUARTER].astype(BF16)
    core_copy(0, 0).start()

    @pl.loop(0, steps)
    def _(back):
        k = steps - 1 - back

        @pl.when(k < steps - 2)
        def _():
            fill_copy(k).wait()

        make_onehot(k)

        @pl.when(back == 0)
        def _():
            grad[...] = head_back[k]

        @pl.when(back > 0)
        def _():
            grad[...] = (0.5 * grad[...]).astype(BF16).astype(F32) + head_back[k]

        tower_backward(k, 1, 2 * back)
        core_copy(2 * back + 1, 1).start()
        for part in chunks:
            grad[:, part] = contract(weights[k, 5], prod_a[:, part], 1, 0) + contract(
                chance_head[...], dchance[k, :, part], 0, 0
            )
        tower_backward(k, 0, 2 * back + 1)

        @pl.when(k > 0)
        def _():
            core_copy(2 * back + 2, 0).start()

        @pl.when(k > 0)
        def _():
            for part in chunks:
                grad[:, part] = contract(weights[k, 0], prod_a[:, part], 1, 0)

        @pl.when(k >= 2)
        def _():
            fill_copy(k - 2).start()

    for j in range(steps):
        sent[0, j, QUARTER:LAST] = misc_grad[j].astype(BF16)
    core_copy(batches + 1, 0).start()

    loss_at = [{"dp": mate}] + [{"section": section_at(o)} for o in range(1, steps)]
    loss_at += [{"dp": near_line(o)} for o in range(1, near_count)]
    loss_at += [{"dp": far_line(o)} for o in range(1, far_count)]
    rounds = [1, steps - 1, near_count - 1, far_count - 1]
    bounds = [sum(rounds[:n]) for n in range(5)]

    def loss_copy(n, stage_at):
        return send(loss_sum.at[stage_at], loss_in.at[n], loss_send.at[n], loss_recv.at[n], loss_at[n])

    def loss_start(stage_at):
        for n in range(bounds[stage_at], bounds[stage_at + 1]):
            loss_copy(n, stage_at).start()

    def loss_wait(stage_at):
        total = loss_sum[stage_at]
        for n in range(bounds[stage_at], bounds[stage_at + 1]):
            loss_copy(n, stage_at).wait()
            total = total + loss_in[n]
        loss_sum[stage_at + 1] = total

    def misc_copy():
        return send(
            quarter.at[batches, QUARTER:LAST], misc_both.at[core], extra_send.at[0], extra_recv.at[0], {"dp": mate}
        )

    loss_start(0)
    def run(phase, *numbers):
        for b in numbers:
            if phase is finish or phase is share_wait or phase is fill_and_share:
                phase(b, 2 if b == 0 else (0 if b > batches else b % 2))
            else:
                phase(b, 0 if b > batches else b % 2)

    last = batches
    run(near_wait, last - 4)
    run(part_wait, last - 2)
    run(core_wait, last)
    for part in chunks:
        latent_out[part] = 0.5 * contract(prod_a[:, part], weights[0, 0], 0, 1)
    run(core_wait, last + 1)
    outs = [(latent_out, latent_to), (misc_both, misc_to)]
    outs += [(both.at[:, n], both_to.at[:, n]) for n in (2, 1, 0)]
    outs = [pltpu.make_async_copy(src, dst, out_sem.at[n]) for n, (src, dst) in enumerate(outs)]
    outs[0].start()
    loss_wait(0)
    loss_start(1)
    run(near_wait, last - 3)
    run(fill_and_share, last - 6, last - 5)
    run(share_wait, last - 8)
    run(part_wait, last - 1)
    run(near_wait, last - 2)
    run(fill_and_share, last - 4)
    run(share_wait, last - 7)
    run(finish, last - 8)
    run(part_wait, last, last + 1)
    loss_wait(1)
    loss_start(2)
    run(fill_and_share, last - 3)
    run(near_wait, last - 1)
    run(fill_and_share, last - 2)
    run(share_wait, last - 6, last - 5)
    run(near_wait, last, last + 1)
    loss_wait(2)
    loss_start(3)
    run(fill_and_share, last - 1)
    run(share_wait, last - 4, last - 3)
    run(finish, last - 7, last - 6, last - 5)
    run(fill_and_share, last, last + 1)
    misc_copy().start()
    run(share_wait, last - 2, last - 1)
    run(finish, last - 4, last - 3, last - 2)
    outs[2].start()
    run(share_wait, last, last + 1)
    run(finish, last - 1)
    outs[3].start()
    run(finish, last, last + 1)
    outs[4].start()
    loss_wait(3)
    loss_out[...] = jnp.sum(loss_sum[4, 0:1], axis=1, keepdims=True) * scale
    misc_both[core] = quarter[batches, QUARTER:LAST]
    misc_copy().wait_send()
    landed(misc_both.at[1 - core], extra_recv.at[0])
    outs[1].start()
    for out in outs:
        out.wait()


def finish_kernel(
    scale, latent_from, both_from, misc_from,
    latent_out, entry_out, block_out, action_out, chance_out, gain_out, shift_out, head_out, chead_out,
    latent_in, both, misc_both, sem,
):
    copies = [(both_from, both), (misc_from, misc_both), (latent_from, latent_in)]
    copies = [pltpu.make_async_copy(src, dst, sem.at[n]) for n, (src, dst) in enumerate(copies)]
    for copy in copies:
        copy.start()
    steps = both.shape[2]
    feat = entry_out.shape[-1]
    size = feat // steps
    head_width = head_out.shape[0]
    chance_count = chead_out.shape[0]
    copies[0].wait()
    copies[1].wait()
    for part in range(2):
        lanes = slice(part * LANES, (part + 1) * LANES)
        for j in range(steps):
            at = slice(j * size, (j + 1) * size)
            for tower in range(2):
                got = both[part, tower, j].astype(F32) * scale
                entry_out[0, tower, at, lanes] = got[PLACE[0] * size : (PLACE[0] + 1) * size]
                for m in range(4):
                    row = PLACE[m + 1] * size
                    block_out[0, tower, m // 2, m % 2, at, lanes] = got[row : row + size]
            got = both[part, 2, j].astype(F32) * scale
            start = j * QUARTER
            stop = min(start + QUARTER, head_width)
            head_out[start:stop, lanes] = got[0 : stop - start]
            if stop < start + QUARTER:
                chead_out[:, lanes] = got[stop - start : stop - start + chance_count]
        got = misc_both[part].astype(F32) * scale
        chance_out[0, :, lanes] = got[0:chance_count]
        action_out[0, :, lanes] = got[ACT_ROW : ACT_ROW + action_out.shape[1]]
        for tower in range(2):
            for n in range(NORMS):
                at = GAIN_ROW + tower * NORMS + n
                gain_out[0, n, tower : tower + 1, lanes] = got[at : at + 1]
                at = SHIFT_ROW + tower * NORMS + n
                shift_out[0, n, tower : tower + 1, lanes] = got[at : at + 1]
    copies[2].wait()
    latent_out[:, 0, :] = latent_in[...]


def per_device(
    latent, lengths, actions, chances, value_bins, reward_bins,
    entry_w, action_w, chance_w, block_w, gain_w, shift_w, state_head, chance_head,
):
    steps = lax.axis_size("section")
    lines = lax.axis_size("dp")
    near_count = min(4, lines // 2)
    far_count = lines // 2 // near_count
    rows = latent.shape[0] // steps
    feat = latent.shape[1]
    head_width = state_head.shape[1]
    head_pad = steps * QUARTER
    batches = 2 * steps + 2
    vmem = pl.BlockSpec(memory_space=pltpu.VMEM)
    anys = pl.BlockSpec(memory_space=pl.ANY)
    dma = pltpu.SemaphoreType.DMA
    tiny = 1 + (steps - 1) + (near_count - 1) + (far_count - 1)
    far_slots = max(far_count - 1, 1)
    scratch = [
        pltpu.VMEM((steps, 10, feat, feat), BF16),
        pltpu.VMEM((steps, MISC_ROWS, feat), BF16),
        pltpu.VMEM((head_pad, feat), BF16),
        pltpu.VMEM((2, 2, 15, feat, rows), BF16),
        pltpu.VMEM((2 * steps, 8, rows), F32),
        pltpu.VMEM((steps, 8, rows), F32),
        pltpu.VMEM((MISC_ROWS, rows), BF16),
        pltpu.VMEM((feat, rows), BF16),
        pltpu.VMEM((feat, rows), F32),
        pltpu.VMEM((feat, rows), BF16),
        pltpu.VMEM((feat, rows), BF16),
        pltpu.VMEM((feat, rows), F32),
        pltpu.VMEM((feat, 2 * NORMS * LANES), F32),
        pltpu.VMEM((2 * NORMS, feat, LANES), F32),
        pltpu.VMEM((head_pad, LANES), F32),
        pltpu.VMEM((head_pad, rows), BF16),
        pltpu.VMEM((steps, 32, rows), BF16),
        pltpu.VMEM((steps, feat, rows), F32),
        pltpu.VMEM((head_pad, feat), F32),
        pltpu.VMEM((32, feat), F32),
        pltpu.VMEM((steps, MISC_ROWS, feat), F32),
        pltpu.VMEM((5, 8, LANES), F32),
        pltpu.VMEM((steps * WIDE, WIDE), BF16),
        pltpu.VMEM((32, latent.shape[0]), F32),
        pltpu.VMEM(latent.shape, BF16),
        pltpu.VMEM((2, steps, LAST, feat), BF16),
        pltpu.VMEM((2, steps, LAST, LANES), BF16),
        pltpu.VMEM((2, steps, LAST, LANES), BF16),
        pltpu.VMEM((batches, steps - 1, QUARTER, LANES), BF16),
        pltpu.VMEM((2, LAST, LANES), BF16),
        pltpu.VMEM((batches, near_count - 1, QUARTER // near_count, LANES), BF16),
        pltpu.VMEM((batches, far_slots, QUARTER // near_count, LANES), BF16),
        pltpu.VMEM((batches - 1, LAST, LANES), BF16),
        pltpu.VMEM((tiny, 8, LANES), F32),
        pltpu.VMEM((1, latent.shape[0]), jnp.int32),
        pltpu.VMEM(actions.shape, jnp.int32),
        pltpu.VMEM(chances.shape, jnp.int32),
        pltpu.VMEM(value_bins.shape, jnp.int32),
        pltpu.VMEM(reward_bins.shape, jnp.int32),
        pltpu.VMEM(action_w.shape, BF16),
        pltpu.VMEM(chance_w.shape, BF16),
        pltpu.VMEM((1, gain_w.shape[2], gain_w.shape[1], feat), BF16),
        pltpu.VMEM((1, gain_w.shape[2], gain_w.shape[1], feat), BF16),
        pltpu.VMEM((head_width, feat), BF16),
        pltpu.VMEM((chance_head.shape[1], feat), BF16),
        pltpu.VMEM((2, MISC_ROWS, 2 * NORMS * LANES), BF16),
        pltpu.VMEM((rows, feat), F32),
        pltpu.VMEM((2, 3, steps, QUARTER, LANES), BF16),
        pltpu.VMEM((2, MISC_ROWS, LANES), BF16),
        dma((8,)),
        dma((11,)),
        dma((6,)),
        dma((4,)),
        dma((9,)), dma((9,)),
        dma((2, 3)), dma((steps, 3)), dma((3,)),
        dma((steps, 9)), dma((steps, 9)),
        dma((batches,)), dma((batches,)),
        dma((batches, steps - 1)), dma((batches, steps - 1)),
        dma((batches, near_count - 1)), dma((batches, near_count - 1)),
        dma((batches, far_slots)), dma((batches, far_slots)),
        dma((batches, near_count - 1)), dma((batches, near_count - 1)),
        dma((batches, steps - 1)), dma((4, steps - 1)),
        dma((4,)), dma((4,)),
        dma((1,)), dma((1,)),
        dma((tiny,)), dma((tiny,)),
    ]
    scale = 1.0 / (latent.shape[0] * lines)
    outs = pl.pallas_call(
        functools.partial(kernel, scale, near_count, far_count),
        out_shape=(
            jax.ShapeDtypeStruct((rows, feat), F32),
            jax.ShapeDtypeStruct((2, 3, steps, QUARTER, LANES), BF16),
            jax.ShapeDtypeStruct((2, MISC_ROWS, LANES), BF16),
            jax.ShapeDtypeStruct((1, 1), F32),
            jax.ShapeDtypeStruct((steps - 2, 2, 15, feat, rows), BF16),
        ),
        in_specs=[anys] * 14,
        out_specs=(anys,) * 3 + (vmem, anys),
        scratch_shapes=scratch,
        compiler_params=pltpu.CompilerParams(
            vmem_limit_bytes=63 * 2**20, collective_id=0, has_side_effects=True
        ),
    )(
        latent, lengths.reshape(1, -1), actions, chances, value_bins, reward_bins,
        entry_w, block_w.reshape(1, 2, 4, feat, feat), action_w, chance_w,
        jnp.swapaxes(gain_w, 1, 2), jnp.swapaxes(shift_w, 1, 2), state_head.T, chance_head.T,
    )
    swapped = (1, gain_w.shape[2], gain_w.shape[1], feat)
    done = pl.pallas_call(
        functools.partial(finish_kernel, scale),
        out_shape=(
            jax.ShapeDtypeStruct((rows, 1, feat), F32),
            jax.ShapeDtypeStruct(entry_w.shape, F32),
            jax.ShapeDtypeStruct(block_w.shape, F32),
            jax.ShapeDtypeStruct(action_w.shape, F32),
            jax.ShapeDtypeStruct(chance_w.shape, F32),
            jax.ShapeDtypeStruct(swapped, F32),
            jax.ShapeDtypeStruct(swapped, F32),
            jax.ShapeDtypeStruct((head_width, feat), F32),
            jax.ShapeDtypeStruct((chance_head.shape[1], feat), F32),
        ),
        in_specs=[anys] * 3,
        out_specs=(vmem,) * 9,
        scratch_shapes=[
            pltpu.VMEM((rows, feat), F32),
            pltpu.VMEM((2, 3, steps, QUARTER, LANES), BF16),
            pltpu.VMEM((2, MISC_ROWS, LANES), BF16),
            dma((3,)),
        ],
        compiler_params=pltpu.CompilerParams(vmem_limit_bytes=63 * 2**20),
    )(outs[0], outs[1], outs[2])
    latent_grad, entry_grad, block_grad, action_grad, chance_grad, gain_grad, shift_grad, head_grad, chead_grad = done
    return (
        latent_grad, entry_grad, action_grad, chance_grad, block_grad,
        jnp.swapaxes(gain_grad, 1, 2), jnp.swapaxes(shift_grad, 1, 2),
        head_grad.T, chead_grad.T, outs[3].reshape(()),
    )


def solution(mesh):
    placed = (
        P("dp", None), P("dp"), P(None, "dp"), P(None, "dp"), P(None, "dp"), P(None, "dp"),
        P("section", None, None, None), P("section", None, None), P("section", None, None),
        P("section", None, None, None, None, None), P("section", None, None, None), P("section", None, None, None),
        P(), P(),
    )
    return jax.shard_map(
        per_device,
        mesh=mesh,
        in_specs=placed,
        out_specs=(
            P("dp", "section", None), P("section", None, None, None), P("section", None, None),
            P("section", None, None), P("section", None, None, None, None, None),
            P("section", None, None, None), P("section", None, None, None), P(), P(), P(),
        ),
        check_vma=False,
    )
```
